32 devices in a mesh: ctx: 8 (over y, x, core), fsdp: 4 (over z).
Axes of the slice: x: 2, y: 2, z: 4, core: 2. Of those that a mesh axis runs over, the one named last changes fastest.
Arguments:
- tokens: bfloat16 [4, 1024, 1024], P('fsdp', 'ctx'), may hold values from -6 to 6
- encoder_states: bfloat16 [4, 256, 1024], P('fsdp', 'ctx'), may hold values from -6 to 6
- grad_out: bfloat16 [4, 1024, 1024], P('fsdp', 'ctx'), may hold values from -8 to 8
- doc_starts: int32 [4, 8], P('fsdp'), may hold values from 0 to 1023, as said below
- source_doc: int32 [4, 8], P('fsdp'), may hold values from 0 to 7, as said below
- source_offsets: int32 [4, 8], P('fsdp'), may hold values from 0 to 255, as said below
- self_qkv: bfloat16 [2, 1024, 3072], P(None, 'fsdp'), may hold values from -0.1875 to 0.1875
- self_out: bfloat16 [2, 1024, 1024], P(None, 'fsdp'), may hold values from -1.5 to 1.5
- cross_q: bfloat16 [2, 1024, 1024], P(None, 'fsdp'), may hold values from -0.1875 to 0.1875
- cross_kv: bfloat16 [2, 1024, 2048], P(None, 'fsdp'), may hold values from -0.1875 to 0.1875
- cross_out: bfloat16 [2, 1024, 1024], P(None, 'fsdp'), may hold values from -1.5 to 1.5
- ffn_in: bfloat16 [2, 1024, 8192], P(None, 'fsdp'), may hold values from -0.1875 to 0.1875
- ffn_out: bfloat16 [2, 8192, 1024], P(None, 'fsdp'), may hold values from -0.0625 to 0.0625
- norm_gains: bfloat16 [2, 3, 1024], P(None, None, 'fsdp'), may hold values from 0.5 to 1.5
- vec_biases: bfloat16 [2, 10, 1024], P(None, None, 'fsdp'), may hold values from -1.25 to 1.25
- fc1_bias: bfloat16 [2, 8192], P(None, 'fsdp'), may hold values from -1.25 to 1.25
Outputs:
- output: bfloat16 [4, 1024, 1024], P('fsdp', 'ctx')
- tokens_grad: float32 [4, 1024, 1024], P('fsdp', 'ctx')
- encoder_grad: float32 [4, 256, 1024], P('fsdp', 'ctx')
- self_qkv_grad: float32 [2, 1024, 3072], P(None, ('ctx', 'fsdp'))
- self_out_grad: float32 [2, 1024, 1024], P(None, ('ctx', 'fsdp'))
- cross_q_grad: float32 [2, 1024, 1024], P(None, ('ctx', 'fsdp'))
- cross_kv_grad: float32 [2, 1024, 2048], P(None, ('ctx', 'fsdp'))
- cross_out_grad: float32 [2, 1024, 1024], P(None, ('ctx', 'fsdp'))
- ffn_in_grad: float32 [2, 1024, 8192], P(None, ('ctx', 'fsdp'))
- ffn_out_grad: float32 [2, 8192, 1024], P(None, ('ctx', 'fsdp'))
- norm_gains_grad: float32 [2, 3, 1024], P(None, None, ('ctx', 'fsdp'))
- vec_biases_grad: float32 [2, 10, 1024], P(None, None, ('ctx', 'fsdp'))
- fc1_bias_grad: float32 [2, 8192], P(None, ('ctx', 'fsdp'))
The draws below stay inside these ranges and needn't reach their ends.
Inputs may be any that keep to these rules, and one draw needn't show every extreme that they name: `doc_starts`: each stream's 8 starts rise strictly from 0; a document runs to the next start or to the stream's end. Exactly one document of each stream has 896 tokens, and it is the first or the last; the others are shorter. `source_doc`: the document of 896 tokens reads the source document that starts within the first 32 states. `source_offsets`: each stream's 8 starts rise strictly from 0; a source document runs to the next start or to the end of the 256 states. Exactly one starts within the first 32 states and ends within the last 32; the others are shorter than 32.
All inputs are finite; a program needn't handle non-finite values.
Results may differ from the reference program's by a relative error of at most 0.017.
Values may be sent and summed in bfloat16 or wider, within the bound.
No kernel may reach another device: no remote copies, remote signals or barrier semaphores. Data moves between devices by JAX's collectives and lax.ppermute only.
A program may use at most 512 MiB of HBM per device.

```python
import jax
import jax.numpy as jnp
from jax import lax

D = 1024
HEADS = 16
F = 8192
LAYERS = 2
TOK_DEV = 128
SRC_DEV = 32
NDOC = 8
NSRC = 8
STREAMS = 4
LEN = 1024
SRC_LEN = 256
DOC_MOST = 896
N_CTX = 8


def layout_flags(key):
    flag_key, source_key = jax.random.split(jax.random.fold_in(key, 77))
    long_first = jax.random.randint(flag_key, (STREAMS,), 0, 2)
    long_source = jax.random.randint(source_key, (STREAMS,), 0, NSRC)
    return (long_first, long_source)


def sorted_picks(key, span_size, picked, lowest):
    chosen = jax.random.permutation(key, span_size)[:picked]
    return jnp.sort(chosen).astype(jnp.int32) + lowest


def draw_doc_starts(key, part):
    long_first, long_source = layout_flags(key)
    key = jax.random.fold_in(key, 1)
    short_span = LEN - DOC_MOST
    cut_points = jax.vmap(lambda stream_key: sorted_picks(stream_key, short_span - 1, NDOC - 2, 1))(jax.random.split(key, STREAMS))
    zero_column = jnp.zeros((STREAMS, 1), jnp.int32)
    long_last = jnp.concatenate([zero_column, cut_points, jnp.full((STREAMS, 1), short_span, jnp.int32)], axis=1)
    long_head = jnp.concatenate([zero_column, jnp.full((STREAMS, 1), DOC_MOST, jnp.int32), cut_points + DOC_MOST], axis=1)
    return jnp.where(long_first[:, None] == 1, long_head, long_last).astype(jnp.int32)


def draw_source_doc(key, part):
    long_first, long_source = layout_flags(key)
    key = jax.random.fold_in(key, 2)
    chosen_docs = jax.random.randint(key, (STREAMS, NDOC), 0, NSRC)
    long_slot = jnp.where(long_first == 1, 0, NDOC - 1)
    slot_index = jnp.arange(NDOC, dtype=jnp.int32)
    return jnp.where(slot_index[None, :] == long_slot[:, None], long_source[:, None], chosen_docs).astype(jnp.int32)


def draw_source_offsets(key, part):
    long_first, long_source = layout_flags(key)
    key = jax.random.fold_in(key, 3)
    early_key, late_key = jax.random.split(key)
    early_cuts = jax.vmap(lambda stream_key: sorted_picks(stream_key, SRC_DEV - 1, NSRC - 1, 1))(jax.random.split(early_key, STREAMS))
    late_cuts = jax.vmap(lambda stream_key: sorted_picks(stream_key, SRC_DEV - 1, NSRC - 1, SRC_LEN - SRC_DEV + 1))(jax.random.split(late_key, STREAMS))
    slot_index = jnp.arange(1, NSRC, dtype=jnp.int32)
    later_starts = jnp.where(slot_index[None, :] <= long_source[:, None], early_cuts, late_cuts)
    return jnp.concatenate([jnp.zeros((STREAMS, 1), jnp.int32), later_starts], axis=1).astype(jnp.int32)


def draw_grad_out(key, part):
    key = jax.random.fold_in(key, 4)
    noise_key, column_key = jax.random.split(key)
    noise = jnp.clip(jax.random.normal(noise_key, (STREAMS, LEN, D), jnp.float32), -6.0, 6.0)
    column_part = 0.3 * jnp.clip(jax.random.normal(column_key, (1, 1, D), jnp.float32), -6.0, 6.0)
    return jnp.clip(noise + column_part, -8.0, 8.0).astype(jnp.bfloat16)


def steps_of(rng, shape, pieces, low, high):
    level = 1.0
    for axis_at, shards_of in pieces:
        heights = jax.random.uniform(jax.random.fold_in(jax.random.fold_in(rng, 6), axis_at), (shards_of,), jnp.float32, low / len(pieces), high / len(pieces))
        level = level * jnp.repeat(jnp.exp(heights), shape[axis_at] // shards_of).reshape((-1,) + (1,) * (len(shape) - 1 - axis_at))
    return level


def bell_draw(key, extent, scale, most, cuts=(), kind=jnp.bfloat16):
    gain = steps_of(key, extent, cuts, -0.22, 0.18) if cuts else 1.0
    drawn = jax.random.normal(key, extent, jnp.float32) * scale * gain
    return jnp.minimum(jnp.maximum(drawn, -most), most).astype(kind)


def setup_inputs(seed: int = 0) -> dict:
    streams_of = jax.random.split(jax.random.key(seed), 17)
    tokens = bell_draw(streams_of[0], (STREAMS, LEN, D), 1.0, 6.0, ((0, 4), (1, 8)))
    encoder_states = bell_draw(streams_of[1], (STREAMS, SRC_LEN, D), 1.0, 6.0, ((0, 4), (1, 8)))
    grad_out = draw_grad_out(jax.random.fold_in(streams_of[16], 71), 0)
    doc_starts = draw_doc_starts(jax.random.fold_in(streams_of[16], 71), 0)
    source_doc = draw_source_doc(jax.random.fold_in(streams_of[16], 71), 0)
    source_offsets = draw_source_offsets(jax.random.fold_in(streams_of[16], 71), 0)
    self_qkv = bell_draw(streams_of[6], (LAYERS, D, 3 * D), D ** -0.5, 0.1875, ((1, 4),))
    self_out = bell_draw(streams_of[7], (LAYERS, D, D), (D // 64) ** -0.5, 1.5, ((1, 4),))
    cross_q = bell_draw(streams_of[8], (LAYERS, D, D), D ** -0.5, 0.1875, ((1, 4),))
    cross_kv = bell_draw(streams_of[9], (LAYERS, D, 2 * D), D ** -0.5, 0.1875, ((1, 4),))
    cross_out = bell_draw(streams_of[10], (LAYERS, D, D), (D // 64) ** -0.5, 1.5, ((1, 4),))
    ffn_in = bell_draw(streams_of[11], (LAYERS, D, F), D ** -0.5, 0.1875, ((1, 4),))
    ffn_out = bell_draw(streams_of[12], (LAYERS, F, D), F ** -0.5, 0.0625, ((1, 4),))
    norm_gains = jnp.clip(1.0 + 0.1 * jax.random.normal(streams_of[13], (LAYERS, 3, D), jnp.float32), 0.5, 1.5).astype(jnp.bfloat16)
    vec_biases = bell_draw(streams_of[14], (LAYERS, 10, D), 0.2, 1.25, ((2, 4),))
    fc1_bias = bell_draw(streams_of[15], (LAYERS, F), 0.2, 1.25, ((1, 4),))
    return {"tokens": tokens, "encoder_states": encoder_states, "grad_out": grad_out, "doc_starts": doc_starts, "source_doc": source_doc, "source_offsets": source_offsets, "self_qkv": self_qkv, "self_out": self_out, "cross_q": cross_q, "cross_kv": cross_kv, "cross_out": cross_out, "ffn_in": ffn_in, "ffn_out": ffn_out, "norm_gains": norm_gains, "vec_biases": vec_biases, "fc1_bias": fc1_bias}


@jax.custom_vjp
def low(v):
    return lax.optimization_barrier(v.astype(jnp.bfloat16)).astype(jnp.float32)

@jax.custom_vjp
def low_back(v):
    return v

def low_keep(v):
    return (low(v), None)

def low_pass(kept, grad):
    return (grad,)

def back_keep(v):
    return (v, None)

def back_low(kept, grad):
    return (low(grad),)
low.defvjp(low_keep, low_pass)
low_back.defvjp(back_keep, back_low)
EPSILON = 1e-05
PRECISE = lax.Precision.HIGHEST

def product(left, right):
    return jnp.dot(left, right, precision=PRECISE)

def layer_norm(values, gain_row, offset_row):
    center = values - lax.optimization_barrier(jnp.mean(values, axis=-1, keepdims=True))
    spread = lax.optimization_barrier(jnp.mean(center * center, axis=-1, keepdims=True))
    return center * lax.rsqrt(spread + EPSILON) * gain_row + offset_row

def stored_positions(row_index, row_count, dev_count):
    device = row_index // row_count
    offset = row_index % row_count
    half_rows = row_count // 2
    return jnp.where(offset < half_rows, device * half_rows + offset, (2 * dev_count - 1 - device) * half_rows + offset - half_rows)

def group_of(places, starts):
    return lax.optimization_barrier(jnp.sum((starts[None, :] <= places[:, None]).astype(jnp.int32), axis=1)) - 1

def attention(queries, keys_low, values_low, geometry):
    query_group, key_group, query_place, key_place = geometry
    head_width = queries.shape[1] // HEADS
    blocks = queries.shape[0] // TOK_DEV
    query_heads = queries.reshape(blocks, TOK_DEV, HEADS, head_width)
    key_heads = keys_low.reshape(keys_low.shape[0], HEADS, head_width)
    value_heads = values_low.reshape(values_low.shape[0], HEADS, head_width)

    def one_block(block_item):
        query_block, group_block, place_block = block_item
        scores = low_back(jnp.einsum('qhd,khd->hqk', query_block, key_heads, precision=PRECISE))
        allowed_mask = (group_block[:, None] == key_group[None, :]) & (key_place[None, :] <= place_block[:, None])
        mask_weight = jnp.broadcast_to(allowed_mask, scores.shape).astype(scores.dtype)
        log_mass = jax.nn.logsumexp(scores, axis=-1, b=mask_weight, keepdims=True)
        weights_low = low(jnp.where(allowed_mask, jnp.exp(scores - log_mass), 0.0))
        mixed_out = jnp.einsum('hqk,khd->qhd', weights_low, value_heads, precision=PRECISE)
        return low(low_back(mixed_out)).reshape(TOK_DEV, HEADS * head_width)
    mixed_all = lax.map(jax.checkpoint(one_block), (query_heads, query_group.reshape(blocks, TOK_DEV), query_place.reshape(blocks, TOK_DEV)))
    return mixed_all.reshape(queries.shape[0], HEADS * head_width)

def decoder_layer(hidden, encoder_rows, weights, self_geometry, cross_geometry):
    w_qkv, w_out, w_cross_q, w_cross_kv, w_cross_out, w_up, w_down, gains, biases, up_bias = weights
    width_all = hidden.shape[1]
    normed_one = low(layer_norm(hidden, gains[0], biases[0]))
    qkv_rows = product(normed_one, w_qkv)
    queries = low(low_back((qkv_rows[:, :width_all] + biases[3]) * 0.125))
    keys_low = low(low_back(qkv_rows[:, width_all:2 * width_all]))
    values_low = low(low_back(qkv_rows[:, 2 * width_all:] + biases[4]))
    self_mixed = attention(queries, keys_low, values_low, self_geometry)
    after_self = hidden + low_back(product(self_mixed, w_out) + biases[5])
    normed_two = low(layer_norm(after_self, gains[1], biases[1]))
    cross_queries = low(low_back((product(normed_two, w_cross_q) + biases[6]) * 0.125))
    enc_proj = product(encoder_rows, w_cross_kv)
    enc_keys = low(low_back(enc_proj[:, :width_all]))
    enc_values = low(low_back(enc_proj[:, width_all:] + biases[7]))
    cross_mixed = attention(cross_queries, enc_keys, enc_values, cross_geometry)
    after_cross = after_self + low_back(product(cross_mixed, w_cross_out) + biases[8])
    normed_three = low(layer_norm(after_cross, gains[2], biases[2]))
    hidden_pre = low_back(product(normed_three, w_up) + up_bias)
    hidden_act = low(jax.nn.gelu(hidden_pre, approximate=False))
    return after_cross + low_back(product(hidden_act, w_down) + biases[9])

def reference(tokens, encoder_states, grad_out, doc_starts, source_doc, source_offsets, self_qkv, self_out, cross_q, cross_kv, cross_out, ffn_in, ffn_out, norm_gains, vec_biases, fc1_bias):
    floats = tuple((array.astype(jnp.float32) for array in (tokens, encoder_states, self_qkv, self_out, cross_q, cross_kv, cross_out, ffn_in, ffn_out, norm_gains, vec_biases, fc1_bias)))
    key_place = stored_positions(jnp.arange(LEN, dtype=jnp.int32), TOK_DEV, N_CTX)
    source_place = jnp.arange(SRC_LEN, dtype=jnp.int32)
    zero_queries = jnp.zeros((LEN,), jnp.int32)
    zero_sources = jnp.zeros((SRC_LEN,), jnp.int32)
    doc_slots = jnp.arange(NDOC, dtype=jnp.int32)

    def forward(values_all):
        stream_outs = []
        for stream in range(STREAMS):
            documents = group_of(key_place, doc_starts[stream])
            cross_group = lax.optimization_barrier(jnp.sum(jnp.where(documents[:, None] == doc_slots[None, :], source_doc[stream][None, :], 0), axis=1))
            source_group = group_of(source_place, source_offsets[stream])
            self_geometry = (documents, documents, key_place, key_place)
            cross_geometry = (cross_group, source_group, zero_queries, zero_sources)
            hidden = values_all[0][stream]
            for layer_index in range(LAYERS):
                weights = tuple((values_all[slot][layer_index] for slot in range(2, 12)))
                hidden = decoder_layer(hidden, values_all[1][stream], weights, self_geometry, cross_geometry)
            stream_outs.append(hidden)
        return jnp.stack(stream_outs)
    result, pullback = jax.vjp(forward, floats)
    grads, = pullback(grad_out.astype(jnp.float32))
    return (result.astype(jnp.bfloat16), grads[0], grads[1], grads[2], grads[3], grads[4], grads[5], grads[6], grads[7], grads[8], grads[9], grads[10], grads[11])
```

```python
from functools import partial

import jax
import jax.numpy as jnp
from jax import lax
from jax.experimental import pallas as pl
from jax.experimental.pallas import tpu as pltpu
from jax.sharding import PartitionSpec as P

HEADS = 16
EPSILON = 1e-05
NEGATIVE = -1e30
F32 = jnp.float32
LOW = jnp.bfloat16


def swap(values, bits):
    count = lax.axis_size("ctx")
    return lax.ppermute(values, "ctx", [(i, i ^ bits) for i in range(count)])


def gather_slots(rows):
    count = lax.axis_size("ctx")
    if count == 8:
        near_x, near_y = swap(rows, 2), swap(rows, 4)
        half = rows.shape[0] // 2
        far = jnp.concatenate([swap(near_x[:half], 4), swap(near_y[half:], 2)])
        blocks = []
        for block in (rows, near_x, near_y, far):
            blocks += [block, swap(block, 1)]
        return jnp.stack(blocks)
    stack = rows[None]
    bit = 1
    while bit < count:
        stack = jnp.concatenate([stack, swap(stack, bit)])
        bit *= 2
    return stack


def reduce_slots(parts, kind=LOW):
    count = lax.axis_size("ctx")
    if count == 8 and parts.shape[1] % 32 == 0:
        other = swap(parts[1::2].astype(kind), 1)
        chip = parts[0::2].astype(F32) + other.astype(F32)
        half = parts.shape[1] // 2
        far = chip[3].astype(kind)
        far_x, far_y = swap(far[:half], 2), swap(far[half:], 4)
        to_x = jnp.concatenate([chip[1][:half], chip[1][half:] + far_y.astype(F32)]).astype(kind)
        to_y = jnp.concatenate([chip[2][:half] + far_x.astype(F32), chip[2][half:]]).astype(kind)
        return chip[0] + swap(to_x, 2).astype(F32) + swap(to_y, 4).astype(F32)
    total = parts.astype(F32)
    bit = count // 2
    while bit:
        total = total[:bit] + swap(total[bit : 2 * bit].astype(kind), bit).astype(F32)
        bit //= 2
    return total[0]


def exchange_slots(parts):
    return jnp.stack([parts[0]] + [swap(parts[k], k) for k in range(1, parts.shape[0])])


def turn(values, axis):
    count = lax.axis_size("ctx")
    here = lax.axis_index("ctx")
    width = values.shape[axis] // count
    return jnp.concatenate(
        [
            lax.dynamic_slice_in_dim(values, (here ^ k) * width, width, axis)
            for k in range(count)
        ],
        axis=axis,
    )


def gather_planes(values):
    return lax.all_gather(values, "fsdp", axis=0, tiled=True)


def reduce_planes(parts):
    return lax.psum_scatter(parts, "fsdp", scatter_dimension=0, tiled=False)


def attend_forward_kernel(head_width, q_ref, k_ref, v_ref, low_ref, high_ref, place_ref, o_ref, lse_ref):
    place = place_ref[...]
    mask = (place >= low_ref[...]) & (place <= high_ref[...])
    outs, masses = [], []
    for start in range(0, q_ref.shape[1], head_width):
        span = slice(start, start + head_width)
        scores = lax.dot_general(
            q_ref[:, span], k_ref[:, span], (((1,), (1,)), ((), ())), preferred_element_type=F32
        )
        scores = jnp.where(mask, scores, NEGATIVE)
        top = jnp.max(scores, axis=1, keepdims=True)
        raised = jnp.exp(scores - top)
        mass = jnp.sum(raised, axis=1, keepdims=True)
        weights = (raised * (1.0 / mass)).astype(LOW)
        outs.append(jnp.dot(weights, v_ref[:, span], preferred_element_type=F32))
        masses.append(top + jnp.log(mass))
    o_ref[...] = jnp.concatenate(outs, axis=1).astype(LOW)
    lse_ref[0] = jnp.concatenate(masses, axis=1)


def attend_backward_kernel(
    head_width, q_ref, k_ref, v_ref, d_ref, lse_ref, low_ref, high_ref, place_ref, dq_ref, dk_ref, dv_ref
):
    @pl.when(pl.program_id(1) == 0)
    def _():
        dk_ref[...] = jnp.zeros_like(dk_ref)
        dv_ref[...] = jnp.zeros_like(dv_ref)

    place = place_ref[...]
    mask = (place >= low_ref[...]) & (place <= high_ref[...])
    dqs, dks, dvs = [], [], []
    for index, start in enumerate(range(0, q_ref.shape[1], head_width)):
        span = slice(start, start + head_width)
        q, k, v, d = q_ref[:, span], k_ref[:, span], v_ref[:, span], d_ref[:, span]
        across = (((1,), (1,)), ((), ()))
        down = (((0,), (0,)), ((), ()))
        scores = lax.dot_general(q, k, across, preferred_element_type=F32)
        weights = jnp.where(mask, jnp.exp(scores - lse_ref[0][:, index : index + 1]), 0.0)
        weight_grad = lax.dot_general(d, v, across, preferred_element_type=F32)
        delta = jnp.sum(weights * weight_grad, axis=1, keepdims=True)
        score_grad = (weights * (weight_grad - delta)).astype(LOW)
        dqs.append(jnp.dot(score_grad, k, preferred_element_type=F32))
        dks.append(lax.dot_general(score_grad, q, down, preferred_element_type=F32))
        dvs.append(lax.dot_general(weights.astype(LOW), d, down, preferred_element_type=F32))
    dq_ref[...] = (jnp.concatenate(dqs, axis=1).astype(LOW).astype(F32) * 0.125).astype(LOW)
    dk_ref[...] += jnp.concatenate(dks, axis=1)
    dv_ref[...] += jnp.concatenate(dvs, axis=1)


def attention_specs(rows, keys, width, head_width):
    block = min(128, width)
    step = min(rows, 256 if keys <= 1024 else 128)
    grid = (width // block, rows // step)
    q_spec = pl.BlockSpec((step, block), lambda j, i: (i, j))
    k_spec = pl.BlockSpec((keys, block), lambda j, i: (0, j))
    edge_spec = pl.BlockSpec((step, 1), lambda j, i: (i, 0))
    place_spec = pl.BlockSpec((1, keys), lambda j, i: (0, 0))
    lse_spec = pl.BlockSpec((1, step, block // head_width), lambda j, i: (j, i, 0))
    lse_shape = jax.ShapeDtypeStruct((width // block, rows, block // head_width), F32)
    params = pltpu.CompilerParams(vmem_limit_bytes=48 * 2**20)
    return grid, q_spec, k_spec, edge_spec, place_spec, lse_spec, lse_shape, params


def attend_forward(q, k, v, bounds, head_width):
    rows, width = q.shape
    keys = k.shape[0]
    grid, q_spec, k_spec, edge_spec, place_spec, lse_spec, lse_shape, params = attention_specs(
        rows, keys, width, head_width
    )
    return pl.pallas_call(
        partial(attend_forward_kernel, head_width),
        grid=grid,
        in_specs=[q_spec, k_spec, k_spec, edge_spec, edge_spec, place_spec],
        out_specs=[q_spec, lse_spec],
        out_shape=[jax.ShapeDtypeStruct((rows, width), LOW), lse_shape],
        compiler_params=params,
        cost_estimate=pl.CostEstimate(
            flops=4 * rows * keys * width,
            bytes_accessed=4 * (rows + keys) * width,
            transcendentals=rows * keys * width // head_width,
        ),
    )(q, k, v, *bounds)


def attend_backward(q, k, v, d, lse, bounds, head_width):
    rows, width = q.shape
    keys = k.shape[0]
    grid, q_spec, k_spec, edge_spec, place_spec, lse_spec, lse_shape, params = attention_specs(
        rows, keys, width, head_width
    )
    return pl.pallas_call(
        partial(attend_backward_kernel, head_width),
        grid=grid,
        in_specs=[q_spec, k_spec, k_spec, q_spec, lse_spec, edge_spec, edge_spec, place_spec],
        out_specs=[q_spec, k_spec, k_spec],
        out_shape=[
            jax.ShapeDtypeStruct((rows, width), LOW),
            jax.ShapeDtypeStruct((keys, width), F32),
            jax.ShapeDtypeStruct((keys, width), F32),
        ],
        compiler_params=params,
        cost_estimate=pl.CostEstimate(
            flops=10 * rows * keys * width,
            bytes_accessed=6 * (rows + 2 * keys) * width,
            transcendentals=rows * keys * width // head_width,
        ),
    )(q, k, v, d, lse, *bounds)


def layer_norm(values, gain_row, offset_row):
    center = values - jnp.mean(values, axis=-1, keepdims=True)
    spread = jnp.mean(center * center, axis=-1, keepdims=True)
    return center * lax.rsqrt(spread + EPSILON) * gain_row + offset_row


def layer_norm_back(values, gain_row, grad):
    center = values - jnp.mean(values, axis=-1, keepdims=True)
    inverse = lax.rsqrt(jnp.mean(center * center, axis=-1, keepdims=True) + EPSILON)
    normed = center * inverse
    scaled = grad * gain_row
    back = inverse * (
        scaled
        - jnp.mean(scaled, axis=-1, keepdims=True)
        - normed * jnp.mean(scaled * normed, axis=-1, keepdims=True)
    )
    return back, jnp.sum(grad * normed, axis=0), jnp.sum(grad, axis=0)


def dot(left, right):
    return jnp.dot(left, right, preferred_element_type=F32)


def dot_t(left, right):
    return lax.dot_general(left, right, (((1,), (1,)), ((), ())), preferred_element_type=F32)


def t_dot(left, right):
    return lax.dot_general(left, right, (((0,), (0,)), ((), ())), preferred_element_type=F32)


def column_sum(values):
    return jnp.sum(values.astype(F32), axis=0)


def stored_positions(row_index, row_count, dev_count):
    device = row_index // row_count
    offset = row_index % row_count
    half_rows = row_count // 2
    return jnp.where(
        offset < half_rows,
        device * half_rows + offset,
        (2 * dev_count - 1 - device) * half_rows + offset - half_rows,
    )


def ranges_of(starts, length):
    return starts, jnp.concatenate([starts[1:], jnp.full((1,), length, jnp.int32)]) - 1


def group_of(places, starts):
    return jnp.sum((starts[None, :] <= places[:, None]).astype(jnp.int32), axis=1) - 1


def pick(table, index):
    slots = jnp.arange(table.shape[0], dtype=jnp.int32)
    return jnp.sum(jnp.where(index[:, None] == slots[None, :], table[None, :], 0), axis=1)


def on_device(
    tokens,
    encoder_states,
    grad_out,
    doc_starts,
    source_doc,
    source_offsets,
    self_qkv,
    self_out,
    cross_q,
    cross_kv,
    cross_out,
    ffn_in,
    ffn_out,
    norm_gains,
    vec_biases,
    fc1_bias,
):
    n, m = lax.axis_size("ctx"), lax.axis_size("fsdp")
    c, f = lax.axis_index("ctx"), lax.axis_index("fsdp")
    layers = self_qkv.shape[0]
    rows, width = tokens.shape[1:]
    source_rows = encoder_states.shape[1]
    length, source_length = n * rows, n * source_rows
    hidden = ffn_out.shape[1] * m
    head_width = width // HEADS
    groups = min(n, HEADS)
    split = n // groups
    group, part = c // split, c % split
    own = width // groups
    col = width // n
    piece = hidden // (n * m)
    high_c, low_c = c // m, c % m

    slot_rows = ((c ^ jnp.arange(n, dtype=jnp.int32)) * rows)[:, None] + jnp.arange(
        rows, dtype=jnp.int32
    )[None, :]
    places = stored_positions(slot_rows.reshape(-1), rows, n)
    own_places = places.reshape(n // split, split, rows)[:, 0].reshape(-1)
    doc_low, doc_high = ranges_of(doc_starts[0], length)
    self_bounds = (
        pick(doc_low, group_of(own_places, doc_starts[0]))[:, None],
        own_places[:, None],
        places[None, :],
    )
    source_low, source_high = ranges_of(source_offsets[0], source_length)
    read_doc = pick(source_doc[0], group_of(places[:rows], doc_starts[0]))
    cross_bounds = (
        pick(source_low, read_doc)[:, None],
        pick(source_high, read_doc)[:, None],
        jnp.arange(source_length, dtype=jnp.int32)[None, :],
    )

    def columns(array, start, count):
        return lax.dynamic_slice_in_dim(array, start, count, 1)

    def fetch_self(layer):
        blocks = [columns(self_qkv[layer], i * width + group * own, own) for i in range(3)]
        return gather_planes(jnp.concatenate(blocks, axis=1))

    def fetch_cross(layer):
        kv = [columns(cross_kv[layer], i * width + c * col, col) for i in range(2)]
        got = gather_planes(
            jnp.concatenate(
                kv + [columns(cross_q[layer], c * col, col), columns(cross_out[layer], c * col, col)],
                axis=1,
            )
        )
        return got[:, : 2 * col], got[:, 2 * col :]

    def fetch_ffn(layer):
        up = ffn_in[layer].reshape(ffn_in.shape[1], m, n, piece)
        blocks = [
            lax.dynamic_index_in_dim(up[:, j], m * high_c + (j + low_c) % m, 1, False)
            for j in range(m)
        ]
        up = jnp.concatenate(blocks, axis=1)
        start = (m * high_c + (f + low_c) % m) * piece
        down = lax.dynamic_slice_in_dim(ffn_out[layer], start, piece, 0)
        return gather_planes(up), gather_planes(down)

    def fetch_out():
        here = self_out.shape[1]
        start = group * own
        source = start // here
        got = lax.dynamic_slice_in_dim(self_out, start % here, own, 1)
        bit = 1
        while bit < m:
            pairs = []
            for device in range(n):
                at = (device // split) * own // here
                for near in range(bit):
                    pairs.append((device * m + (at ^ near), device * m + (at ^ near ^ bit)))
            arrived = lax.ppermute(got, ("ctx", "fsdp"), pairs)
            got = jnp.where((f ^ source) // bit == 1, arrived, got)
            bit *= 2
        return got

    vectors = jnp.concatenate([norm_gains, vec_biases], axis=1).astype(LOW)
    vectors = lax.all_gather(vectors, "fsdp", axis=2, tiled=True).astype(F32)
    gains, biases = vectors[:, :3], vectors[:, 3:]
    up_bias = lax.dynamic_slice_in_dim(
        fc1_bias, (m * high_c + (f + low_c) % m) * piece, piece, 1
    )
    up_bias = lax.all_gather(up_bias, "fsdp", axis=1, tiled=True).astype(F32)
    w_out = fetch_out()
    weights = []
    for layer in range(layers):
        w_qkv = fetch_self(layer)
        w_kv, w_cross = fetch_cross(layer)
        w_up, w_down = fetch_ffn(layer)
        weights.append((w_qkv, w_out[layer], w_kv, w_cross, w_up, w_down))

    def own_slots(values):
        if split == 1:
            return values
        shaped = values.reshape((n // split, split, rows) + values.shape[1:])
        return shaped[:, 0].reshape((-1,) + values.shape[1:])

    def slots_of(values):
        shaped = values.reshape(n // split, 1, rows, values.shape[1])
        if split > 1:
            shaped = jnp.pad(shaped, ((0, 0), (0, split - 1), (0, 0), (0, 0)))
        return shaped.reshape(n, rows, values.shape[1])

    def share(parts):
        if split == 1:
            return parts[0]
        total = lax.dynamic_index_in_dim(parts, part, 0, False).astype(F32)
        for other in range(1, split):
            term = lax.dynamic_index_in_dim(parts, part ^ other, 0, False)
            total = total + swap(term, other).astype(F32)
        return total

    encoder_all = gather_slots(encoder_states[0]).reshape(source_length, width)
    grad_low = grad_out[0]

    x = tokens[0].astype(F32)
    kept = []
    for layer in range(layers):
        w_qkv, w_self_out, w_kv, w_cross, w_up, w_down = weights[layer]
        gain, bias = gains[layer], biases[layer]
        enc = dot(encoder_all, w_kv)
        enc = enc + jnp.concatenate([jnp.zeros((col,), F32), lax.dynamic_slice_in_dim(bias[7], c * col, col)])
        enc = turn(enc.astype(LOW), 0)
        enc_all = gather_slots(enc)
        ek = turn(jnp.concatenate([enc_all[k][:, :col] for k in range(n)], axis=1), 1)
        ev = turn(jnp.concatenate([enc_all[k][:, col:] for k in range(n)], axis=1), 1)
        cross_full = gather_slots(w_cross.T)
        cross_q_t = turn(cross_full[:, :col].reshape(width, width), 0)
        cross_out_t = turn(cross_full[:, col:].reshape(width, width), 0)

        h1 = layer_norm(x, gain[0], bias[0]).astype(LOW)
        h1_all = gather_slots(h1).reshape(length, width)
        z = dot(h1_all, w_qkv)
        q = own_slots((z[:, :own] + lax.dynamic_slice_in_dim(bias[3], group * own, own)) * 0.125)
        q = q.astype(LOW)
        k = z[:, own : 2 * own].astype(LOW)
        v = (z[:, 2 * own :] + lax.dynamic_slice_in_dim(bias[4], group * own, own)).astype(LOW)
        a, self_lse = attend_forward(q, k, v, self_bounds, head_width)
        x1 = x + reduce_slots(slots_of(dot(a, w_self_out))) + bias[5]
        h2 = layer_norm(x1, gain[1], bias[1]).astype(LOW)
        cq = ((dot_t(h2, cross_q_t) + bias[6]) * 0.125).astype(LOW)
        mixed, cross_lse = attend_forward(cq, ek, ev, cross_bounds, head_width)
        x2 = x1 + dot_t(mixed, cross_out_t) + bias[8]
        h3 = layer_norm(x2, gain[2], bias[2]).astype(LOW)
        h3_all = gather_slots(h3).reshape(length, width)
        u = dot(h3_all, w_up) + up_bias[layer]
        g = jax.nn.gelu(u, approximate=False).astype(LOW)
        y = x2 + reduce_slots(dot(g, w_down).reshape(n, rows, width)) + bias[9]
        kept.append(
            (x, x1, x2, h1_all, q, k, v, a, self_lse, h2, cq, ek, ev, mixed, cross_lse)
            + (h3_all, u, g, cross_q_t, cross_out_t)
        )
        x = y
    result = x.astype(LOW)

    grad_x = grad_low.astype(F32)
    enc_total = jnp.zeros((source_length, width), F32)
    grads = [None] * layers
    vec_rows = [None] * layers
    for layer in reversed(range(layers)):
        w_qkv, w_self_out, w_kv, w_cross, w_up, w_down = weights[layer]
        x, x1, x2, h1_all, q, k, v, a, self_lse, h2, cq, ek, ev, mixed, cross_lse = kept[layer][:15]
        h3_all, u, g, cross_q_t, cross_out_t = kept[layer][15:]
        gain = gains[layer]
        e3 = grad_x.astype(LOW)
        e3_all = gather_slots(e3).reshape(length, width)
        act_grad = dot_t(e3_all, w_down)
        unused, gelu_back = jax.vjp(partial(jax.nn.gelu, approximate=False), u)
        du = gelu_back(act_grad)[0].astype(LOW)
        dh3 = reduce_slots(dot_t(du, w_up).reshape(n, rows, width))
        down_grad = t_dot(g, e3_all).astype(LOW).reshape(m, piece, width)
        to_plane = [
            lax.dynamic_index_in_dim(down_grad, (p - low_c) % m, 0, False) for p in range(m)
        ]
        down_grad = jnp.stack(to_plane)
        up_grad = t_dot(h3_all, du).astype(LOW)
        up_grad = up_grad.reshape(n, m, width // (n * m), m * piece).transpose(1, 0, 2, 3)
        up_grad = up_grad.reshape(m, width // m, m * piece)
        fc1_grad = column_sum(du).reshape(m, piece)
        fc1_grad = jnp.stack(
            [lax.dynamic_index_in_dim(fc1_grad, (p - low_c) % m, 0, False) for p in range(m)]
        )
        back, gain_two, shift_two = layer_norm_back(x2, gain[2], dh3)
        dx2 = grad_x + back
        e2 = dx2.astype(LOW)
        d_mixed = dot(e2, cross_out_t).astype(LOW)
        dcq, dek, dev = attend_backward(cq, ek, ev, d_mixed, cross_lse, cross_bounds, head_width)
        dh2 = dot(dcq, cross_q_t)
        back, gain_one, shift_one = layer_norm_back(x1, gain[1], dh2)
        dx1 = dx2 + back
        e1 = dx1.astype(LOW)
        e1_all = gather_slots(e1).reshape(length, width)
        e1_own = own_slots(e1_all)
        d_a = dot_t(e1_own, w_self_out).astype(LOW)
        dq, dk, dv = attend_backward(q, k, v, d_a, self_lse, self_bounds, head_width)
        dkv = jnp.concatenate([dk, dv], axis=1).astype(LOW)
        if split > 1:
            shaped = dkv.reshape(n // split, split, rows, 2 * own)
            total = shaped[:, 0].astype(F32)
            for other in range(1, split):
                total = total + swap(shaped[:, other], other).astype(F32)
            dkv = total.astype(LOW).reshape(-1, 2 * own)
        dqkv = jnp.concatenate([dq, dkv], axis=1)
        dh1 = reduce_slots(slots_of(dot_t(dqkv, w_qkv)))
        back, gain_zero, shift_zero = layer_norm_back(x, gain[0], dh1)
        grad_x = dx1 + back

        dek_slots = turn(dek.astype(LOW), 1).reshape(source_length, n, col)
        dev_slots = turn(dev.astype(LOW), 1).reshape(source_length, n, col)
        dkv_cross = jnp.concatenate([dek_slots, dev_slots], axis=2).transpose(1, 0, 2)
        dkv_cross = reduce_slots(dkv_cross).astype(LOW)
        dkv_cross = turn(dkv_cross, 0)
        enc_total = enc_total + dot_t(dkv_cross, w_kv)
        kv_grad = t_dot(encoder_all, dkv_cross).astype(LOW)

        q_grad = t_dot(turn(h2, 1), dcq).reshape(n, col, width)
        out_grad = t_dot(turn(mixed, 1), e2).reshape(n, col, width)
        cross_grad = reduce_slots(jnp.concatenate([q_grad, out_grad], axis=1))
        cross_grad = cross_grad.reshape(2, m, col // m, width).transpose(1, 0, 2, 3)
        cross_grad = cross_grad.reshape(m, 2 * col // m, width).astype(LOW)

        qkv_grad = t_dot(own_slots(h1_all), dqkv).astype(LOW)
        qkv_grad = share(qkv_grad.reshape(width, 3, split, own // split).transpose(2, 0, 1, 3))
        qkv_grad = qkv_grad.astype(LOW).reshape(width, 3 * col)
        o_grad = share(t_dot(a, e1_own).astype(LOW).reshape(split, own // split, width))
        o_grad = o_grad.reshape(m, col // m, width).astype(LOW)

        def by_rows(grad):
            shaped = grad.reshape(n, m, width // (n * m), grad.shape[1]).transpose(1, 0, 2, 3)
            return shaped.reshape(m, width // m, grad.shape[1])

        def to_rows(summed):
            r = width // (n * m)
            return turn(exchange_slots(turn(summed, 0).reshape(n, r, summed.shape[1])).reshape(n * r, -1), 0).reshape(n, r, -1).transpose(1, 0, 2)

        down_sum = reduce_planes(down_grad)
        up_sum = reduce_planes(up_grad)
        cross_sum = reduce_planes(cross_grad)
        kv_sum = reduce_planes(by_rows(kv_grad))
        o_sum = reduce_planes(o_grad)
        qkv_sum = reduce_planes(by_rows(qkv_grad))
        fc1_sum = lax.psum_scatter(fc1_grad, "fsdp", scatter_dimension=0, tiled=False)
        moves = [
            (i * m + p, ((n // m) * ((p - i % m) % m) + i // m) * m + p)
            for i in range(n)
            for p in range(m)
        ]
        down_own = lax.ppermute(down_sum, ("ctx", "fsdp"), moves).astype(F32)
        fc1_own = lax.ppermute(fc1_sum, ("ctx", "fsdp"), moves)
        r = width // (n * m)
        up_own = to_rows(up_sum).astype(F32)
        up_own = up_own.reshape(r, n // m, m, m, piece)
        up_blocks = [
            jnp.stack([up_own[:, :, (s - j) % m, j] for s in range(m)], axis=2) for j in range(m)
        ]
        up_own = jnp.stack(up_blocks, axis=1).reshape(r, hidden)
        kv_own = to_rows(kv_sum).astype(F32).reshape(r, n, 2, col).transpose(0, 2, 1, 3)
        kv_own = kv_own.reshape(r, 2 * width)
        qkv_own = to_rows(qkv_sum).astype(F32).reshape(r, n, 3, col).transpose(0, 2, 1, 3)
        qkv_own = qkv_own.reshape(r, 3 * width)
        cross_own = cross_sum.reshape(2, col // m, width).astype(F32)
        grads[layer] = (
            qkv_own,
            o_sum.astype(F32),
            cross_own[0],
            kv_own,
            cross_own[1],
            up_own,
            down_own,
            fc1_own,
        )
        zero = jnp.zeros((width,), F32)
        summed = jnp.stack(
            [gain_zero, gain_one, gain_two, shift_zero, shift_one, shift_two]
            + [zero, zero, column_sum(e1), column_sum(dcq), zero, column_sum(e2), column_sum(e3)]
        )
        owned_q = share(column_sum(dq).reshape(split, col))
        owned_v = share(column_sum(dkv[:, own:]).reshape(split, col))
        owned_ev = column_sum(dkv_cross[:, col:])
        blank = jnp.zeros((col,), F32)
        owned = jnp.stack([blank] * 6 + [owned_q, owned_v, blank, blank, owned_ev, blank, blank])
        vec_rows[layer] = (summed, owned)

    enc_grad = reduce_slots(enc_total.reshape(n, source_rows, width), F32)
    summed = jnp.concatenate([pair[0] for pair in vec_rows])
    owned = jnp.concatenate([pair[1] for pair in vec_rows])
    summed = turn(summed, 1).reshape(-1, n, col).transpose(1, 0, 2)
    vec = reduce_slots(summed, F32) + owned
    vec = vec.reshape(-1, m, col // m).transpose(1, 0, 2)
    vec = lax.psum_scatter(vec, "fsdp", scatter_dimension=0, tiled=False)
    vec = vec.reshape(layers, -1, col // m)
    stacked = [jnp.stack([grads[layer][i] for layer in range(layers)]) for i in range(8)]
    return (
        (result[None], grad_x[None], enc_grad[None])
        + tuple(stacked[:7])
        + (vec[:, :3], vec[:, 3:], stacked[7])
    )


def solution(mesh):
    tokens = P("fsdp", "ctx", None)
    per_stream = P("fsdp", None)
    weight = P(None, "fsdp", None)
    vector = P(None, None, "fsdp")
    grad = P(None, ("ctx", "fsdp"), None)
    vector_grad = P(None, None, ("ctx", "fsdp"))
    return jax.shard_map(
        on_device,
        mesh=mesh,
        in_specs=(tokens,) * 3 + (per_stream,) * 3 + (weight,) * 7 + (vector,) * 2 + (P(None, "fsdp"),),
        out_specs=(tokens,) * 3 + (grad,) * 7 + (vector_grad,) * 2 + (P(None, ("ctx", "fsdp")),),
        check_vma=False,
    )
```

```python
from functools import partial

import jax
import jax.numpy as jnp
from jax import lax
from jax.experimental import pallas as pl
from jax.experimental.pallas import tpu as pltpu
from jax.sharding import PartitionSpec as P

HEADS = 16
EPSILON = 1e-05
NEGATIVE = -1e30
F32 = jnp.float32
LOW = jnp.bfloat16
VMEM = pl.BlockSpec(memory_space=pltpu.VMEM)
SMEM = pl.BlockSpec(memory_space=pltpu.SMEM)
FAR = pl.BlockSpec(memory_space=pl.ANY)
VMEM_BYTES = 56 * 2**20


def swap(values, bits):
    count = lax.axis_size("ctx")
    return lax.ppermute(values, "ctx", [(i, i ^ bits) for i in range(count)])


def gather_near(rows):
    if lax.axis_size("ctx") == 8:
        return swap(rows, 2), swap(rows, 4)
    return ()


def gather_slots(rows, near=None):
    count = lax.axis_size("ctx")
    if count == 8:
        near_x, near_y = near or gather_near(rows)
        half = rows.shape[0] // 2
        far = jnp.concatenate([swap(near_x[:half], 4), swap(near_y[half:], 2)])
        blocks = []
        for block in (rows, near_x, near_y, far):
            blocks += [block, swap(block, 1)]
        return blocks
    blocks = [rows]
    bit = 1
    while bit < count:
        blocks = blocks + [swap(block, bit) for block in blocks]
        bit *= 2
    return blocks


def gather_joined(rows, near):
    count = lax.axis_size("ctx")
    size = rows.shape[0]
    if count == 8:
        half = size // 2
        joined = swap(jnp.concatenate([rows, *near]), 1)
        far = jnp.concatenate([swap(near[0][:half], 4), swap(near[1][half:], 2)])
        arrays = [rows, *near, far, joined, swap(far, 1)]
        where = [(0, 0), (4, 0), (1, 0), (4, size), (2, 0), (4, 2 * size), (3, 0), (5, 0)]
        return arrays, where
    return gather_slots(rows), [(k, 0) for k in range(count)]


def send_chip(chip, kind):
    count = lax.axis_size("ctx")
    if count == 8:
        return [chip[0]] + [swap(chip[i].astype(kind), 2 * i) for i in (1, 2, 3)]
    bit = count // 4
    while bit:
        chip = chip[:bit] + swap(chip[bit : 2 * bit].astype(kind), 2 * bit).astype(F32)
        bit //= 2
    return [chip[0]]


def reduce_slots(even, odd, kind=LOW, hold=None):
    count = lax.axis_size("ctx")
    if isinstance(odd, list):
        odd = jnp.concatenate([swap(block, 1) for block in odd])
    else:
        odd = swap(odd.astype(kind), 1)
    chip = even.astype(F32) + odd.astype(F32)
    if count == 8:
        sent = [chip[i].astype(kind) for i in (1, 2, 3)]
        if hold is not None:
            sent = after(sent, hold)
        return [chip[0]] + [swap(sent[i], 2 * i + 2) for i in range(3)]
    bit = count // 4
    while bit:
        chip = chip[:bit] + swap(chip[bit : 2 * bit].astype(kind), 2 * bit).astype(F32)
        bit //= 2
    return [chip[0]]


def total_of(terms):
    total = terms[0].astype(F32)
    for term in terms[1:]:
        total = total + term.astype(F32)
    return total


def turn(values, axis):
    count = lax.axis_size("ctx")
    here = lax.axis_index("ctx")
    width = values.shape[axis] // count
    return jnp.concatenate(
        [
            lax.dynamic_slice_in_dim(values, (here ^ k) * width, width, axis)
            for k in range(count)
        ],
        axis=axis,
    )


def sum_planes(parts):
    count = lax.axis_size("fsdp")
    here = lax.axis_index("fsdp")
    total = lax.dynamic_index_in_dim(parts, here, 0, False)
    for step in range(1, count):
        term = lax.dynamic_index_in_dim(parts, (here + step) % count, 0, False)
        total = total + lax.ppermute(term, "fsdp", [(i, (i + step) % count) for i in range(count)])
    return total


def after(values, other):
    return lax.optimization_barrier((values, other))[0]


def gather_planes(values):
    return lax.all_gather(values, "fsdp", axis=0, tiled=True)


def reduce_planes(parts):
    return lax.psum_scatter(parts, "fsdp", scatter_dimension=0, tiled=False)


def layer_norm(values, gain_row, offset_row):
    center = values - jnp.mean(values, axis=-1, keepdims=True)
    spread = jnp.mean(center * center, axis=-1, keepdims=True)
    return center * lax.rsqrt(spread + EPSILON) * gain_row + offset_row


def layer_norm_back(values, gain_row, grad):
    center = values - jnp.mean(values, axis=-1, keepdims=True)
    inverse = lax.rsqrt(jnp.mean(center * center, axis=-1, keepdims=True) + EPSILON)
    normed = center * inverse
    scaled = grad * gain_row
    back = inverse * (
        scaled
        - jnp.mean(scaled, axis=-1, keepdims=True)
        - normed * jnp.mean(scaled * normed, axis=-1, keepdims=True)
    )
    return back, row_sum(grad * normed), row_sum(grad)


def row_sum(values):
    return jnp.sum(values.astype(F32), axis=0, keepdims=True)


def dot(left, right):
    return jnp.dot(left, right, preferred_element_type=F32)


def dot_t(left, right):
    return lax.dot_general(left, right, (((1,), (1,)), ((), ())), preferred_element_type=F32)


def t_dot(left, right):
    return lax.dot_general(left, right, (((0,), (0,)), ((), ())), preferred_element_type=F32)


def call(kernel, ins, outs, flops, scratch=(), smem=0, far=0, wait=()):
    count, extra = len(ins), len(wait)

    def body(*refs):
        kernel(*refs[:count], *refs[count + extra :])

    moved = sum(a.size * a.dtype.itemsize for a in ins)
    moved += sum(a.size * a.dtype.itemsize for a in outs)
    return pl.pallas_call(
        body,
        in_specs=[SMEM] * smem + [VMEM] * (count - smem - far) + [FAR] * (far + extra),
        out_specs=[VMEM] * len(outs),
        out_shape=outs,
        scratch_shapes=list(scratch),
        compiler_params=pltpu.CompilerParams(vmem_limit_bytes=VMEM_BYTES),
        cost_estimate=pl.CostEstimate(flops=int(flops), bytes_accessed=int(moved), transcendentals=0),
    )(*ins, *wait)


def like(shape, kind):
    return jax.ShapeDtypeStruct(tuple(shape), kind)


def tile_rows(rows, size):
    return pl.ds(pl.multiple_of(rows * size, size), size)


def put_slots(even_ref, odd_ref, index, values):
    rows = even_ref.shape[1]
    even_ref[index] = values[:rows].astype(LOW)
    odd_ref[index] = values[rows:].astype(LOW)


def self_forward_kernel(n, rows, split, raw, joined, head_width, *refs):
    blocks, refs = refs[:n], refs[n:]
    vec_ref, bias_ref, w_ref, low_ref, high_ref, place_ref = refs[:6]
    (wo_ref, *refs) = refs[6:] if joined else (None, *refs[6:])
    h_ref, q_ref, k_ref, v_ref, a_ref, lse_ref, *out_refs = refs
    own = k_ref.shape[1]
    for k in range(n):
        block = blocks[k][:rows]
        if raw:
            block = layer_norm(block.astype(F32), vec_ref[0:1], vec_ref[3:4]).astype(LOW)
        h_ref[k * rows : (k + 1) * rows] = block

    @pl.loop(0, n // 2)
    def _(i):
        at = tile_rows(i, 2 * rows)
        z = dot(h_ref[at], w_ref[:, : 3 * own])
        q = ((z[:, :own] + bias_ref[0:1]) * 0.125).astype(LOW)
        if split == 1:
            q_ref[at] = q
        else:
            q_ref[tile_rows(i, rows)] = q[:rows]
        k_ref[at] = z[:, own : 2 * own].astype(LOW)
        v_ref[at] = (z[:, 2 * own :] + bias_ref[1:2]).astype(LOW)

    step = 2 * rows // split

    @pl.loop(0, n // 2)
    def _(i):
        at = tile_rows(i, step)
        mask = (place_ref[...] >= low_ref[at]) & (place_ref[...] <= high_ref[at])
        outs, masses = [], []
        for start in range(0, own, head_width):
            span = slice(start, start + head_width)
            scores = jnp.where(mask, dot_t(q_ref[at, span], k_ref[:, span]), NEGATIVE)
            top = jnp.max(scores, axis=1, keepdims=True)
            raised = jnp.exp(scores - top)
            mass = jnp.sum(raised, axis=1, keepdims=True)
            outs.append(dot((raised * (1.0 / mass)).astype(LOW), v_ref[:, span]))
            masses.append(top + jnp.log(mass))
        a = jnp.concatenate(outs, axis=1).astype(LOW)
        a_ref[at] = a
        lse_ref[at] = jnp.concatenate(masses, axis=1)
        if joined:
            put_product(split, a, wo_ref, *out_refs, i)


def put_product(split, a, wo_ref, even_ref, odd_ref, i):
    y = dot(a, wo_ref[...])
    if split > 1:
        y = jnp.concatenate([y, jnp.zeros_like(y)])
    put_slots(even_ref, odd_ref, i, y)


def self_out_kernel(n, rows, split, a_ref, wo_ref, even_ref, odd_ref):
    step = 2 * rows // split

    @pl.loop(0, n // 2)
    def _(i):
        put_product(split, a_ref[tile_rows(i, step)], wo_ref, even_ref, odd_ref, i)


def mid_forward_kernel(n, terms, arrays, where, head_width, here_ref, *refs):
    x_ref, refs = refs[0], refs[1:]
    term_refs, refs = refs[:terms], refs[terms:]
    w_refs, refs = refs[:arrays], refs[arrays:]
    vec_ref, low_ref, high_ref, place_ref = refs[:4]
    x1_ref, x2_ref, h2_ref, cq_ref, c_ref, lse_ref, h3_ref = refs[4:11]
    wq_ref, wo_ref, ek_ref, ev_ref = refs[11:]
    col = w_refs[0].shape[0] // 2
    width = wq_ref.shape[1]
    here = here_ref[0]
    for k in range(n):
        at = tile_rows(here ^ k, col)
        array, first = where[k]
        top, bottom = pl.ds(first, col), pl.ds(first + col, col)
        wq_ref[at] = w_refs[array][top, :width]
        wo_ref[at] = w_refs[array][bottom, :width]
        ek_ref[at] = w_refs[array][top, width:]
        ev_ref[at] = w_refs[array][bottom, width:]
    x1 = x_ref[...].astype(F32) + total_of([t[...] for t in term_refs]) + vec_ref[8:9]
    x1_ref[...] = x1
    h2 = layer_norm(x1, vec_ref[1:2], vec_ref[4:5]).astype(LOW)
    h2_ref[...] = h2
    cq_ref[...] = ((dot_t(h2, wq_ref[...]) + vec_ref[9:10]) * 0.125).astype(LOW)
    mask = (place_ref[...] >= low_ref[...]) & (place_ref[...] <= high_ref[...])
    outs, masses = [], []
    for start in range(0, cq_ref.shape[1], head_width):
        span = slice(start, start + head_width)
        scores = jnp.where(mask, dot(cq_ref[:, span], ek_ref[span]), NEGATIVE)
        top = jnp.max(scores, axis=1, keepdims=True)
        raised = jnp.exp(scores - top)
        mass = jnp.sum(raised, axis=1, keepdims=True)
        outs.append(dot_t((raised * (1.0 / mass)).astype(LOW), ev_ref[span]))
        masses.append(top + jnp.log(mass))
    c_ref[...] = jnp.concatenate(outs, axis=1).astype(LOW)
    lse_ref[...] = jnp.concatenate(masses, axis=1)
    x2 = x1 + dot_t(c_ref[...], wo_ref[...]) + vec_ref[11:12]
    x2_ref[...] = x2
    h3_ref[...] = layer_norm(x2, vec_ref[2:3], vec_ref[5:6]).astype(LOW)


def copies_of(sources, up_ref, down_ref, sems):
    if len(sources) == 2:
        pairs = [(sources[0], up_ref), (sources[1], down_ref)]
    else:
        planes, both = sources[0].shape[:2]
        size = up_ref.shape[0] // planes
        pairs = []
        for j in range(planes):
            at = pl.ds(j * size, size)
            pairs.append((sources[0].at[j, pl.ds(0, size)], up_ref.at[at]))
            pairs.append((sources[0].at[j, pl.ds(size, size)], down_ref.at[at]))
    return [pltpu.make_async_copy(a, b, sems.at[i]) for i, (a, b) in enumerate(pairs)]


def ffn_forward_kernel(n, sources, *refs):
    blocks, refs = refs[:n], refs[n:]
    bias_ref, refs = refs[0], refs[1:]
    sources, refs = refs[:sources], refs[sources:]
    h_ref, g_ref, slope_ref, even_ref, odd_ref, up_ref, down_ref, sems = refs
    rows = blocks[0].shape[0]
    copies = copies_of(sources, up_ref, down_ref, sems)
    for copy in copies:
        copy.start()
    for k in range(n):
        h_ref[k * rows : (k + 1) * rows] = blocks[k][...]
    for copy in copies:
        copy.wait()

    @pl.loop(0, n // 2)
    def _(i):
        at = tile_rows(i, 2 * rows)
        u = dot(h_ref[at], up_ref[...]) + bias_ref[...]
        share = 0.5 + 0.5 * lax.erf(u * 0.7071067811865476)
        g = (u * share).astype(LOW)
        g_ref[at] = g
        slope_ref[at] = (share + u * (jnp.exp(-0.5 * u * u) * 0.3989422804014327)).astype(LOW)
        put_slots(even_ref, odd_ref, i, dot(g, down_ref[...]))


def ffn_backward_kernel(n, sources, *refs):
    blocks, refs = refs[:n], refs[n:]
    slope_ref, refs = refs[0], refs[1:]
    sources, refs = refs[:sources], refs[sources:]
    e_ref, du_ref, sum_ref, even_ref, odd_ref, up_ref, down_ref, sems = refs
    rows = blocks[0].shape[0]
    copies = copies_of(sources, up_ref, down_ref, sems)
    for copy in copies:
        copy.start()
    for k in range(n):
        e_ref[k * rows : (k + 1) * rows] = blocks[k][...]
    sum_ref[...] = jnp.zeros_like(sum_ref)
    for copy in copies:
        copy.wait()

    @pl.loop(0, n // 2)
    def _(i):
        at = tile_rows(i, 2 * rows)
        du = (dot_t(e_ref[at], down_ref[...]) * slope_ref[at].astype(F32)).astype(LOW)
        du_ref[at] = du
        sum_ref[...] += row_sum(du)
        put_slots(even_ref, odd_ref, i, dot_t(du, up_ref[...]))


def pack_kernel(m, n, jobs, where_ref, *refs):
    count = sum(len(FED[kind]) for kind, layer in jobs)
    sources, packed, sems = refs[:count], refs[count:-1], refs[-1]
    c, f = where_ref[0], where_ref[1]
    high, low = c // m, c % m
    copies = []

    def add(source, target):
        copies.append(pltpu.make_async_copy(source, target, sems.at[len(copies)]))

    def columns(start, size):
        return pl.ds(pl.multiple_of(start, 128), size)

    for (kind, layer), target in zip(jobs, packed):
        fed, sources = sources[: len(FED[kind])], sources[len(FED[kind]) :]
        at = 0
        if kind == "ffn":
            up, down = fed
            rows, piece = up.shape[1], down.shape[1] // n
            for j in range(m):
                start = (n * j + m * high + (j + low) % m) * piece
                add(up.at[layer, :, columns(start, piece)], target.at[pl.ds(0, rows), pl.ds(j * piece, piece)])
            start = (m * high + (f + low) % m) * piece
            add(down.at[layer, pl.ds(pl.multiple_of(start, piece), piece)], target.at[pl.ds(rows, piece)])
            continue
        for source, (name, parts) in zip(fed, FED[kind].items()):
            if parts == 0:
                add(source, target.at[:, pl.ds(at, source.shape[1])])
                continue
            width = source.shape[2] // parts
            col = width // n
            if name == "self_out":
                for l in range(source.shape[0]):
                    add(source.at[l, :, columns(c * col, col)], target.at[:, pl.ds(at, col)])
                    at += col
                continue
            for i in range(parts):
                add(source.at[layer, :, columns(i * width + c * col, col)], target.at[:, pl.ds(at, col)])
                at += col
    for copy in copies:
        copy.start()
    for copy in copies:
        copy.wait()


FED = {
    "first": {"qkv": 3, "kv": 2, "q": 1, "out": 1, "self_out": 1, "vec": 0},
    "attention": {"qkv": 3, "kv": 2, "q": 1, "out": 1},
    "ffn": {"up": 1, "down": 1},
}


def late_kernel(*refs):
    out_ref = refs[-1]
    size = out_ref.shape[1] // (len(refs) - 1)
    for layer, ref in enumerate(refs[:-1]):
        out_ref[:, layer * size : (layer + 1) * size] = ref[:, :size]


def copy_kernel(in_ref, out_ref):
    out_ref[...] = in_ref[...]


def assemble_kernel(n, skip, here_ref, *refs):
    out_ref = refs[n]
    size = refs[0].shape[0] - skip
    for k in range(n):
        out_ref[tile_rows(here_ref[0] ^ k, size)] = refs[k][skip:]


def cross_prepare_kernel(col, skip, w_ref, enc_ref, bias_ref, out_ref):
    kv = dot(enc_ref[...], w_ref[:, skip : skip + 2 * col]) + bias_ref[...]
    width = w_ref.shape[0]
    out_ref[:, width:] = kv.T.astype(LOW)
    out_ref[:, :width] = w_ref[:, skip + 2 * col : skip + 4 * col].astype(F32).T.astype(LOW)


def between_kernel(terms, last, *refs):
    x2_ref, refs = refs[0], refs[1:]
    term_refs, refs = refs[:terms], refs[terms:]
    y = x2_ref[...] + total_of([t[...] for t in term_refs]) + refs[0][12:13]
    if last:
        refs[1][...] = y.astype(LOW)
    else:
        next_ref, y_ref, h_ref = refs[1:]
        y_ref[...] = y
        h_ref[...] = layer_norm(y, next_ref[0:1], next_ref[3:4]).astype(LOW)


def put_folded(out_ref, grad, at, n, m):
    size, width = grad.shape[0] // m, grad.shape[1] // n
    for p in range(m):
        for i in range(n):
            block = grad[p * size : (p + 1) * size, i * width : (i + 1) * width]
            out_ref[p, i * size : (i + 1) * size, at : at + width] = block


def attention_weights_kernel(n, m, skip, terms, full, here_ref, *refs):
    w_refs, refs = refs[:terms], refs[terms:]
    own_refs, refs = (refs[:5], refs[5:]) if full else ((), refs)
    enc_ref, w_kv_ref, before_ref, out_ref, total_ref, sum_ref, even_ref, odd_ref = refs
    col = w_refs[0].shape[0] // 2
    width = w_kv_ref.shape[0]
    grad = total_of([t[:, :width] for t in w_refs]).astype(LOW)
    for i in range(2):
        at = (5 + i if full else 2 + i) * col
        put_folded(out_ref, grad[i * col : (i + 1) * col], at, n, m)
    dkv_t = total_of([t[:, width:] for t in w_refs])
    sum_ref[...] = jnp.sum(dkv_t.astype(LOW).astype(F32), axis=1, keepdims=True)
    dkv = dkv_t.T.astype(LOW)
    total_ref[...] = before_ref[...] + dot_t(dkv, w_kv_ref[:, skip : skip + 2 * col])
    put_by_rows(out_ref, t_dot(enc_ref[...], dkv).astype(LOW), 0, width, n, m)
    for k in range(n):
        part = total_ref[tile_rows(here_ref[0] ^ k, even_ref.shape[1])]
        (odd_ref if k % 2 else even_ref)[k // 2] = part
    if not full:
        return
    h_ref, dq_ref, dkv_ref, a_ref, e_ref = own_refs
    own = dq_ref.shape[1]
    step = min(256, width)
    for first in range(0, width, step):
        part = h_ref[:, first : first + step]
        grad = jnp.concatenate([t_dot(part, dq_ref[...]), t_dot(part, dkv_ref[...])], axis=1)
        put_by_rows(out_ref, grad.astype(LOW), first, width, n, m, 2 * own)
    put_folded(out_ref, t_dot(a_ref[...], e_ref[...]).astype(LOW), 7 * own, n, m)


def put_by_rows(out_ref, grad, first, total, n, m, at=0):
    size = total // (n * m)
    for i in range(grad.shape[0] // size):
        block = first // size + i
        device, plane = block // m, block % m
        part = grad[i * size : (i + 1) * size]
        out_ref[plane, device * size : (device + 1) * size, at : at + grad.shape[1]] = part


def ffn_weights_kernel(n, m, here_ref, h_ref, du_ref, g_ref, e_ref, sum_ref, up_ref, down_ref=None):
    piece = g_ref.shape[1] // m
    low = here_ref[0] % m
    first = h_ref.shape[1] // m if down_ref is None else 0
    down_ref = up_ref if down_ref is None else down_ref
    for j in range(m):
        plane = (low + j) % m
        grad = t_dot(g_ref[:, j * piece : (j + 1) * piece], e_ref[...]).astype(LOW)
        down_ref[plane, first : first + piece] = grad
        part = sum_ref[:, j * piece : (j + 1) * piece].astype(LOW)
        down_ref[plane, first + piece :] = jnp.zeros((16, down_ref.shape[2]), LOW)
        down_ref[plane, first + piece : first + piece + 1, :piece] = part
    step = min(256, h_ref.shape[1])
    for first in range(0, h_ref.shape[1], step):
        grad = t_dot(h_ref[:, first : first + step], du_ref[...]).astype(LOW)
        put_by_rows(up_ref, grad, first, h_ref.shape[1], n, m)


def mid_backward_kernel(n, terms, head_width, here_ref, *refs):
    dy_ref, refs = refs[0], refs[1:]
    term_refs, refs = refs[:terms], refs[terms:]
    x1_ref, x2_ref, vec_ref, wq_ref, wo_ref, ek_ref, ev_ref, cq_ref, lse_ref = refs[:9]
    low_ref, high_ref, place_ref = refs[9:12]
    dx1_ref, e1_ref, e2_ref, dcq_ref, even_ref, odd_ref, sum_ref = refs[12:19]
    dek_ref, dev_ref = refs[19:]
    col = even_ref.shape[1] // 2
    dy = dy_ref[...].astype(F32)
    back, gain_two, shift_two = layer_norm_back(
        x2_ref[...], vec_ref[2:3], total_of([t[...] for t in term_refs])
    )
    dx2 = dy + back
    e2 = dx2.astype(LOW)
    e2_ref[...] = e2
    d_all = dot(e2, wo_ref[...]).astype(LOW)
    mask = (place_ref[...] >= low_ref[...]) & (place_ref[...] <= high_ref[...])
    dqs = []
    for index, start in enumerate(range(0, cq_ref.shape[1], head_width)):
        span = slice(start, start + head_width)
        q, d, ek, ev = cq_ref[:, span], d_all[:, span], ek_ref[span], ev_ref[span]
        weights = jnp.where(mask, jnp.exp(dot(q, ek) - lse_ref[:, index : index + 1]), 0.0)
        weight_grad = dot(d, ev)
        delta = jnp.sum(weights * weight_grad, axis=1, keepdims=True)
        score_grad = (weights * (weight_grad - delta)).astype(LOW)
        dqs.append(dot_t(score_grad, ek))
        dek_ref[span] = t_dot(q, score_grad).astype(LOW)
        dev_ref[span] = t_dot(d, weights.astype(LOW)).astype(LOW)
    dcq = (jnp.concatenate(dqs, axis=1).astype(LOW).astype(F32) * 0.125).astype(LOW)
    dcq_ref[...] = dcq
    here = here_ref[0]
    for k in range(n):
        at = tile_rows(here ^ k, col)
        out = odd_ref if k % 2 else even_ref
        out[k // 2, :col] = dek_ref[at]
        out[k // 2, col:] = dev_ref[at]
    back, gain_one, shift_one = layer_norm_back(x1_ref[...], vec_ref[1:2], dot(dcq, wq_ref[...]))
    dx1 = dx2 + back
    dx1_ref[...] = dx1
    e1 = dx1.astype(LOW)
    e1_ref[...] = e1
    sums = [gain_one, gain_two, shift_one, shift_two]
    sums += [row_sum(e1), row_sum(dcq), row_sum(e2), row_sum(dy)]
    sum_ref[...] = jnp.concatenate(sums, axis=0)


def cross_weights_kernel(n, here_ref, h_ref, dcq_ref, c_ref, e_ref, kv_even, kv_odd, even_ref, *refs):
    odd_refs, (q_ref, o_ref) = refs[:2], refs[2:]
    col = even_ref.shape[1] // 2
    width = q_ref.shape[1]
    q_ref[...] = t_dot(h_ref[...], dcq_ref[...]).astype(LOW)
    o_ref[...] = t_dot(c_ref[...], e_ref[...]).astype(LOW)
    here = here_ref[0]
    for k in range(n):
        at = tile_rows(here ^ k, col)
        out, i = (odd_refs[2 * k // n], k // 2 % (n // 4)) if k % 2 else (even_ref, k // 2)
        out[i, :col, :width] = q_ref[at]
        out[i, col:, :width] = o_ref[at]
    even_ref[:, :, width:] = kv_even[...]
    for i in range(2):
        odd_refs[i][:, :, width:] = kv_odd[i * n // 4 : (i + 1) * n // 4]


def self_backward_kernel(n, split, head_width, *refs):
    blocks, refs = refs[:n], refs[n:]
    wo_ref, w_ref, q_ref, k_ref, v_ref, lse_ref, low_ref, high_ref, place_ref = refs[:9]
    e_ref, dq_ref, dkv_ref, even_ref, odd_ref, dk_ref, dv_ref = refs[9:]
    rows = blocks[0].shape[0]
    own = wo_ref.shape[0]
    for i, k in enumerate(range(0, n, split)):
        e_ref[i * rows : (i + 1) * rows] = blocks[k][...]
    dk_ref[...] = jnp.zeros_like(dk_ref)
    dv_ref[...] = jnp.zeros_like(dv_ref)
    step = 2 * rows // split

    @pl.loop(0, n // 2)
    def _(i):
        at = tile_rows(i, step)
        mask = (place_ref[...] >= low_ref[at]) & (place_ref[...] <= high_ref[at])
        d_all = dot_t(e_ref[at], wo_ref[...]).astype(LOW)
        dqs, dks, dvs = [], [], []
        for index, start in enumerate(range(0, own, head_width)):
            span = slice(start, start + head_width)
            q, k, v, d = q_ref[at, span], k_ref[:, span], v_ref[:, span], d_all[:, span]
            weights = jnp.where(mask, jnp.exp(dot_t(q, k) - lse_ref[at, index : index + 1]), 0.0)
            weight_grad = dot_t(d, v)
            delta = jnp.sum(weights * weight_grad, axis=1, keepdims=True)
            score_grad = (weights * (weight_grad - delta)).astype(LOW)
            dqs.append(dot(score_grad, k))
            dks.append(t_dot(score_grad, q))
            dvs.append(t_dot(weights.astype(LOW), d))
        dq = jnp.concatenate(dqs, axis=1).astype(LOW).astype(F32) * 0.125
        dq_ref[at] = dq.astype(LOW)
        dk_ref[...] += jnp.concatenate(dks, axis=1)
        dv_ref[...] += jnp.concatenate(dvs, axis=1)

    dkv_ref[:, :own] = dk_ref[...].astype(LOW)
    dkv_ref[:, own:] = dv_ref[...].astype(LOW)
    if split > 1:
        return

    @pl.loop(0, n // 2)
    def _(i):
        at = tile_rows(i, 2 * rows)
        put_slots(
            even_ref, odd_ref, i, dot_t(dq_ref[at], w_ref[:, :own]) + dot_t(dkv_ref[at], w_ref[:, own : 3 * own])
        )


def place_ffn_kernel(n, m, layers, *refs):
    up_refs, down_refs = refs[:layers], refs[layers : 2 * layers]
    up_out, down_out, fc1_out = refs[2 * layers :]
    piece = fc1_out.shape[1]
    for layer in range(layers):
        down_out[layer] = down_refs[layer][:piece].astype(F32)
        fc1_out[layer : layer + 1] = down_refs[layer][piece : piece + 16, :piece].astype(F32)[:1]
        for device in range(n):
            high, low = device // m, device % m
            for j in range(m):
                at = (n * j + m * high + (j + low) % m) * piece
                block = up_refs[layer][device, :, j * piece : (j + 1) * piece]
                up_out[layer, :, at : at + piece] = block.astype(F32)


def place_attention_kernel(n, layers, *refs):
    late, both, outs = refs[0], refs[1 : layers + 1], refs[layers + 1 :]
    qkv_out, o_out, q_out, kv_out, cross_out = outs
    col = both[0].shape[1] // 8
    rows = both[0].shape[0] // n
    for layer in range(layers):
        for i in range(n):
            for part in range(5):
                out, at = (kv_out, part) if part < 2 else (qkv_out, part - 2)
                start = (5 * layer + part) * col
                block = late[i, :, start : start + col]
                out[layer, :, (at * n + i) * col : (at * n + i + 1) * col] = block.astype(F32)
            for out, part in ((q_out, 5), (cross_out, 6), (o_out, 7)):
                block = both[layer][i * rows : (i + 1) * rows, part * col : (part + 1) * col]
                out[layer, :, i * col : (i + 1) * col] = block.astype(F32)


def last_backward_kernel(terms, *refs):
    dx1_ref, refs = refs[0], refs[1:]
    term_refs, refs = refs[:terms], refs[terms:]
    x_ref, vec_ref, dx_ref, e_ref, sum_ref = refs
    back, gain, shift = layer_norm_back(
        x_ref[...].astype(F32), vec_ref[0:1], total_of([t[...] for t in term_refs])
    )
    dx = dx1_ref[...] + back
    dx_ref[...] = dx
    e_ref[...] = dx.astype(LOW)
    sum_ref[...] = jnp.concatenate([gain, shift], axis=0)


def stored_positions(row_index, row_count, dev_count):
    device = row_index // row_count
    offset = row_index % row_count
    half_rows = row_count // 2
    return jnp.where(
        offset < half_rows,
        device * half_rows + offset,
        (2 * dev_count - 1 - device) * half_rows + offset - half_rows,
    )


def ranges_of(starts, length):
    return starts, jnp.concatenate([starts[1:], jnp.full((1,), length, jnp.int32)]) - 1


def group_of(places, starts):
    return jnp.sum((starts[None, :] <= places[:, None]).astype(jnp.int32), axis=1) - 1


def pick(table, index):
    slots = jnp.arange(table.shape[0], dtype=jnp.int32)
    return jnp.sum(jnp.where(index[:, None] == slots[None, :], table[None, :], 0), axis=1)


def on_device(
    tokens,
    encoder_states,
    grad_out,
    doc_starts,
    source_doc,
    source_offsets,
    self_qkv,
    self_out,
    cross_q,
    cross_kv,
    cross_out,
    ffn_in,
    ffn_out,
    norm_gains,
    vec_biases,
    fc1_bias,
):
    n, m = lax.axis_size("ctx"), lax.axis_size("fsdp")
    c, f = lax.axis_index("ctx"), lax.axis_index("fsdp")
    layers = self_qkv.shape[0]
    rows, width = tokens.shape[1:]
    source_rows = encoder_states.shape[1]
    length, source_length = n * rows, n * source_rows
    held = self_out.shape[1]
    hidden = ffn_out.shape[1] * m
    head_width = width // HEADS
    groups = min(n, HEADS)
    split = n // groups
    group, part = c // split, c % split
    own = width // groups
    col = width // n
    piece = hidden // (n * m)
    units = m * piece
    high_c, low_c = c // m, c % m
    here = jnp.stack([c, f]).astype(jnp.int32)
    queries = length // split
    packs = split == 1 and col % 128 == 0 and units == width and piece == held

    slot_rows = ((c ^ jnp.arange(n, dtype=jnp.int32)) * rows)[:, None] + jnp.arange(
        rows, dtype=jnp.int32
    )[None, :]
    places = stored_positions(slot_rows.reshape(-1), rows, n)
    own_places = places.reshape(n // split, split, rows)[:, 0].reshape(-1)
    doc_low, doc_high = ranges_of(doc_starts[0], length)
    self_bounds = [
        pick(doc_low, group_of(own_places, doc_starts[0]))[:, None],
        own_places[:, None],
        places[None, :],
    ]
    source_low, source_high = ranges_of(source_offsets[0], source_length)
    read_doc = pick(source_doc[0], group_of(places[:rows], doc_starts[0]))
    cross_bounds = [
        pick(source_low, read_doc)[:, None],
        pick(source_high, read_doc)[:, None],
        jnp.arange(source_length, dtype=jnp.int32)[None, :],
    ]

    def fetch_out():
        start = group * own
        got = lax.dynamic_slice(self_out, (0, start % held, 0), (layers, own, width))
        got = jnp.where(f == start // held, got, jnp.zeros_like(got))
        covered = [{(device // split) * own // held} for device in range(n)]
        while any(len(planes) < m for planes in covered):
            pairs = []
            for device, planes in enumerate(covered):
                reached = set()
                for plane in sorted(planes):
                    free = [p for p in (plane + 1, plane - 1) if 0 <= p < m and p not in planes | reached]
                    if free:
                        reached.add(free[0])
                        pairs.append((device * m + plane, device * m + free[0]))
                planes |= reached
            got = got + lax.ppermute(got, ("ctx", "fsdp"), pairs)
        return got

    def columns(array, layer, start, count):
        return lax.dynamic_slice(array, (layer, 0, start), (1, array.shape[1], count))[0]

    first_rows = jnp.concatenate([tokens[0], encoder_states[0]])
    first_slots = gather_slots(first_rows)
    unit_start = (m * high_c + (f + low_c) % m) * piece
    last_slots = gather_slots(after(grad_out[0], first_slots))
    vec_rows = jnp.concatenate([norm_gains, vec_biases], axis=1)
    fc1_rows = lax.dynamic_slice(fc1_bias, (0, unit_start), (layers, piece))
    fc1_rows = jnp.pad(fc1_rows, ((0, 0), (0, held - piece)))
    vec_rows = jnp.concatenate([vec_rows.reshape(-1, held), fc1_rows])
    if packs:
        arrays = dict(qkv=self_qkv, kv=cross_kv, q=cross_q, out=cross_out, up=ffn_in, down=ffn_out)
        arrays["self_out"] = self_out
        arrays["vec"] = jnp.pad(vec_rows.T, ((0, 0), (0, 128 - vec_rows.shape[0])))
        first_size = (7 + layers) * col
        sizes = {
            "first": (held, first_size + 128),
            "attention": (held, 7 * col),
            "ffn": (held + piece, units),
        }

        def pack(jobs, wait=()):
            fed = [arrays[name] for kind, layer in jobs for name in FED[kind]]
            return call(
                partial(pack_kernel, m, n, jobs),
                [here] + fed,
                [like(sizes[kind], LOW) for kind, layer in jobs],
                0,
                scratch=[pltpu.SemaphoreType.DMA((8 * len(jobs) + 8,))],
                smem=1,
                far=len(fed),
                wait=wait,
            )

        packed = pack([("first", 0)])
        packed += pack([("ffn", 0)], [first_slots[-1], last_slots[-1]])
        for layer in range(1, layers):
            packed += pack([("attention", layer), ("ffn", layer)])
        got = []
        for index, operand in enumerate(packed):
            if index > 1:
                operand = after(operand, got[index - 2])
            tiled = operand.shape[0] == held
            got.append(lax.all_gather(operand, "fsdp", axis=0, tiled=tiled))
        w_qkv = w_rest = got[0::2]
        w_ffn = [[both] for both in got[1::2]]
        skip = [3 * col] * layers
        ordered = got[0][:, first_size : first_size + vec_rows.shape[0]].T.astype(F32)
        w_out = got[0][:, 7 * col : first_size].reshape(n, col, layers, col)
        w_out = lax.all_to_all(w_out, "ctx", 0, 0).transpose(2, 1, 0, 3).reshape(layers, col, width)
    else:
        w_out = fetch_out()
        ordered = gather_planes(vec_rows.T).T.astype(F32)
        w_qkv, w_rest, w_ffn, skip = [], [], [], [0] * layers
        for layer in range(layers):
            blocks = [columns(self_qkv, layer, i * width + group * own, own) for i in range(3)]
            w_qkv.append(gather_planes(jnp.concatenate(blocks, axis=1)))
            blocks = [columns(cross_kv, layer, i * width + c * col, col) for i in range(2)]
            blocks += [columns(cross_q, layer, c * col, col), columns(cross_out, layer, c * col, col)]
            w_rest.append(gather_planes(jnp.concatenate(blocks, axis=1)))
            blocks = [
                columns(ffn_in, layer, (n * j + m * high_c + (j + low_c) % m) * piece, piece)
                for j in range(m)
            ]
            down = lax.dynamic_slice(ffn_out, (layer, unit_start, 0), (1, piece, width))[0]
            w_ffn.append([gather_planes(jnp.concatenate(blocks, axis=1)), gather_planes(down)])
    vectors = ordered[:-layers].reshape(layers, -1, width)
    up_bias = ordered[-layers:].reshape(layers, m, held)[:, :, :piece].reshape(layers, units)
    w_sems = pltpu.SemaphoreType.DMA((2 * m,))
    w_scratch = [pltpu.VMEM((width, units), LOW), pltpu.VMEM((units, width), LOW), w_sems]
    qv_bias = lax.dynamic_slice(vectors, (0, 6, group * own), (layers, 2, own))
    ev_bias = lax.dynamic_slice(vectors, (0, 10, c * col), (layers, 1, col))
    ev_bias = jnp.pad(ev_bias, ((0, 0), (0, 0), (col, 0)))

    def own_slots(values):
        if split == 1:
            return values
        shaped = values.reshape((n // split, split, rows) + values.shape[1:])
        return shaped[:, 0].reshape((-1,) + values.shape[1:])

    def share(parts):
        if split == 1:
            return parts[0]
        total = lax.dynamic_index_in_dim(parts, part, 0, False).astype(F32)
        for other in range(1, split):
            term = lax.dynamic_index_in_dim(parts, part ^ other, 0, False)
            total = total + swap(term, other).astype(F32)
        return total

    def half_slots(width_of, kind=LOW):
        return [like((n // 2, rows, width_of), kind)] * 2

    (encoder_all,) = call(
        partial(assemble_kernel, n, rows),
        [here] + first_slots,
        [like((source_length, width), LOW)],
        0,
        smem=1,
    )

    def prepare(layer):
        return call(
            partial(cross_prepare_kernel, col, skip[layer]),
            [w_rest[layer], encoder_all, ev_bias[layer]],
            [like((2 * col, width + source_length), LOW)],
            4 * source_length * width * col,
        )[0]

    x = tokens[0]
    h1_slots = first_slots
    kept = []
    matmul = 2 * length * width
    for layer in range(layers):
        vec = vectors[layer]
        w_t = after(prepared if layer else prepare(0), h1_slots)
        near = gather_near(w_t)
        joined = layer > 0
        h1_all, q, k, v, a, self_lse, *parts = call(
            partial(self_forward_kernel, n, rows, split, layer == 0, joined, head_width),
            h1_slots
            + [vec, after(qv_bias[layer], w_t), w_qkv[layer]]
            + self_bounds
            + [w_out[layer]] * joined,
            [like((length, width), LOW), like((queries, own), LOW)]
            + [like((length, own), LOW)] * 2
            + [like((queries, own), LOW), like((queries, own // head_width), F32)]
            + half_slots(width) * joined,
            matmul * 4 * own + 4 * queries * length * own,
        )
        if not joined:
            parts = call(
                partial(self_out_kernel, n, rows, split),
                [a, w_out[layer]],
                half_slots(width),
                matmul * own,
            )
        even, odd = parts
        near, odd = lax.optimization_barrier((near, odd))
        terms = reduce_slots(even, odd)
        w_slots, where = gather_joined(w_t, near)
        x1, x2, h2, cq, mixed, cross_lse, h3, wq_t, wo_t, ek_t, ev_t = call(
            partial(mid_forward_kernel, n, len(terms), len(w_slots), where, head_width),
            [here, x] + terms + w_slots + [vec] + cross_bounds,
            [like((rows, width), F32)] * 2
            + [like((rows, width), LOW)] * 3
            + [like((rows, HEADS), F32), like((rows, width), LOW)]
            + [like((width, width), LOW)] * 2
            + [like((width, source_length), LOW)] * 2,
            4 * rows * width * (width + source_length),
            smem=1,
        )
        h3_all, g, slope, even, odd = call(
            partial(ffn_forward_kernel, n, len(w_ffn[layer])),
            gather_slots(h3) + [up_bias[layer][None]] + w_ffn[layer],
            [like((length, width), LOW)] + [like((length, units), LOW)] * 2 + half_slots(width),
            2 * matmul * units,
            scratch=w_scratch,
            far=len(w_ffn[layer]),
        )
        last = layer == layers - 1
        if last:
            result_parts = (even, odd)
        else:
            terms = reduce_slots(even, odd)
        kept.append(
            (x, x1, x2, h1_all, q, k, v, a, self_lse, h2, cq, mixed, cross_lse)
            + (h3_all, g, slope, wq_t, wo_t, ek_t, ev_t)
        )
        if last:
            continue
        prepared = prepare(layer + 1)
        outs = call(
            partial(between_kernel, len(terms), False),
            [x2] + terms + [vec, vectors[layer + 1]],
            [like((rows, width), F32), like((rows, width), LOW)],
            rows * width * 20,
        )
        x = outs[0]
        h1_slots = gather_slots(outs[1])

    r = width // (n * m)
    grad_x, e3_slots = grad_out[0], last_slots
    enc_total = jnp.zeros((source_length, width), F32)
    vec_sums = [None] * layers
    moves = [
        (i * m + p, ((n // m) * ((p - i % m) % m) + i // m) * m + p) for i in range(n) for p in range(m)
    ]

    def to_rows(summed):
        return lax.all_to_all(summed.reshape(n, r, summed.shape[1]), "ctx", 0, 0)

    def move_down(sums):
        down = sums[0][n * r :] if units == width else sums[1]
        return lax.ppermute(down, ("ctx", "fsdp"), moves)

    up_rows, down_rows = [None] * layers, [None] * layers
    finish = []
    for layer in reversed(range(layers)):
        x, x1, x2, h1_all, q, k, v, a, self_lse, h2, cq, mixed, cross_lse = kept[layer][:13]
        h3_all, g, slope, wq_t, wo_t, ek_t, ev_t = kept[layer][13:]
        vec = vectors[layer]
        if finish:
            slope = after(slope, cross_grad)
        e3_all, du, fc1_grad, even, odd = call(
            partial(ffn_backward_kernel, n, len(w_ffn[layer])),
            e3_slots + [slope] + w_ffn[layer],
            [like((length, width), LOW), like((length, units), LOW), like((1, units), F32)]
            + half_slots(width),
            2 * matmul * units,
            scratch=w_scratch,
            far=len(w_ffn[layer]),
        )
        terms = reduce_slots(even, odd)
        shapes = [like((m, n * r, units), LOW), like((m, piece + 16, width), LOW)]
        if units == width:
            shapes = [like((m, n * r + piece + 16, width), LOW)]
        ffn_grads = call(
            partial(ffn_weights_kernel, n, m),
            [here, h3_all, after(du, terms[0]), g, e3_all, fc1_grad],
            shapes,
            2 * matmul * units,
            smem=1,
        )
        x1 = after(x1, ffn_grads)
        dx1, e1, e2, dcq, even, odd, sums = call(
            partial(mid_backward_kernel, n, len(terms), head_width),
            [here, grad_x]
            + terms
            + [x1, x2, vec, wq_t, wo_t, ek_t, ev_t, cq, cross_lse]
            + cross_bounds,
            [like((rows, width), F32)]
            + [like((rows, width), LOW)] * 3
            + [like((n // 2, 2 * col, source_length), LOW)] * 2
            + [like((8, width), F32)],
            4 * rows * width * width + 10 * rows * source_length * width,
            scratch=[pltpu.VMEM((width, source_length), LOW)] * 2,
            smem=1,
        )
        ffn_sums = [reduce_planes(grad) for grad in after(ffn_grads, dx1)]
        e1_slots = gather_slots(e1)
        kv_parts = [even, odd]
        even, *odd = call(
            partial(cross_weights_kernel, n),
            [here, h2, dcq, mixed, e2] + kv_parts,
            [like((n // size, 2 * col, width + source_length), LOW) for size in (2, 4, 4)],
            4 * rows * width * width,
            scratch=[pltpu.VMEM((width, width), LOW)] * 2,
            smem=1,
            wait=[entry[2] for entry in finish[-1:]],
        )
        w_terms = reduce_slots(even, list(odd), hold=e1_slots)
        e1_own, dq, dkv, even, odd = call(
            partial(self_backward_kernel, n, split, head_width),
            e1_slots + [w_out[layer], w_qkv[layer], after(q, w_terms[0]), k, v, self_lse] + self_bounds,
            [like((queries, width), LOW), like((queries, own), LOW), like((length, 2 * own), LOW)]
            + half_slots(width),
            matmul * 4 * own + 10 * queries * length * own,
            scratch=[pltpu.VMEM((length, own), F32)] * 2,
        )
        if split > 1:
            shaped = dkv.reshape(n // split, split, rows, 2 * own)
            total = shaped[:, 0].astype(F32)
            for other in range(1, split):
                total = total + swap(shaped[:, other], other).astype(F32)
            dkv = total.astype(LOW).reshape(-1, 2 * own)
            even = dot_t(jnp.concatenate([dq, dkv], axis=1), w_qkv[layer][:, : 3 * own])
            even = even.reshape(n // 2, rows, width)
            odd = jnp.zeros_like(even)
        terms = reduce_slots(even, after(odd, w_terms))
        beside = []
        for done in finish if layer == 0 else ():
            up_rows[done[0]], down_rows[done[0]] = to_rows(done[1][0][: n * r]), move_down(done[1])
            beside += [up_rows[done[0]], down_rows[done[0]]]
        before = []
        if layer == 0:
            up_rows[0], down_rows[0] = to_rows(ffn_sums[0][: n * r]), move_down(ffn_sums)
            *ffn_grads, fc1_own = call(
                partial(place_ffn_kernel, n, m, layers),
                up_rows + down_rows,
                [like((layers, r, hidden), F32), like((layers, piece, width), F32), like((layers, piece), F32)],
                layers * r * hidden,
            )
            before = ffn_grads[:1]
        grad_x, e3, last_sums = call(
            partial(last_backward_kernel, len(terms)),
            [dx1] + terms + [x, vec],
            [like((rows, width), F32), like((rows, width), LOW), like((2, width), F32)],
            rows * width * 20,
            wait=before,
        )

        e3_slots = gather_slots(e3) if layer else None
        hold = (e3_slots[2], e3_slots[4]) if layer else terms[0]
        own_parts = [h1_all, dq, dkv, a, e1_own] if split == 1 else []
        cross_grad, enc_total, ev_sum, *enc_parts = call(
            partial(attention_weights_kernel, n, m, skip[layer], len(terms), split == 1),
            [here]
            + w_terms
            + own_parts
            + [encoder_all, w_rest[layer], after(enc_total, hold)],
            [like((m, n * r, (8 if split == 1 else 4) * col), LOW)]
            + [like((source_length, width), F32), like((2 * col, 1), F32)]
            + [like((n // 2, source_rows, width), F32)] * 2,
            8 * source_length * col * width + matmul * 4 * own,
            smem=1,
            wait=ffn_sums + beside,
        )
        if split > 1:
            qkv_grad = t_dot(own_slots(h1_all), jnp.concatenate([dq, dkv], axis=1)).astype(LOW)
            qkv_grad = share(qkv_grad.reshape(width, 3, split, col).transpose(2, 0, 1, 3))
            qkv_grad = qkv_grad.astype(LOW).reshape(n, m, r, 3 * col).transpose(1, 0, 2, 3)
            o_grad = share(t_dot(a, e1_own).astype(LOW).reshape(split, own // split, width))
            o_grad = o_grad.astype(LOW).reshape(m, r, n, col).transpose(0, 2, 1, 3)
            kv_q = jnp.split(cross_grad, [2 * col], axis=2)
            self_grad = jnp.concatenate([qkv_grad, o_grad], axis=3).reshape(m, n * r, 4 * col)
            parts = [kv_q[0], self_grad[:, :, : 3 * col], kv_q[1], self_grad[:, :, 3 * col :]]
            cross_grad = jnp.concatenate(parts, axis=2)
        both_sum = reduce_planes(cross_grad)
        finish.append((layer, ffn_sums, both_sum))
        zero = jnp.zeros((1, width), F32)
        summed = jnp.concatenate(
            [last_sums[0:1], sums[0:2], last_sums[1:2], sums[2:4], zero, zero]
            + [sums[4:6], zero, sums[6:8]]
        )
        owned_q = share(row_sum(dq).reshape(split, col))
        owned_v = share(row_sum(dkv[:, own:]).reshape(split, col))
        blank = jnp.zeros((col,), F32)
        owned = [blank] * 6 + [owned_q, owned_v, blank, blank, ev_sum[col:, 0], blank, blank]
        vec_sums[layer] = (summed, jnp.stack(owned))

    finish.sort(key=lambda entry: entry[0])
    result_terms = reduce_slots(*result_parts)
    (result,) = call(
        partial(between_kernel, len(result_terms), True),
        [kept[-1][2]] + result_terms + [vectors[-1]],
        [like((rows, width), LOW)],
        rows * width * 20,
    )
    enc_grad = total_of(reduce_slots(*after(enc_parts, grad_x), F32))
    summed = jnp.concatenate([pair[0] for pair in vec_sums])
    owned = jnp.concatenate([pair[1] for pair in vec_sums])
    summed = turn(summed, 1).reshape(-1, n, col).transpose(1, 0, 2)
    vec = total_of(reduce_slots(summed[0::2], summed[1::2], F32)) + owned
    (late,) = call(
        late_kernel,
        [entry[2] for entry in finish],
        [like((n * r, layers * 5 * col), LOW)],
        0,
        wait=[enc_grad],
    )
    late_rows = to_rows(late)
    attention_grads = call(
        partial(place_attention_kernel, n, layers),
        [late_rows] + [entry[2] for entry in finish],
        [like((layers, r, parts * width), F32) for parts in (3, 1, 1, 2, 1)],
        layers * r * 8 * width,
    )
    (vec,) = call(copy_kernel, [vec], [like(vec.shape, F32)], 0, wait=[late])
    vec = sum_planes(vec.reshape(-1, m, col // m).transpose(1, 0, 2))
    vec = vec.reshape(layers, -1, col // m)
    return (
        (result[None], grad_x[None], enc_grad[None])
        + tuple(attention_grads)
        + tuple(ffn_grads)
        + (vec[:, :3], vec[:, 3:], fc1_own)
    )


def solution(mesh):
    tokens = P("fsdp", "ctx", None)
    per_stream = P("fsdp", None)
    weight = P(None, "fsdp", None)
    vector = P(None, None, "fsdp")
    grad = P(None, ("ctx", "fsdp"), None)
    vector_grad = P(None, None, ("ctx", "fsdp"))
    return jax.shard_map(
        on_device,
        mesh=mesh,
        in_specs=(tokens,) * 3 + (per_stream,) * 3 + (weight,) * 7 + (vector,) * 2 + (P(None, "fsdp"),),
        out_specs=(tokens,) * 3 + (grad,) * 7 + (vector_grad,) * 2 + (P(None, ("ctx", "fsdp")),),
        check_vma=False,
    )
```

```python
from functools import partial

import jax
import jax.numpy as jnp
from jax import lax
from jax.experimental import pallas as pl
from jax.experimental.pallas import tpu as pltpu
from jax.sharding import PartitionSpec as P

HEADS = 16
EPSILON = 1e-05
NEGATIVE = -1e30
F32 = jnp.float32
LOW = jnp.bfloat16
VMEM = pl.BlockSpec(memory_space=pltpu.VMEM)
SMEM = pl.BlockSpec(memory_space=pltpu.SMEM)
FAR = pl.BlockSpec(memory_space=pl.ANY)
VMEM_BYTES = 60 * 2**20


def swap(values, bits):
    count = lax.axis_size("ctx")
    return lax.ppermute(values, "ctx", [(i, i ^ bits) for i in range(count)])


def gather_near(rows):
    if lax.axis_size("ctx") == 8:
        return swap(rows, 2), swap(rows, 4)
    return ()


def gather_slots(rows, near=None):
    count = lax.axis_size("ctx")
    if count == 8:
        near_x, near_y = near or gather_near(rows)
        half = rows.shape[0] // 2
        far = jnp.concatenate([swap(near_x[:half], 4), swap(near_y[half:], 2)])
        blocks = []
        for block in (rows, near_x, near_y, far):
            blocks += [block, swap(block, 1)]
        return blocks
    blocks = [rows]
    bit = 1
    while bit < count:
        blocks = blocks + [swap(block, bit) for block in blocks]
        bit *= 2
    return blocks


def gather_joined(rows, near):
    count = lax.axis_size("ctx")
    size = rows.shape[0]
    if count == 8:
        half = size // 2
        joined = swap(jnp.concatenate([rows, *near]), 1)
        far = jnp.concatenate([swap(near[0][:half], 4), swap(near[1][half:], 2)])
        arrays = [rows, *near, far, joined, swap(far, 1)]
        where = [(0, 0), (4, 0), (1, 0), (4, size), (2, 0), (4, 2 * size), (3, 0), (5, 0)]
        return arrays, where
    return gather_slots(rows), [(k, 0) for k in range(count)]


def reduce_slots(even, odd, kind=LOW, hold=None):
    count = lax.axis_size("ctx")
    odd = [swap(block.astype(kind), 1) for block in (odd if isinstance(odd, list) else [odd])]
    if count == 8:
        size = odd[0].shape[0]
        chip = [even[i].astype(F32) + odd[i // size][i % size].astype(F32) for i in range(4)]
        sent = [chip[i].astype(kind) for i in (1, 2, 3)]
        if hold is not None:
            sent = after(sent, hold)
        return [chip[0]] + [swap(sent[i], 2 * i + 2) for i in range(3)]
    chip = even.astype(F32) + jnp.concatenate(odd).astype(F32)
    bit = count // 4
    while bit:
        chip = chip[:bit] + swap(chip[bit : 2 * bit].astype(kind), 2 * bit).astype(F32)
        bit //= 2
    return [chip[0]]


def total_of(terms):
    total = terms[0].astype(F32)
    for term in terms[1:]:
        total = total + term.astype(F32)
    return total


def turn(values, axis):
    count = lax.axis_size("ctx")
    here = lax.axis_index("ctx")
    width = values.shape[axis] // count
    return jnp.concatenate(
        [
            lax.dynamic_slice_in_dim(values, (here ^ k) * width, width, axis)
            for k in range(count)
        ],
        axis=axis,
    )


def sum_planes(parts):
    count = lax.axis_size("fsdp")
    here = lax.axis_index("fsdp")
    total = lax.dynamic_index_in_dim(parts, here, 0, False)
    for step in range(1, count):
        term = lax.dynamic_index_in_dim(parts, (here + step) % count, 0, False)
        total = total + lax.ppermute(term, "fsdp", [(i, (i + step) % count) for i in range(count)])
    return total


def after(values, other):
    return lax.optimization_barrier((values, other))[0]


def gather_planes(values):
    return lax.all_gather(values, "fsdp", axis=0, tiled=True)


def reduce_planes(parts):
    return lax.psum_scatter(parts, "fsdp", scatter_dimension=0, tiled=False)


def layer_norm(values, gain_row, offset_row):
    center = values - jnp.mean(values, axis=-1, keepdims=True)
    spread = jnp.mean(center * center, axis=-1, keepdims=True)
    return center * lax.rsqrt(spread + EPSILON) * gain_row + offset_row


def layer_norm_back(values, gain_row, grad):
    center = values - jnp.mean(values, axis=-1, keepdims=True)
    inverse = lax.rsqrt(jnp.mean(center * center, axis=-1, keepdims=True) + EPSILON)
    normed = center * inverse
    scaled = grad * gain_row
    back = inverse * (
        scaled
        - jnp.mean(scaled, axis=-1, keepdims=True)
        - normed * jnp.mean(scaled * normed, axis=-1, keepdims=True)
    )
    return back, row_sum(grad * normed), row_sum(grad)


def row_sum(values):
    return jnp.sum(values.astype(F32), axis=0, keepdims=True)


def dot(left, right):
    return jnp.dot(left, right, preferred_element_type=F32)


def dot_t(left, right):
    return lax.dot_general(left, right, (((1,), (1,)), ((), ())), preferred_element_type=F32)


def t_dot(left, right):
    return lax.dot_general(left, right, (((0,), (0,)), ((), ())), preferred_element_type=F32)


def call(kernel, ins, outs, flops, scratch=(), smem=0, far=0, wait=(), steps=0, tiles=None):
    count, extra = len(ins), len(wait)

    def spec(index, array):
        if not steps and not (tiles and index in tiles):
            return VMEM
        block, axis = (tiles or {}).get(index, (array.shape, None))
        dims = len(block)
        if not steps:
            return pl.BlockSpec(block, lambda: (0,) * dims)
        return pl.BlockSpec(block, lambda i: tuple(i if d == axis else 0 for d in range(dims)))

    def body(*refs):
        kernel(*refs[:count], *refs[count + extra :])

    moved = sum(a.size * a.dtype.itemsize for a in ins)
    moved += sum(a.size * a.dtype.itemsize for a in outs)
    return pl.pallas_call(
        body,
        grid=(steps,) if steps else (),
        in_specs=[SMEM] * smem
        + [spec(i, ins[i]) for i in range(smem, count - far)]
        + [FAR] * (far + extra),
        out_specs=[spec(count + i, array) for i, array in enumerate(outs)],
        out_shape=outs,
        scratch_shapes=list(scratch),
        compiler_params=pltpu.CompilerParams(vmem_limit_bytes=VMEM_BYTES),
        cost_estimate=pl.CostEstimate(flops=int(flops), bytes_accessed=int(moved), transcendentals=0),
    )(*ins, *wait)


def like(shape, kind):
    return jax.ShapeDtypeStruct(tuple(shape), kind)


def tile_rows(rows, size):
    return pl.ds(pl.multiple_of(rows * size, size), size)


def join_rows(blocks, out_ref):
    rows = blocks[0].shape[0]
    for k, block in enumerate(blocks):
        out_ref[k * rows : (k + 1) * rows] = block[...]


def put_slots(even_ref, odd_ref, index, values):
    rows = even_ref.shape[1]
    for i in range(values.shape[0] // (2 * rows)):
        even_ref[index + i] = values[2 * i * rows : (2 * i + 1) * rows].astype(LOW)
        odd_ref[index + i] = values[(2 * i + 1) * rows : (2 * i + 2) * rows].astype(LOW)


def pairs_at_once(n, rows, split):
    return 2 if split == 1 and n % 4 == 0 and n * rows <= 1024 else 1


def self_forward_kernel(n, rows, split, raw, joined, head_width, *refs):
    blocks, refs = refs[:n], refs[n:]
    vec_ref, bias_ref, w_ref, low_ref, high_ref, place_ref = refs[:6]
    (wo_ref, *refs) = refs[6:] if joined else (None, *refs[6:])
    h_ref, q_ref, k_ref, v_ref, a_ref, lse_ref, *out_refs = refs
    own = k_ref.shape[1]
    for k in range(n):
        block = blocks[k][:rows]
        if raw:
            block = layer_norm(block.astype(F32), vec_ref[0:1], vec_ref[3:4]).astype(LOW)
        h_ref[k * rows : (k + 1) * rows] = block

    @pl.loop(0, n // 2)
    def _(i):
        at = tile_rows(i, 2 * rows)
        z = dot(h_ref[at], w_ref[:, : 3 * own])
        q = ((z[:, :own] + bias_ref[0:1]) * 0.125).astype(LOW)
        if split == 1:
            q_ref[at] = q
        else:
            q_ref[tile_rows(i, rows)] = q[:rows]
        k_ref[at] = z[:, own : 2 * own].astype(LOW)
        v_ref[at] = (z[:, 2 * own :] + bias_ref[1:2]).astype(LOW)

    wide = pairs_at_once(n, rows, split)
    step = 2 * rows * wide // split

    @pl.loop(0, n // 2 // wide)
    def _(i):
        at = tile_rows(i, step)
        mask = (place_ref[...] >= low_ref[at]) & (place_ref[...] <= high_ref[at])
        outs, masses = [], []
        for start in range(0, own, head_width):
            span = slice(start, start + head_width)
            scores = jnp.where(mask, dot_t(q_ref[at, span], k_ref[:, span]), NEGATIVE)
            top = jnp.max(scores, axis=1, keepdims=True)
            raised = jnp.exp(scores - top)
            mass = jnp.sum(raised, axis=1, keepdims=True)
            outs.append(dot((raised * (1.0 / mass)).astype(LOW), v_ref[:, span]))
            masses.append(top + jnp.log(mass))
        a = jnp.concatenate(outs, axis=1).astype(LOW)
        a_ref[at] = a
        lse_ref[at] = jnp.concatenate(masses, axis=1)
        if joined:
            put_product(split, a, wo_ref, *out_refs, i * wide)


def put_product(split, a, wo_ref, even_ref, odd_ref, i):
    y = dot(a, wo_ref[...])
    if split > 1:
        y = jnp.concatenate([y, jnp.zeros_like(y)])
    put_slots(even_ref, odd_ref, i, y)


def self_out_kernel(n, rows, split, a_ref, wo_ref, even_ref, odd_ref):
    wide = pairs_at_once(n, rows, split)
    step = 2 * rows * wide // split

    @pl.loop(0, n // 2 // wide)
    def _(i):
        put_product(split, a_ref[tile_rows(i, step)], wo_ref, even_ref, odd_ref, i * wide)


def mid_forward_kernel(n, terms, arrays, where, head_width, here_ref, *refs):
    x_ref, refs = refs[0], refs[1:]
    term_refs, refs = refs[:terms], refs[terms:]
    w_refs, refs = refs[:arrays], refs[arrays:]
    vec_ref, low_ref, high_ref, place_ref = refs[:4]
    x1_ref, x2_ref, h2_ref, cq_ref, c_ref, lse_ref, h3_ref = refs[4:11]
    wq_ref, wo_ref, ek_ref, ev_ref = refs[11:]
    col = w_refs[0].shape[0] // 2
    width = wq_ref.shape[1]
    here = here_ref[0]
    for k in range(n):
        at = tile_rows(here ^ k, col)
        array, first = where[k]
        top, bottom = pl.ds(first, col), pl.ds(first + col, col)
        wq_ref[at] = w_refs[array][top, :width]
        wo_ref[at] = w_refs[array][bottom, :width]
        ek_ref[at] = w_refs[array][top, width:]
        ev_ref[at] = w_refs[array][bottom, width:]
    x1 = x_ref[...].astype(F32) + total_of([t[...] for t in term_refs]) + vec_ref[8:9]
    x1_ref[...] = x1
    h2 = layer_norm(x1, vec_ref[1:2], vec_ref[4:5]).astype(LOW)
    h2_ref[...] = h2
    cq_ref[...] = ((dot_t(h2, wq_ref[...]) + vec_ref[9:10]) * 0.125).astype(LOW)
    mask = (place_ref[...] >= low_ref[...]) & (place_ref[...] <= high_ref[...])
    outs, masses = [], []
    for start in range(0, cq_ref.shape[1], head_width):
        span = slice(start, start + head_width)
        scores = jnp.where(mask, dot(cq_ref[:, span], ek_ref[span]), NEGATIVE)
        top = jnp.max(scores, axis=1, keepdims=True)
        raised = jnp.exp(scores - top)
        mass = jnp.sum(raised, axis=1, keepdims=True)
        outs.append(dot_t((raised * (1.0 / mass)).astype(LOW), ev_ref[span]))
        masses.append(top + jnp.log(mass))
    c_ref[...] = jnp.concatenate(outs, axis=1).astype(LOW)
    lse_ref[...] = jnp.concatenate(masses, axis=1)
    x2 = x1 + dot_t(c_ref[...], wo_ref[...]) + vec_ref[11:12]
    x2_ref[...] = x2
    h3_ref[...] = layer_norm(x2, vec_ref[2:3], vec_ref[5:6]).astype(LOW)


def copies_of(sources, up_ref, down_ref, sems):
    if len(sources) == 2:
        pairs = [(sources[0], up_ref), (sources[1], down_ref)]
    else:
        planes, both = sources[0].shape[:2]
        size = up_ref.shape[0] // planes
        pairs = []
        for j in range(planes):
            at = pl.ds(j * size, size)
            pairs.append((sources[0].at[j, pl.ds(0, size)], up_ref.at[at]))
            pairs.append((sources[0].at[j, pl.ds(size, size)], down_ref.at[at]))
    return [pltpu.make_async_copy(a, b, sems.at[i]) for i, (a, b) in enumerate(pairs)]


def ffn_forward_kernel(n, sources, *refs):
    blocks, refs = refs[:n], refs[n:]
    bias_ref, refs = refs[0], refs[1:]
    sources, refs = refs[:sources], refs[sources:]
    g_ref, slope_ref, even_ref, odd_ref, h_ref, up_ref, down_ref, sems = refs
    step = pl.program_id(0)

    @pl.when(step == 0)
    def _():
        copies = copies_of(sources, up_ref, down_ref, sems)
        for copy in copies:
            copy.start()
        join_rows(blocks, h_ref)
        for copy in copies:
            copy.wait()

    u = dot(h_ref[tile_rows(step, g_ref.shape[0])], up_ref[...]) + bias_ref[...]
    share = 0.5 + 0.5 * lax.erf(u * 0.7071067811865476)
    g = (u * share).astype(LOW)
    g_ref[...] = g
    slope_ref[...] = (share + u * (jnp.exp(-0.5 * u * u) * 0.3989422804014327)).astype(LOW)
    put_slots(even_ref, odd_ref, 0, dot(g, down_ref[...]))


def ffn_backward_kernel(n, sources, *refs):
    blocks, refs = refs[:n], refs[n:]
    slope_ref, refs = refs[0], refs[1:]
    sources, refs = refs[:sources], refs[sources:]
    du_ref, sum_ref, even_ref, odd_ref, e_ref, up_ref, down_ref, sems = refs
    step = pl.program_id(0)

    @pl.when(step == 0)
    def _():
        copies = copies_of(sources, up_ref, down_ref, sems)
        for copy in copies:
            copy.start()
        join_rows(blocks, e_ref)
        sum_ref[...] = jnp.zeros_like(sum_ref)
        for copy in copies:
            copy.wait()

    grad = dot_t(e_ref[tile_rows(step, du_ref.shape[0])], down_ref[...])
    du = (grad * slope_ref[...].astype(F32)).astype(LOW)
    du_ref[...] = du
    sum_ref[...] += row_sum(du)
    put_slots(even_ref, odd_ref, 0, dot_t(du, up_ref[...]))


def pack_kernel(m, n, jobs, where_ref, *refs):
    count = sum(len(FED[kind]) for kind, layer in jobs)
    sources, packed, sems = refs[:count], refs[count:-1], refs[-1]
    c, f = where_ref[0], where_ref[1]
    high, low = c // m, c % m
    copies = []

    def add(source, target):
        copies.append(pltpu.make_async_copy(source, target, sems.at[len(copies)]))

    def columns(start, size):
        return pl.ds(pl.multiple_of(start, 128), size)

    for (kind, layer), target in zip(jobs, packed):
        fed, sources = sources[: len(FED[kind])], sources[len(FED[kind]) :]
        at = 0
        if kind == "ffn":
            up, down = fed
            rows, piece = up.shape[1], down.shape[1] // n
            for j in range(m):
                start = (n * j + m * high + (j + low) % m) * piece
                add(up.at[layer, :, columns(start, piece)], target.at[pl.ds(0, rows), pl.ds(j * piece, piece)])
            start = (m * high + (f + low) % m) * piece
            add(down.at[layer, pl.ds(pl.multiple_of(start, piece), piece)], target.at[pl.ds(rows, piece)])
            continue
        for source, (name, parts) in zip(fed, FED[kind].items()):
            if parts == 0:
                add(source, target.at[:, pl.ds(at, source.shape[1])])
                continue
            width = source.shape[2] // parts
            col = width // n
            if name == "self_out":
                for l in range(source.shape[0]):
                    add(source.at[l, :, columns(c * col, col)], target.at[:, pl.ds(at, col)])
                    at += col
                continue
            for i in range(parts):
                add(source.at[layer, :, columns(i * width + c * col, col)], target.at[:, pl.ds(at, col)])
                at += col
    for copy in copies:
        copy.start()
    for copy in copies:
        copy.wait()


FED = {
    "first": {"qkv": 3, "kv": 2, "q": 1, "out": 1, "self_out": 1, "vec": 0},
    "attention": {"qkv": 3, "kv": 2, "q": 1, "out": 1},
    "ffn": {"up": 1, "down": 1},
}


def late_kernel(*refs):
    out_ref = refs[-1]
    size = out_ref.shape[1] // (len(refs) - 1)
    for layer, ref in enumerate(refs[:-1]):
        out_ref[:, layer * size : (layer + 1) * size] = ref[:, :size]


def copy_kernel(*refs):
    count = len(refs) // 2
    for in_ref, out_ref in zip(refs[:count], refs[count:]):
        out_ref[...] = in_ref[...]


def assemble_kernel(n, skip, here_ref, *refs):
    out_ref = refs[n]
    size = refs[0].shape[0] - skip
    for k in range(n):
        out_ref[tile_rows(here_ref[0] ^ k, size)] = refs[k][skip:]


def cross_prepare_kernel(col, skip, w_ref, enc_ref, bias_ref, out_ref):
    kv = dot(enc_ref[...], w_ref[:, skip : skip + 2 * col]) + bias_ref[...]
    width = w_ref.shape[0]
    out_ref[:, width:] = kv.T.astype(LOW)
    out_ref[:, :width] = w_ref[:, skip + 2 * col : skip + 4 * col].astype(F32).T.astype(LOW)


def between_kernel(terms, last, *refs):
    x2_ref, refs = refs[0], refs[1:]
    term_refs, refs = refs[:terms], refs[terms:]
    y = x2_ref[...] + total_of([t[...] for t in term_refs]) + refs[0][12:13]
    if last:
        refs[1][...] = y.astype(LOW)
    else:
        next_ref, y_ref, h_ref = refs[1:]
        y_ref[...] = y
        h_ref[...] = layer_norm(y, next_ref[0:1], next_ref[3:4]).astype(LOW)


def put_folded(out_ref, grad, at, n, m):
    size, width = grad.shape[0] // m, grad.shape[1] // n
    for p in range(m):
        for i in range(n):
            block = grad[p * size : (p + 1) * size, i * width : (i + 1) * width]
            out_ref[p, i * size : (i + 1) * size, at : at + width] = block


def attention_weights_kernel(n, m, skip, terms, full, here_ref, *refs):
    w_refs, refs = refs[:terms], refs[terms:]
    own_refs, refs = (refs[:5], refs[5:]) if full else ((), refs)
    enc_ref, w_kv_ref, before_ref, out_ref, total_ref, sum_ref, even_ref, odd_ref = refs
    col = w_refs[0].shape[0] // 2
    width = w_kv_ref.shape[0]
    grad = total_of([t[:, :width] for t in w_refs]).astype(LOW)
    for i in range(2):
        at = (5 + i if full else 2 + i) * col
        put_folded(out_ref, grad[i * col : (i + 1) * col], at, n, m)
    dkv_t = total_of([t[:, width:] for t in w_refs])
    sum_ref[...] = jnp.sum(dkv_t.astype(LOW).astype(F32), axis=1, keepdims=True)
    dkv = dkv_t.T.astype(LOW)
    total_ref[...] = before_ref[...] + dot_t(dkv, w_kv_ref[:, skip : skip + 2 * col])
    put_by_rows(out_ref, t_dot(enc_ref[...], dkv).astype(LOW), 0, width, n, m)
    for k in range(n):
        part = total_ref[tile_rows(here_ref[0] ^ k, even_ref.shape[1])]
        (odd_ref if k % 2 else even_ref)[k // 2] = part
    if not full:
        return
    h_ref, dq_ref, dkv_ref, a_ref, e_ref = own_refs
    own = dq_ref.shape[1]
    step = min(256, width)
    for first in range(0, width, step):
        part = h_ref[:, first : first + step]
        grad = jnp.concatenate([t_dot(part, dq_ref[...]), t_dot(part, dkv_ref[...])], axis=1)
        put_by_rows(out_ref, grad.astype(LOW), first, width, n, m, 2 * own)
    put_folded(out_ref, t_dot(a_ref[...], e_ref[...]).astype(LOW), 7 * own, n, m)


def put_by_rows(out_ref, grad, first, total, n, m, at=0):
    size = total // (n * m)
    for i in range(grad.shape[0] // size):
        block = first // size + i
        device, plane = block // m, block % m
        part = grad[i * size : (i + 1) * size]
        out_ref[plane, device * size : (device + 1) * size, at : at + grad.shape[1]] = part


def ffn_weights_kernel(n, m, here_ref, du_ref, g_ref, sum_ref, *refs):
    h_blocks, e_blocks, outs = refs[:n], refs[n : 2 * n], refs[2 * n : -2]
    h_ref, e_ref = refs[-2:]
    up_ref, down_ref = outs if len(outs) == 2 else (outs[0], None)
    join_rows(h_blocks, h_ref)
    join_rows(e_blocks, e_ref)
    piece = g_ref.shape[1] // m
    low = here_ref[0] % m
    first = h_ref.shape[1] // m if down_ref is None else 0
    down_ref = up_ref if down_ref is None else down_ref
    for j in range(m):
        plane = (low + j) % m
        grad = t_dot(g_ref[:, j * piece : (j + 1) * piece], e_ref[...]).astype(LOW)
        down_ref[plane, first : first + piece] = grad
        part = sum_ref[:, j * piece : (j + 1) * piece].astype(LOW)
        down_ref[plane, first + piece :] = jnp.zeros((16, down_ref.shape[2]), LOW)
        down_ref[plane, first + piece : first + piece + 1, :piece] = part
    step = min(256, h_ref.shape[1])
    for first in range(0, h_ref.shape[1], step):
        grad = t_dot(h_ref[:, first : first + step], du_ref[...]).astype(LOW)
        put_by_rows(up_ref, grad, first, h_ref.shape[1], n, m)


def mid_backward_kernel(n, terms, head_width, here_ref, *refs):
    dy_ref, refs = refs[0], refs[1:]
    term_refs, refs = refs[:terms], refs[terms:]
    x1_ref, x2_ref, vec_ref, wq_ref, wo_ref, ek_ref, ev_ref, cq_ref, lse_ref = refs[:9]
    low_ref, high_ref, place_ref = refs[9:12]
    dx1_ref, e1_ref, e2_ref, dcq_ref, even_ref, odd_ref, sum_ref = refs[12:19]
    dek_ref, dev_ref = refs[19:]
    col = even_ref.shape[1] // 2
    dy = dy_ref[...].astype(F32)
    back, gain_two, shift_two = layer_norm_back(
        x2_ref[...], vec_ref[2:3], total_of([t[...] for t in term_refs])
    )
    dx2 = dy + back
    e2 = dx2.astype(LOW)
    e2_ref[...] = e2
    d_all = dot(e2, wo_ref[...]).astype(LOW)
    mask = (place_ref[...] >= low_ref[...]) & (place_ref[...] <= high_ref[...])
    dqs = []
    for index, start in enumerate(range(0, cq_ref.shape[1], head_width)):
        span = slice(start, start + head_width)
        q, d, ek, ev = cq_ref[:, span], d_all[:, span], ek_ref[span], ev_ref[span]
        weights = jnp.where(mask, jnp.exp(dot(q, ek) - lse_ref[:, index : index + 1]), 0.0)
        weight_grad = dot(d, ev)
        delta = jnp.sum(weights * weight_grad, axis=1, keepdims=True)
        score_grad = (weights * (weight_grad - delta)).astype(LOW)
        dqs.append(dot_t(score_grad, ek))
        dek_ref[span] = t_dot(q, score_grad).astype(LOW)
        dev_ref[span] = t_dot(d, weights.astype(LOW)).astype(LOW)
    dcq = (jnp.concatenate(dqs, axis=1).astype(LOW).astype(F32) * 0.125).astype(LOW)
    dcq_ref[...] = dcq
    here = here_ref[0]
    for k in range(n):
        at = tile_rows(here ^ k, col)
        out = odd_ref if k % 2 else even_ref
        out[k // 2, :col] = dek_ref[at]
        out[k // 2, col:] = dev_ref[at]
    back, gain_one, shift_one = layer_norm_back(x1_ref[...], vec_ref[1:2], dot(dcq, wq_ref[...]))
    dx1 = dx2 + back
    dx1_ref[...] = dx1
    e1 = dx1.astype(LOW)
    e1_ref[...] = e1
    sums = [gain_one, gain_two, shift_one, shift_two]
    sums += [row_sum(e1), row_sum(dcq), row_sum(e2), row_sum(dy)]
    sum_ref[...] = jnp.concatenate(sums, axis=0)


def cross_weights_kernel(n, here_ref, h_ref, dcq_ref, c_ref, e_ref, kv_even, kv_odd, even_ref, *refs):
    odd_refs, (q_ref, o_ref) = refs[:2], refs[2:]
    col = even_ref.shape[1] // 2
    width = q_ref.shape[1]
    q_ref[...] = t_dot(h_ref[...], dcq_ref[...]).astype(LOW)
    o_ref[...] = t_dot(c_ref[...], e_ref[...]).astype(LOW)
    here = here_ref[0]
    for k in range(n):
        at = tile_rows(here ^ k, col)
        out, i = (odd_refs[2 * k // n], k // 2 % (n // 4)) if k % 2 else (even_ref, k // 2)
        out[i, :col, :width] = q_ref[at]
        out[i, col:, :width] = o_ref[at]
    even_ref[:, :, width:] = kv_even[...]
    for i in range(2):
        odd_refs[i][:, :, width:] = kv_odd[i * n // 4 : (i + 1) * n // 4]


def self_backward_kernel(n, split, head_width, *refs):
    blocks, refs = refs[:n], refs[n:]
    wo_ref, w_ref, q_ref, k_ref, v_ref, lse_ref, low_ref, high_ref, place_ref = refs[:9]
    e_ref, dq_ref, dkv_ref, even_ref, odd_ref, dk_ref, dv_ref = refs[9:]
    rows = blocks[0].shape[0]
    own = wo_ref.shape[0]
    for i, k in enumerate(range(0, n, split)):
        e_ref[i * rows : (i + 1) * rows] = blocks[k][...]
    dk_ref[...] = jnp.zeros_like(dk_ref)
    dv_ref[...] = jnp.zeros_like(dv_ref)
    wide = pairs_at_once(n, rows, split)
    step = 2 * rows * wide // split

    @pl.loop(0, n // 2 // wide)
    def _(i):
        at = tile_rows(i, step)
        mask = (place_ref[...] >= low_ref[at]) & (place_ref[...] <= high_ref[at])
        d_all = dot_t(e_ref[at], wo_ref[...]).astype(LOW)
        dqs, dks, dvs = [], [], []
        for index, start in enumerate(range(0, own, head_width)):
            span = slice(start, start + head_width)
            q, k, v, d = q_ref[at, span], k_ref[:, span], v_ref[:, span], d_all[:, span]
            weights = jnp.where(mask, jnp.exp(dot_t(q, k) - lse_ref[at, index : index + 1]), 0.0)
            weight_grad = dot_t(d, v)
            delta = jnp.sum(weights * weight_grad, axis=1, keepdims=True)
            score_grad = (weights * (weight_grad - delta)).astype(LOW)
            dqs.append(dot(score_grad, k))
            dks.append(t_dot(score_grad, q))
            dvs.append(t_dot(weights.astype(LOW), d))
        dq = jnp.concatenate(dqs, axis=1).astype(LOW).astype(F32) * 0.125
        dq_ref[at] = dq.astype(LOW)
        dk_ref[...] += jnp.concatenate(dks, axis=1)
        dv_ref[...] += jnp.concatenate(dvs, axis=1)

    dkv_ref[:, :own] = dk_ref[...].astype(LOW)
    dkv_ref[:, own:] = dv_ref[...].astype(LOW)
    if split > 1:
        return

    @pl.loop(0, n // 2 // wide)
    def _(i):
        at = tile_rows(i, step)
        put_slots(
            even_ref, odd_ref, i * wide, dot_t(dq_ref[at], w_ref[:, :own]) + dot_t(dkv_ref[at], w_ref[:, own : 3 * own])
        )


def place_ffn_kernel(n, m, layers, *refs):
    up_ref, down_ref, up_out, down_out, fc1_out = refs
    piece = fc1_out.shape[1]
    for layer in range(layers):
        down_out[layer] = down_ref[layer, :piece].astype(F32)
        fc1_out[layer : layer + 1] = down_ref[layer, piece : piece + 16, :piece].astype(F32)[:1]
        for device in range(n):
            high, low = device // m, device % m
            for j in range(m):
                at = (n * j + m * high + (j + low) % m) * piece
                start = (layer * m + j) * piece
                block = up_ref[device, :, start : start + piece]
                up_out[layer, :, at : at + piece] = block.astype(F32)


def place_attention_kernel(n, layers, *refs):
    late, both, outs = refs[0], refs[1 : layers + 1], refs[layers + 1 :]
    qkv_out, o_out, q_out, kv_out, cross_out = outs
    col = both[0].shape[1] // 8
    rows = both[0].shape[0] // n
    for layer in range(layers):
        for i in range(n):
            for part in range(5):
                out, at = (kv_out, part) if part < 2 else (qkv_out, part - 2)
                start = (5 * layer + part) * col
                block = late[i, :, start : start + col]
                out[layer, :, (at * n + i) * col : (at * n + i + 1) * col] = block.astype(F32)
            for out, part in ((q_out, 5), (cross_out, 6), (o_out, 7)):
                block = both[layer][i * rows : (i + 1) * rows, part * col : (part + 1) * col]
                out[layer, :, i * col : (i + 1) * col] = block.astype(F32)


def last_backward_kernel(terms, *refs):
    dx1_ref, refs = refs[0], refs[1:]
    term_refs, refs = refs[:terms], refs[terms:]
    x_ref, vec_ref, dx_ref, e_ref, sum_ref = refs
    back, gain, shift = layer_norm_back(
        x_ref[...].astype(F32), vec_ref[0:1], total_of([t[...] for t in term_refs])
    )
    dx = dx1_ref[...] + back
    dx_ref[...] = dx
    e_ref[...] = dx.astype(LOW)
    sum_ref[...] = jnp.concatenate([gain, shift], axis=0)


def stored_positions(row_index, row_count, dev_count):
    device = row_index // row_count
    offset = row_index % row_count
    half_rows = row_count // 2
    return jnp.where(
        offset < half_rows,
        device * half_rows + offset,
        (2 * dev_count - 1 - device) * half_rows + offset - half_rows,
    )


def ranges_of(starts, length):
    return starts, jnp.concatenate([starts[1:], jnp.full((1,), length, jnp.int32)]) - 1


def group_of(places, starts):
    return jnp.sum((starts[None, :] <= places[:, None]).astype(jnp.int32), axis=1) - 1


def pick(table, index):
    slots = jnp.arange(table.shape[0], dtype=jnp.int32)
    return jnp.sum(jnp.where(index[:, None] == slots[None, :], table[None, :], 0), axis=1)


def on_device(
    tokens,
    encoder_states,
    grad_out,
    doc_starts,
    source_doc,
    source_offsets,
    self_qkv,
    self_out,
    cross_q,
    cross_kv,
    cross_out,
    ffn_in,
    ffn_out,
    norm_gains,
    vec_biases,
    fc1_bias,
):
    n, m = lax.axis_size("ctx"), lax.axis_size("fsdp")
    c, f = lax.axis_index("ctx"), lax.axis_index("fsdp")
    layers = self_qkv.shape[0]
    rows, width = tokens.shape[1:]
    source_rows = encoder_states.shape[1]
    length, source_length = n * rows, n * source_rows
    held = self_out.shape[1]
    hidden = ffn_out.shape[1] * m
    head_width = width // HEADS
    groups = min(n, HEADS)
    split = n // groups
    group, part = c // split, c % split
    own = width // groups
    col = width // n
    piece = hidden // (n * m)
    units = m * piece
    high_c, low_c = c // m, c % m
    here = jnp.stack([c, f]).astype(jnp.int32)
    queries = length // split
    packs = split == 1 and col % 128 == 0 and units == width and piece == held

    slot_rows = ((c ^ jnp.arange(n, dtype=jnp.int32)) * rows)[:, None] + jnp.arange(
        rows, dtype=jnp.int32
    )[None, :]
    places = stored_positions(slot_rows.reshape(-1), rows, n)
    own_places = places.reshape(n // split, split, rows)[:, 0].reshape(-1)
    doc_low, doc_high = ranges_of(doc_starts[0], length)
    self_bounds = [
        pick(doc_low, group_of(own_places, doc_starts[0]))[:, None],
        own_places[:, None],
        places[None, :],
    ]
    source_low, source_high = ranges_of(source_offsets[0], source_length)
    read_doc = pick(source_doc[0], group_of(places[:rows], doc_starts[0]))
    cross_bounds = [
        pick(source_low, read_doc)[:, None],
        pick(source_high, read_doc)[:, None],
        jnp.arange(source_length, dtype=jnp.int32)[None, :],
    ]

    def fetch_out():
        start = group * own
        got = lax.dynamic_slice(self_out, (0, start % held, 0), (layers, own, width))
        got = jnp.where(f == start // held, got, jnp.zeros_like(got))
        covered = [{(device // split) * own // held} for device in range(n)]
        while any(len(planes) < m for planes in covered):
            pairs = []
            for device, planes in enumerate(covered):
                reached = set()
                for plane in sorted(planes):
                    free = [p for p in (plane + 1, plane - 1) if 0 <= p < m and p not in planes | reached]
                    if free:
                        reached.add(free[0])
                        pairs.append((device * m + plane, device * m + free[0]))
                planes |= reached
            got = got + lax.ppermute(got, ("ctx", "fsdp"), pairs)
        return got

    def columns(array, layer, start, count):
        return lax.dynamic_slice(array, (layer, 0, start), (1, array.shape[1], count))[0]

    first_rows = jnp.concatenate([tokens[0], encoder_states[0]])
    first_slots = gather_slots(first_rows)
    unit_start = (m * high_c + (f + low_c) % m) * piece
    last_slots = gather_slots(after(grad_out[0], first_slots))
    vec_rows = jnp.concatenate([norm_gains, vec_biases], axis=1)
    fc1_rows = lax.dynamic_slice(fc1_bias, (0, unit_start), (layers, piece))
    fc1_rows = jnp.pad(fc1_rows, ((0, 0), (0, held - piece)))
    vec_rows = jnp.concatenate([vec_rows.reshape(-1, held), fc1_rows])
    if packs:
        arrays = dict(qkv=self_qkv, kv=cross_kv, q=cross_q, out=cross_out, up=ffn_in, down=ffn_out)
        arrays["self_out"] = self_out
        arrays["vec"] = jnp.pad(vec_rows.T, ((0, 0), (0, 128 - vec_rows.shape[0])))
        first_size = (7 + layers) * col
        sizes = {
            "first": (held, first_size + 128),
            "attention": (held, 7 * col),
            "ffn": (held + piece, units),
        }

        def pack(jobs, wait=()):
            fed = [arrays[name] for kind, layer in jobs for name in FED[kind]]
            return call(
                partial(pack_kernel, m, n, jobs),
                [here] + fed,
                [like(sizes[kind], LOW) for kind, layer in jobs],
                0,
                scratch=[pltpu.SemaphoreType.DMA((8 * len(jobs) + 8,))],
                smem=1,
                far=len(fed),
                wait=wait,
            )

        packed = pack([("first", 0)])
        packed += pack([("ffn", 0)], [first_slots[-1], last_slots[-1]])
        for layer in range(1, layers):
            packed += pack([("attention", layer), ("ffn", layer)])
        got = []
        for index, operand in enumerate(packed):
            if index > 1:
                operand = after(operand, got[index - 2])
            tiled = operand.shape[0] == held
            got.append(lax.all_gather(operand, "fsdp", axis=0, tiled=tiled))
        w_qkv = w_rest = got[0::2]
        w_ffn = [[both] for both in got[1::2]]
        skip = [3 * col] * layers
        ordered = got[0][:, first_size : first_size + vec_rows.shape[0]].T.astype(F32)
        w_out = got[0][:, 7 * col : first_size].reshape(n, col, layers, col)
        w_out = lax.all_to_all(w_out, "ctx", 0, 0).transpose(2, 1, 0, 3).reshape(layers, col, width)
    else:
        w_out = fetch_out()
        ordered = gather_planes(vec_rows.T).T.astype(F32)
        w_qkv, w_rest, w_ffn, skip = [], [], [], [0] * layers
        for layer in range(layers):
            blocks = [columns(self_qkv, layer, i * width + group * own, own) for i in range(3)]
            w_qkv.append(gather_planes(jnp.concatenate(blocks, axis=1)))
            blocks = [columns(cross_kv, layer, i * width + c * col, col) for i in range(2)]
            blocks += [columns(cross_q, layer, c * col, col), columns(cross_out, layer, c * col, col)]
            w_rest.append(gather_planes(jnp.concatenate(blocks, axis=1)))
            blocks = [
                columns(ffn_in, layer, (n * j + m * high_c + (j + low_c) % m) * piece, piece)
                for j in range(m)
            ]
            down = lax.dynamic_slice(ffn_out, (layer, unit_start, 0), (1, piece, width))[0]
            w_ffn.append([gather_planes(jnp.concatenate(blocks, axis=1)), gather_planes(down)])
    vectors = ordered[:-layers].reshape(layers, -1, width)
    up_bias = ordered[-layers:].reshape(layers, m, held)[:, :, :piece].reshape(layers, units)
    w_sems = pltpu.SemaphoreType.DMA((2 * m,))
    w_scratch = [pltpu.VMEM((width, units), LOW), pltpu.VMEM((units, width), LOW), w_sems]
    qv_bias = lax.dynamic_slice(vectors, (0, 6, group * own), (layers, 2, own))
    ev_bias = lax.dynamic_slice(vectors, (0, 10, c * col), (layers, 1, col))
    ev_bias = jnp.pad(ev_bias, ((0, 0), (0, 0), (col, 0)))

    def own_slots(values):
        if split == 1:
            return values
        shaped = values.reshape((n // split, split, rows) + values.shape[1:])
        return shaped[:, 0].reshape((-1,) + values.shape[1:])

    def share(parts):
        if split == 1:
            return parts[0]
        total = lax.dynamic_index_in_dim(parts, part, 0, False).astype(F32)
        for other in range(1, split):
            term = lax.dynamic_index_in_dim(parts, part ^ other, 0, False)
            total = total + swap(term, other).astype(F32)
        return total

    def half_slots(width_of, kind=LOW):
        return [like((n // 2, rows, width_of), kind)] * 2

    (encoder_all,) = call(
        partial(assemble_kernel, n, rows),
        [here] + first_slots,
        [like((source_length, width), LOW)],
        0,
        smem=1,
    )

    def prepare(layer, wait=()):
        return call(
            partial(cross_prepare_kernel, col, skip[layer]),
            [w_rest[layer], encoder_all, ev_bias[layer]],
            [like((2 * col, width + source_length), LOW)],
            4 * source_length * width * col,
            wait=wait,
        )[0]

    x = tokens[0]
    h1_slots = first_slots
    kept = []
    matmul = 2 * length * width
    for layer in range(layers):
        vec = vectors[layer]
        w_t = after(prepared if layer else prepare(0, packed[2:] if packs else ()), h1_slots)
        near = gather_near(w_t)
        joined = layer > 0
        h1_all, q, k, v, a, self_lse, *parts = call(
            partial(self_forward_kernel, n, rows, split, layer == 0, joined, head_width),
            h1_slots
            + [vec, after(qv_bias[layer], w_t), w_qkv[layer]]
            + self_bounds
            + [w_out[layer]] * joined,
            [like((length, width), LOW), like((queries, own), LOW)]
            + [like((length, own), LOW)] * 2
            + [like((queries, own), LOW), like((queries, own // head_width), F32)]
            + half_slots(width) * joined,
            matmul * 4 * own + 4 * queries * length * own,
            steps=int(packs),
            tiles={n + 2: ((width, 3 * own), None)} if packs else None,
        )
        if not joined:
            parts = call(
                partial(self_out_kernel, n, rows, split),
                [a, w_out[layer]],
                half_slots(width),
                matmul * own,
            )
        even, odd = parts
        near, odd = lax.optimization_barrier((near, odd))
        terms = reduce_slots(even, odd)
        w_slots, where = gather_joined(w_t, near)
        x1, x2, h2, cq, mixed, cross_lse, h3, wq_t, wo_t, ek_t, ev_t = call(
            partial(mid_forward_kernel, n, len(terms), len(w_slots), where, head_width),
            [here, x] + terms + w_slots + [vec] + cross_bounds,
            [like((rows, width), F32)] * 2
            + [like((rows, width), LOW)] * 3
            + [like((rows, HEADS), F32), like((rows, width), LOW)]
            + [like((width, width), LOW)] * 2
            + [like((width, source_length), LOW)] * 2,
            4 * rows * width * (width + source_length),
            smem=1,
        )
        h3_slots = gather_slots(h3)
        weight_count = len(w_ffn[layer])
        first = n + 1 + weight_count
        tile = 4 * rows
        g, slope, even, odd = call(
            partial(ffn_forward_kernel, n, weight_count),
            h3_slots + [up_bias[layer][None]] + w_ffn[layer],
            [like((length, units), LOW)] * 2 + half_slots(width),
            2 * matmul * units,
            scratch=[pltpu.VMEM((length, width), LOW)] + w_scratch,
            far=weight_count,
            steps=n // 4,
            tiles={first + i: ((tile, units), 0) for i in range(2)}
            | {first + 2 + i: ((2, rows, width), 0) for i in range(2)},
        )
        last = layer == layers - 1
        if last:
            result_parts = (even, odd)
        else:
            terms = reduce_slots(even, odd)
        kept.append(
            (x, x1, x2, h1_all, q, k, v, a, self_lse, h2, cq, mixed, cross_lse)
            + (h3_slots, g, slope, wq_t, wo_t, ek_t, ev_t)
        )
        if last:
            continue
        prepared = prepare(layer + 1)
        outs = call(
            partial(between_kernel, len(terms), False),
            [x2] + terms + [vec, vectors[layer + 1]],
            [like((rows, width), F32), like((rows, width), LOW)],
            rows * width * 20,
        )
        x = outs[0]
        h1_slots = gather_slots(outs[1])

    r = width // (n * m)
    grad_x, e3_slots = grad_out[0], last_slots
    enc_total = jnp.zeros((source_length, width), F32)
    vec_sums = [None] * layers
    moves = [
        (i * m + p, ((n // m) * ((p - i % m) % m) + i // m) * m + p) for i in range(n) for p in range(m)
    ]

    def to_rows(summed):
        return lax.all_to_all(summed.reshape(n, r, summed.shape[1]), "ctx", 0, 0)

    finish = []
    for layer in reversed(range(layers)):
        x, x1, x2, h1_all, q, k, v, a, self_lse, h2, cq, mixed, cross_lse = kept[layer][:13]
        h3_slots, g, slope, wq_t, wo_t, ek_t, ev_t = kept[layer][13:]
        vec = vectors[layer]
        if finish:
            slope = after(slope, cross_grad)
        weight_count = len(w_ffn[layer])
        first = n + 1 + weight_count
        tile = 4 * rows
        du, fc1_grad, even, odd = call(
            partial(ffn_backward_kernel, n, weight_count),
            e3_slots + [slope] + w_ffn[layer],
            [like((length, units), LOW), like((1, units), F32)] + half_slots(width),
            2 * matmul * units,
            scratch=[pltpu.VMEM((length, width), LOW)] + w_scratch,
            far=weight_count,
            steps=n // 4,
            tiles={n: ((tile, units), 0), first: ((tile, units), 0)}
            | {first + 2 + i: ((2, rows, width), 0) for i in range(2)},
        )
        terms = reduce_slots(even, odd)
        shapes = [like((m, n * r, units), LOW), like((m, piece + 16, width), LOW)]
        if units == width:
            shapes = [like((m, n * r + piece + 16, width), LOW)]
        ffn_grads = call(
            partial(ffn_weights_kernel, n, m),
            [here, after(du, terms[0]), g, fc1_grad] + h3_slots + e3_slots,
            shapes,
            2 * matmul * units,
            scratch=[pltpu.VMEM((length, width), LOW)] * 2,
            smem=1,
        )
        x1 = after(x1, ffn_grads)
        if layer == 0:
            result_terms = reduce_slots(*result_parts)
        dx1, e1, e2, dcq, even, odd, sums = call(
            partial(mid_backward_kernel, n, len(terms), head_width),
            [here, grad_x]
            + terms
            + [x1, x2, vec, wq_t, wo_t, ek_t, ev_t, cq, cross_lse]
            + cross_bounds,
            [like((rows, width), F32)]
            + [like((rows, width), LOW)] * 3
            + [like((n // 2, 2 * col, source_length), LOW)] * 2
            + [like((8, width), F32)],
            4 * rows * width * width + 10 * rows * source_length * width,
            scratch=[pltpu.VMEM((width, source_length), LOW)] * 2,
            smem=1,
        )
        ffn_sums = [reduce_planes(grad) for grad in after(ffn_grads, dx1 if layer else terms)]
        e1_slots = gather_slots(e1)
        kv_parts = [even, odd]
        even, *odd = call(
            partial(cross_weights_kernel, n),
            [here, h2, dcq, mixed, e2] + kv_parts,
            [like((n // size, 2 * col, width + source_length), LOW) for size in (2, 4, 4)],
            4 * rows * width * width,
            scratch=[pltpu.VMEM((width, width), LOW)] * 2,
            smem=1,
            wait=[entry[2] for entry in finish[-1:]] + ([] if layer else result_terms[1:]),
        )
        w_terms = reduce_slots(even, list(odd), hold=e1_slots)
        e1_own, dq, dkv, even, odd = call(
            partial(self_backward_kernel, n, split, head_width),
            e1_slots + [w_out[layer], w_qkv[layer], after(q, w_terms[0]), k, v, self_lse] + self_bounds,
            [like((queries, width), LOW), like((queries, own), LOW), like((length, 2 * own), LOW)]
            + half_slots(width),
            matmul * 4 * own + 10 * queries * length * own,
            scratch=[pltpu.VMEM((length, own), F32)] * 2,
            steps=int(packs),
            tiles={n + 1: ((width, 3 * own), None)} if packs else None,
        )
        if split > 1:
            shaped = dkv.reshape(n // split, split, rows, 2 * own)
            total = shaped[:, 0].astype(F32)
            for other in range(1, split):
                total = total + swap(shaped[:, other], other).astype(F32)
            dkv = total.astype(LOW).reshape(-1, 2 * own)
            even = dot_t(jnp.concatenate([dq, dkv], axis=1), w_qkv[layer][:, : 3 * own])
            even = even.reshape(n // 2, rows, width)
            odd = jnp.zeros_like(even)
        terms = reduce_slots(even, after(odd, w_terms))
        before = []
        if layer == 0:
            sums_of = [ffn_sums] + [done[1] for done in reversed(finish)]
            up_rows = to_rows(jnp.concatenate([sums[0][: n * r] for sums in sums_of], axis=1))
            down_rows = [sums[0][n * r :] if units == width else sums[1] for sums in sums_of]
            down_rows = lax.ppermute(jnp.stack(down_rows), ("ctx", "fsdp"), moves)
            before = [up_rows, down_rows]
            *ffn_grads, fc1_own = call(
                partial(place_ffn_kernel, n, m, layers),
                [up_rows, down_rows],
                [like((layers, r, hidden), F32), like((layers, piece, width), F32), like((layers, piece), F32)],
                layers * r * hidden,
            )
        grad_x, e3, last_sums = call(
            partial(last_backward_kernel, len(terms)),
            [dx1] + terms + [x, vec],
            [like((rows, width), F32), like((rows, width), LOW), like((2, width), F32)],
            rows * width * 20,
            wait=before,
        )

        e3_slots = gather_slots(e3) if layer else None
        hold = (e3_slots[2], e3_slots[4]) if layer else terms[0]
        own_parts = [h1_all, dq, dkv, a, e1_own] if split == 1 else []
        cross_grad, enc_total, ev_sum, *enc_parts = call(
            partial(attention_weights_kernel, n, m, skip[layer], len(terms), split == 1),
            [here]
            + w_terms
            + own_parts
            + [encoder_all, w_rest[layer], after(enc_total, hold)],
            [like((m, n * r, (8 if split == 1 else 4) * col), LOW)]
            + [like((source_length, width), F32), like((2 * col, 1), F32)]
            + [like((n // 2, source_rows, width), F32)] * 2,
            8 * source_length * col * width + matmul * 4 * own,
            smem=1,
            wait=ffn_sums,
        )
        if split > 1:
            qkv_grad = t_dot(own_slots(h1_all), jnp.concatenate([dq, dkv], axis=1)).astype(LOW)
            qkv_grad = share(qkv_grad.reshape(width, 3, split, col).transpose(2, 0, 1, 3))
            qkv_grad = qkv_grad.astype(LOW).reshape(n, m, r, 3 * col).transpose(1, 0, 2, 3)
            o_grad = share(t_dot(a, e1_own).astype(LOW).reshape(split, own // split, width))
            o_grad = o_grad.astype(LOW).reshape(m, r, n, col).transpose(0, 2, 1, 3)
            kv_q = jnp.split(cross_grad, [2 * col], axis=2)
            self_grad = jnp.concatenate([qkv_grad, o_grad], axis=3).reshape(m, n * r, 4 * col)
            parts = [kv_q[0], self_grad[:, :, : 3 * col], kv_q[1], self_grad[:, :, 3 * col :]]
            cross_grad = jnp.concatenate(parts, axis=2)
        both_sum = reduce_planes(cross_grad)
        finish.append((layer, ffn_sums, both_sum))
        zero = jnp.zeros((1, width), F32)
        summed = jnp.concatenate(
            [last_sums[0:1], sums[0:2], last_sums[1:2], sums[2:4], zero, zero]
            + [sums[4:6], zero, sums[6:8]]
        )
        owned_q = share(row_sum(dq).reshape(split, col))
        owned_v = share(row_sum(dkv[:, own:]).reshape(split, col))
        blank = jnp.zeros((col,), F32)
        owned = [blank] * 6 + [owned_q, owned_v, blank, blank, ev_sum[col:, 0], blank, blank]
        vec_sums[layer] = (summed, jnp.stack(owned))

    finish.sort(key=lambda entry: entry[0])
    (result,) = call(
        partial(between_kernel, len(result_terms), True),
        [kept[-1][2]] + result_terms + [vectors[-1]],
        [like((rows, width), LOW)],
        rows * width * 20,
    )
    summed = jnp.concatenate([pair[0] for pair in vec_sums])
    owned = jnp.concatenate([pair[1] for pair in vec_sums])
    enc_grad = total_of(reduce_slots(*enc_parts, F32))
    summed = turn(summed, 1).reshape(-1, n, col).transpose(1, 0, 2)
    vec = total_of(reduce_slots(summed[0::2], summed[1::2], F32)) + owned
    (late,) = call(
        late_kernel,
        [entry[2] for entry in finish],
        [like((n * r, layers * 5 * col), LOW)],
        0,
        wait=[up_rows, down_rows],
    )
    late_rows = to_rows(late)
    (vec,) = call(copy_kernel, [vec], [like(vec.shape, F32)], 0, wait=[late])
    attention_grads = call(
        partial(place_attention_kernel, n, layers),
        [late_rows] + [entry[2] for entry in finish],
        [like((layers, r, parts * width), F32) for parts in (3, 1, 1, 2, 1)],
        layers * r * 8 * width,
    )
    vec = sum_planes(vec.reshape(-1, m, col // m).transpose(1, 0, 2))
    vec = vec.reshape(layers, -1, col // m)
    return (
        (result[None], grad_x[None], enc_grad[None])
        + tuple(attention_grads)
        + tuple(ffn_grads)
        + (vec[:, :3], vec[:, 3:], fc1_own)
    )


def solution(mesh):
    tokens = P("fsdp", "ctx", None)
    per_stream = P("fsdp", None)
    weight = P(None, "fsdp", None)
    vector = P(None, None, "fsdp")
    grad = P(None, ("ctx", "fsdp"), None)
    vector_grad = P(None, None, ("ctx", "fsdp"))
    return jax.shard_map(
        on_device,
        mesh=mesh,
        in_specs=(tokens,) * 3 + (per_stream,) * 3 + (weight,) * 7 + (vector,) * 2 + (P(None, "fsdp"),),
        out_specs=(tokens,) * 3 + (grad,) * 7 + (vector_grad,) * 2 + (P(None, ("ctx", "fsdp")),),
        check_vma=False,
    )
```

```python
from functools import partial

import jax
import jax.numpy as jnp
from jax import lax
from jax.experimental import pallas as pl
from jax.experimental.pallas import tpu as pltpu
from jax.sharding import PartitionSpec as P

HEADS = 16
EPSILON = 1e-05
NEGATIVE = -1e30
F32 = jnp.float32
LOW = jnp.bfloat16
VMEM = pl.BlockSpec(memory_space=pltpu.VMEM)
SMEM = pl.BlockSpec(memory_space=pltpu.SMEM)
FAR = pl.BlockSpec(memory_space=pl.ANY)
VMEM_BYTES = 60 * 2**20


def swap(values, bits):
    count = lax.axis_size("ctx")
    return lax.ppermute(values, "ctx", [(i, i ^ bits) for i in range(count)])


def gather_near(rows):
    if lax.axis_size("ctx") == 8:
        return swap(rows, 2), swap(rows, 4)
    return ()


def gather_slots(rows, near=None):
    count = lax.axis_size("ctx")
    if count == 8:
        near_x, near_y = near or gather_near(rows)
        half = rows.shape[0] // 2
        far = jnp.concatenate([swap(near_x[:half], 4), swap(near_y[half:], 2)])
        blocks = []
        for block in (rows, near_x, near_y, far):
            blocks += [block, swap(block, 1)]
        return blocks
    blocks = [rows]
    bit = 1
    while bit < count:
        blocks = blocks + [swap(block, bit) for block in blocks]
        bit *= 2
    return blocks


def gather_joined(rows, near):
    count = lax.axis_size("ctx")
    size = rows.shape[0]
    if count == 8:
        half = size // 2
        joined = swap(jnp.concatenate([rows, *near]), 1)
        far = jnp.concatenate([swap(near[0][:half], 4), swap(near[1][half:], 2)])
        arrays = [rows, *near, far, joined, swap(far, 1)]
        where = [(0, 0), (4, 0), (1, 0), (4, size), (2, 0), (4, 2 * size), (3, 0), (5, 0)]
        return arrays, where
    return gather_slots(rows), [(k, 0) for k in range(count)]


def reduce_slots(even, odd, kind=LOW, hold=None):
    count = lax.axis_size("ctx")
    odd = [swap(block.astype(kind), 1) for block in (odd if isinstance(odd, list) else [odd])]
    if count == 8:
        size = odd[0].shape[0]
        chip = [even[i].astype(F32) + odd[i // size][i % size].astype(F32) for i in range(4)]
        sent = [chip[i].astype(kind) for i in (1, 2, 3)]
        if hold is not None:
            sent = after(sent, hold)
        return [chip[0]] + [swap(sent[i], 2 * i + 2) for i in range(3)]
    chip = even.astype(F32) + jnp.concatenate(odd).astype(F32)
    bit = count // 4
    while bit:
        chip = chip[:bit] + swap(chip[bit : 2 * bit].astype(kind), 2 * bit).astype(F32)
        bit //= 2
    return [chip[0]]


def total_of(terms):
    total = terms[0].astype(F32)
    for term in terms[1:]:
        total = total + term.astype(F32)
    return total


def turn(values, axis):
    count = lax.axis_size("ctx")
    here = lax.axis_index("ctx")
    width = values.shape[axis] // count
    return jnp.concatenate(
        [
            lax.dynamic_slice_in_dim(values, (here ^ k) * width, width, axis)
            for k in range(count)
        ],
        axis=axis,
    )


def sum_planes(parts):
    count = lax.axis_size("fsdp")
    here = lax.axis_index("fsdp")
    total = lax.dynamic_index_in_dim(parts, here, 0, False)
    for step in range(1, count):
        term = lax.dynamic_index_in_dim(parts, (here + step) % count, 0, False)
        total = total + lax.ppermute(term, "fsdp", [(i, (i + step) % count) for i in range(count)])
    return total


def after(values, other):
    return lax.optimization_barrier((values, other))[0]


def gather_planes(values):
    return lax.all_gather(values, "fsdp", axis=0, tiled=True)


def reduce_planes(parts):
    return lax.psum_scatter(parts, "fsdp", scatter_dimension=0, tiled=False)


def layer_norm(values, gain_row, offset_row):
    center = values - jnp.mean(values, axis=-1, keepdims=True)
    spread = jnp.mean(center * center, axis=-1, keepdims=True)
    return center * lax.rsqrt(spread + EPSILON) * gain_row + offset_row


def layer_norm_back(values, gain_row, grad):
    center = values - jnp.mean(values, axis=-1, keepdims=True)
    inverse = lax.rsqrt(jnp.mean(center * center, axis=-1, keepdims=True) + EPSILON)
    normed = center * inverse
    scaled = grad * gain_row
    back = inverse * (
        scaled
        - jnp.mean(scaled, axis=-1, keepdims=True)
        - normed * jnp.mean(scaled * normed, axis=-1, keepdims=True)
    )
    return back, row_sum(grad * normed), row_sum(grad)


def row_sum(values):
    return jnp.sum(values.astype(F32), axis=0, keepdims=True)


def dot(left, right):
    return jnp.dot(left, right, preferred_element_type=F32)


def dot_t(left, right):
    return lax.dot_general(left, right, (((1,), (1,)), ((), ())), preferred_element_type=F32)


def t_dot(left, right):
    return lax.dot_general(left, right, (((0,), (0,)), ((), ())), preferred_element_type=F32)


def call(kernel, ins, outs, flops, scratch=(), smem=0, far=0, wait=(), steps=0, tiles=None):
    count, extra = len(ins), len(wait)

    def spec(index, array):
        if not steps and not (tiles and index in tiles):
            return VMEM
        block, axis = (tiles or {}).get(index, (array.shape, None))
        dims = len(block)
        if not steps:
            return pl.BlockSpec(block, lambda: (0,) * dims)
        return pl.BlockSpec(block, lambda i: tuple(i if d == axis else 0 for d in range(dims)))

    def body(*refs):
        kernel(*refs[:count], *refs[count + extra :])

    moved = sum(a.size * a.dtype.itemsize for a in ins)
    moved += sum(a.size * a.dtype.itemsize for a in outs)
    return pl.pallas_call(
        body,
        grid=(steps,) if steps else (),
        in_specs=[SMEM] * smem
        + [spec(i, ins[i]) for i in range(smem, count - far)]
        + [FAR] * (far + extra),
        out_specs=[spec(count + i, array) for i, array in enumerate(outs)],
        out_shape=outs,
        scratch_shapes=list(scratch),
        compiler_params=pltpu.CompilerParams(vmem_limit_bytes=VMEM_BYTES),
        cost_estimate=pl.CostEstimate(flops=int(flops), bytes_accessed=int(moved), transcendentals=0),
    )(*ins, *wait)


def like(shape, kind):
    return jax.ShapeDtypeStruct(tuple(shape), kind)


def tile_rows(rows, size):
    return pl.ds(pl.multiple_of(rows * size, size), size)


def join_rows(blocks, out_ref):
    rows = blocks[0].shape[0]
    for k, block in enumerate(blocks):
        out_ref[k * rows : (k + 1) * rows] = block[...]


def put_slots(even_ref, odd_ref, index, values):
    rows = even_ref.shape[1]
    for i in range(values.shape[0] // (2 * rows)):
        even_ref[index + i] = values[2 * i * rows : (2 * i + 1) * rows].astype(LOW)
        odd_ref[index + i] = values[(2 * i + 1) * rows : (2 * i + 2) * rows].astype(LOW)


def pairs_at_once(n, rows, split):
    return 2 if split == 1 and n % 4 == 0 and n * rows <= 1024 else 1


def self_forward_kernel(n, rows, split, raw, joined, head_width, *refs):
    blocks, refs = refs[:n], refs[n:]
    vec_ref, bias_ref, w_ref, low_ref, high_ref, place_ref = refs[:6]
    (wo_ref, *refs) = refs[6:] if joined else (None, *refs[6:])
    h_ref, q_ref, k_ref, v_ref, a_ref, lse_ref, *out_refs = refs
    own = k_ref.shape[1]
    for k in range(n):
        block = blocks[k][:rows]
        if raw:
            block = layer_norm(block.astype(F32), vec_ref[0:1], vec_ref[3:4]).astype(LOW)
        h_ref[k * rows : (k + 1) * rows] = block

    @pl.loop(0, n // 2)
    def _(i):
        at = tile_rows(i, 2 * rows)
        z = dot(h_ref[at], w_ref[:, : 3 * own])
        q = ((z[:, :own] + bias_ref[0:1]) * 0.125).astype(LOW)
        if split == 1:
            q_ref[at] = q
        else:
            q_ref[tile_rows(i, rows)] = q[:rows]
        k_ref[at] = z[:, own : 2 * own].astype(LOW)
        v_ref[at] = (z[:, 2 * own :] + bias_ref[1:2]).astype(LOW)

    wide = pairs_at_once(n, rows, split)
    step = 2 * rows * wide // split

    @pl.loop(0, n // 2 // wide)
    def _(i):
        at = tile_rows(i, step)
        mask = (place_ref[...] >= low_ref[at]) & (place_ref[...] <= high_ref[at])
        outs, masses = [], []
        for start in range(0, own, head_width):
            span = slice(start, start + head_width)
            scores = jnp.where(mask, dot_t(q_ref[at, span], k_ref[:, span]), NEGATIVE)
            top = jnp.max(scores, axis=1, keepdims=True)
            raised = jnp.exp(scores - top)
            mass = jnp.sum(raised, axis=1, keepdims=True)
            outs.append(dot((raised * (1.0 / mass)).astype(LOW), v_ref[:, span]))
            masses.append(top + jnp.log(mass))
        a = jnp.concatenate(outs, axis=1).astype(LOW)
        a_ref[at] = a
        lse_ref[at] = jnp.concatenate(masses, axis=1)
        if joined:
            put_product(split, a, wo_ref, *out_refs, i * wide)


def put_product(split, a, wo_ref, even_ref, odd_ref, i):
    y = dot(a, wo_ref[...])
    if split > 1:
        y = jnp.concatenate([y, jnp.zeros_like(y)])
    put_slots(even_ref, odd_ref, i, y)


def self_out_kernel(n, rows, split, a_ref, wo_ref, even_ref, odd_ref):
    wide = pairs_at_once(n, rows, split)
    step = 2 * rows * wide // split

    @pl.loop(0, n // 2 // wide)
    def _(i):
        put_product(split, a_ref[tile_rows(i, step)], wo_ref, even_ref, odd_ref, i * wide)


def mid_forward_kernel(n, terms, arrays, where, head_width, here_ref, *refs):
    x_ref, refs = refs[0], refs[1:]
    term_refs, refs = refs[:terms], refs[terms:]
    w_refs, refs = refs[:arrays], refs[arrays:]
    vec_ref, low_ref, high_ref, place_ref = refs[:4]
    x1_ref, x2_ref, h2_ref, cq_ref, c_ref, lse_ref, h3_ref = refs[4:11]
    wq_ref, wo_ref, ek_ref, ev_ref = refs[11:]
    col = w_refs[0].shape[0] // 2
    width = wq_ref.shape[1]
    here = here_ref[0]
    for k in range(n):
        at = tile_rows(here ^ k, col)
        array, first = where[k]
        top, bottom = pl.ds(first, col), pl.ds(first + col, col)
        wq_ref[at] = w_refs[array][top, :width]
        wo_ref[at] = w_refs[array][bottom, :width]
        ek_ref[at] = w_refs[array][top, width:]
        ev_ref[at] = w_refs[array][bottom, width:]
    x1 = x_ref[...].astype(F32) + total_of([t[...] for t in term_refs]) + vec_ref[8:9]
    x1_ref[...] = x1
    h2 = layer_norm(x1, vec_ref[1:2], vec_ref[4:5]).astype(LOW)
    h2_ref[...] = h2
    cq_ref[...] = ((dot_t(h2, wq_ref[...]) + vec_ref[9:10]) * 0.125).astype(LOW)
    mask = (place_ref[...] >= low_ref[...]) & (place_ref[...] <= high_ref[...])
    outs, masses = [], []
    for start in range(0, cq_ref.shape[1], head_width):
        span = slice(start, start + head_width)
        scores = jnp.where(mask, dot(cq_ref[:, span], ek_ref[span]), NEGATIVE)
        top = jnp.max(scores, axis=1, keepdims=True)
        raised = jnp.exp(scores - top)
        mass = jnp.sum(raised, axis=1, keepdims=True)
        outs.append(dot_t((raised * (1.0 / mass)).astype(LOW), ev_ref[span]))
        masses.append(top + jnp.log(mass))
    c_ref[...] = jnp.concatenate(outs, axis=1).astype(LOW)
    lse_ref[...] = jnp.concatenate(masses, axis=1)
    x2 = x1 + dot_t(c_ref[...], wo_ref[...]) + vec_ref[11:12]
    x2_ref[...] = x2
    h3_ref[...] = layer_norm(x2, vec_ref[2:3], vec_ref[5:6]).astype(LOW)


def copies_of(sources, up_ref, down_ref, sems):
    if len(sources) == 2:
        pairs = [(sources[0], up_ref), (sources[1], down_ref)]
    else:
        planes, both = sources[0].shape[:2]
        size = up_ref.shape[0] // planes
        pairs = []
        for j in range(planes):
            at = pl.ds(j * size, size)
            pairs.append((sources[0].at[j, pl.ds(0, size)], up_ref.at[at]))
            pairs.append((sources[0].at[j, pl.ds(size, size)], down_ref.at[at]))
    return [pltpu.make_async_copy(a, b, sems.at[i]) for i, (a, b) in enumerate(pairs)]


def ffn_forward_kernel(n, sources, *refs):
    blocks, refs = refs[:n], refs[n:]
    bias_ref, refs = refs[0], refs[1:]
    sources, refs = refs[:sources], refs[sources:]
    g_ref, slope_ref, even_ref, odd_ref, h_ref, up_ref, down_ref, sems = refs
    step = pl.program_id(0)

    @pl.when(step == 0)
    def _():
        copies = copies_of(sources, up_ref, down_ref, sems)
        for copy in copies:
            copy.start()
        join_rows(blocks, h_ref)
        for copy in copies:
            copy.wait()

    u = dot(h_ref[tile_rows(step, g_ref.shape[0])], up_ref[...]) + bias_ref[...]
    share = 0.5 + 0.5 * lax.erf(u * 0.7071067811865476)
    g = (u * share).astype(LOW)
    g_ref[...] = g
    slope_ref[...] = (share + u * (jnp.exp(-0.5 * u * u) * 0.3989422804014327)).astype(LOW)
    put_slots(even_ref, odd_ref, 0, dot(g, down_ref[...]))


def ffn_backward_kernel(n, sources, *refs):
    blocks, refs = refs[:n], refs[n:]
    slope_ref, refs = refs[0], refs[1:]
    sources, refs = refs[:sources], refs[sources:]
    du_ref, sum_ref, even_ref, odd_ref, e_ref, up_ref, down_ref, sems = refs
    step = pl.program_id(0)

    @pl.when(step == 0)
    def _():
        copies = copies_of(sources, up_ref, down_ref, sems)
        for copy in copies:
            copy.start()
        join_rows(blocks, e_ref)
        sum_ref[...] = jnp.zeros_like(sum_ref)
        for copy in copies:
            copy.wait()

    grad = dot_t(e_ref[tile_rows(step, du_ref.shape[0])], down_ref[...])
    du = (grad * slope_ref[...].astype(F32)).astype(LOW)
    du_ref[...] = du
    sum_ref[...] += row_sum(du)
    put_slots(even_ref, odd_ref, 0, dot_t(du, up_ref[...]))


def pack_kernel(m, n, jobs, where_ref, *refs):
    count = sum(len(FED[kind]) for kind, layer in jobs)
    sources, packed, sems = refs[:count], refs[count:-1], refs[-1]
    c, f = where_ref[0], where_ref[1]
    high, low = c // m, c % m
    copies = []

    def add(source, target):
        copies.append(pltpu.make_async_copy(source, target, sems.at[len(copies)]))

    def columns(start, size):
        return pl.ds(pl.multiple_of(start, 128), size)

    for (kind, layer), target in zip(jobs, packed):
        fed, sources = sources[: len(FED[kind])], sources[len(FED[kind]) :]
        at = 0
        if kind == "ffn":
            up, down = fed
            rows, piece = up.shape[1], down.shape[1] // n
            for j in range(m):
                start = (n * j + m * high + (j + low) % m) * piece
                add(up.at[layer, :, columns(start, piece)], target.at[pl.ds(0, rows), pl.ds(j * piece, piece)])
            start = (m * high + (f + low) % m) * piece
            add(down.at[layer, pl.ds(pl.multiple_of(start, piece), piece)], target.at[pl.ds(rows, piece)])
            continue
        for source, (name, parts) in zip(fed, FED[kind].items()):
            if parts == 0:
                add(source, target.at[:, pl.ds(at, source.shape[1])])
                continue
            width = source.shape[2] // parts
            col = width // n
            if name == "self_out":
                for l in range(source.shape[0]):
                    add(source.at[l, :, columns(c * col, col)], target.at[:, pl.ds(at, col)])
                    at += col
                continue
            for i in range(parts):
                add(source.at[layer, :, columns(i * width + c * col, col)], target.at[:, pl.ds(at, col)])
                at += col
    for copy in copies:
        copy.start()
    for copy in copies:
        copy.wait()


FED = {
    "first": {"qkv": 3, "kv": 2, "q": 1, "out": 1, "self_out": 1, "vec": 0},
    "attention": {"qkv": 3, "kv": 2, "q": 1, "out": 1},
    "ffn": {"up": 1, "down": 1},
}


def late_kernel(*refs):
    out_ref = refs[-1]
    size = out_ref.shape[1] // (len(refs) - 1)
    for layer, ref in enumerate(refs[:-1]):
        out_ref[:, layer * size : (layer + 1) * size] = ref[:, :size]


def copy_kernel(*refs):
    count = len(refs) // 2
    for in_ref, out_ref in zip(refs[:count], refs[count:]):
        out_ref[...] = in_ref[...]


def assemble_kernel(n, skip, here_ref, *refs):
    out_ref = refs[n]
    size = refs[0].shape[0] - skip
    for k in range(n):
        out_ref[tile_rows(here_ref[0] ^ k, size)] = refs[k][skip:]


def cross_prepare_kernel(col, skip, w_ref, enc_ref, bias_ref, out_ref):
    kv = dot(enc_ref[...], w_ref[:, skip : skip + 2 * col]) + bias_ref[...]
    width = w_ref.shape[0]
    out_ref[:, width:] = kv.T.astype(LOW)
    out_ref[:, :width] = w_ref[:, skip + 2 * col : skip + 4 * col].astype(F32).T.astype(LOW)


def between_kernel(terms, last, *refs):
    x2_ref, refs = refs[0], refs[1:]
    term_refs, refs = refs[:terms], refs[terms:]
    y = x2_ref[...] + total_of([t[...] for t in term_refs]) + refs[0][12:13]
    if last:
        refs[1][...] = y.astype(LOW)
    else:
        next_ref, y_ref, h_ref = refs[1:]
        y_ref[...] = y
        h_ref[...] = layer_norm(y, next_ref[0:1], next_ref[3:4]).astype(LOW)


def put_folded(out_ref, grad, at, n, m):
    size, width = grad.shape[0] // m, grad.shape[1] // n
    for p in range(m):
        for i in range(n):
            block = grad[p * size : (p + 1) * size, i * width : (i + 1) * width]
            out_ref[p, i * size : (i + 1) * size, at : at + width] = block


def attention_weights_kernel(n, m, skip, terms, full, here_ref, *refs):
    w_refs, refs = refs[:terms], refs[terms:]
    own_refs, refs = (refs[:5], refs[5:]) if full else ((), refs)
    enc_ref, w_kv_ref, before_ref, out_ref, total_ref, sum_ref, even_ref, odd_ref = refs
    col = w_refs[0].shape[0] // 2
    width = w_kv_ref.shape[0]
    grad = total_of([t[:, :width] for t in w_refs]).astype(LOW)
    for i in range(2):
        at = (5 + i if full else 2 + i) * col
        put_folded(out_ref, grad[i * col : (i + 1) * col], at, n, m)
    dkv_t = total_of([t[:, width:] for t in w_refs])
    sum_ref[...] = jnp.sum(dkv_t.astype(LOW).astype(F32), axis=1, keepdims=True)
    dkv = dkv_t.T.astype(LOW)
    total_ref[...] = before_ref[...] + dot_t(dkv, w_kv_ref[:, skip : skip + 2 * col])
    put_by_rows(out_ref, t_dot(enc_ref[...], dkv).astype(LOW), 0, width, n, m)
    for k in range(n):
        part = total_ref[tile_rows(here_ref[0] ^ k, even_ref.shape[1])]
        (odd_ref if k % 2 else even_ref)[k // 2] = part
    if not full:
        return
    h_ref, dq_ref, dkv_ref, a_ref, e_ref = own_refs
    own = dq_ref.shape[1]
    step = min(256, width)
    for first in range(0, width, step):
        part = h_ref[:, first : first + step]
        grad = jnp.concatenate([t_dot(part, dq_ref[...]), t_dot(part, dkv_ref[...])], axis=1)
        put_by_rows(out_ref, grad.astype(LOW), first, width, n, m, 2 * own)
    put_folded(out_ref, t_dot(a_ref[...], e_ref[...]).astype(LOW), 7 * own, n, m)


def put_by_rows(out_ref, grad, first, total, n, m, at=0):
    size = total // (n * m)
    for i in range(grad.shape[0] // size):
        block = first // size + i
        device, plane = block // m, block % m
        part = grad[i * size : (i + 1) * size]
        out_ref[plane, device * size : (device + 1) * size, at : at + grad.shape[1]] = part


def ffn_weights_kernel(n, m, here_ref, du_ref, g_ref, sum_ref, *refs):
    h_blocks, e_blocks, outs = refs[:n], refs[n : 2 * n], refs[2 * n : -2]
    h_ref, e_ref = refs[-2:]
    up_ref, down_ref = outs if len(outs) == 2 else (outs[0], None)
    join_rows(h_blocks, h_ref)
    join_rows(e_blocks, e_ref)
    piece = g_ref.shape[1] // m
    low = here_ref[0] % m
    first = h_ref.shape[1] // m if down_ref is None else 0
    down_ref = up_ref if down_ref is None else down_ref
    for j in range(m):
        plane = (low + j) % m
        grad = t_dot(g_ref[:, j * piece : (j + 1) * piece], e_ref[...]).astype(LOW)
        down_ref[plane, first : first + piece] = grad
        part = jnp.broadcast_to(sum_ref[:, j * piece : (j + 1) * piece], (16, piece))
        top = lax.broadcasted_iota(jnp.int32, (16, piece), 0) == 0
        down_ref[plane, first + piece :] = jnp.zeros((16, down_ref.shape[2]), LOW)
        down_ref[plane, first + piece :, :piece] = jnp.where(top, part, 0.0).astype(LOW)
    step = min(256, h_ref.shape[1])
    for first in range(0, h_ref.shape[1], step):
        grad = t_dot(h_ref[:, first : first + step], du_ref[...]).astype(LOW)
        put_by_rows(up_ref, grad, first, h_ref.shape[1], n, m)


def mid_backward_kernel(n, terms, head_width, here_ref, *refs):
    dy_ref, refs = refs[0], refs[1:]
    term_refs, refs = refs[:terms], refs[terms:]
    x1_ref, x2_ref, vec_ref, wq_ref, wo_ref, ek_ref, ev_ref, cq_ref, lse_ref = refs[:9]
    low_ref, high_ref, place_ref = refs[9:12]
    dx1_ref, e1_ref, e2_ref, dcq_ref, even_ref, odd_ref, sum_ref = refs[12:19]
    dek_ref, dev_ref = refs[19:]
    col = even_ref.shape[1] // 2
    dy = dy_ref[...].astype(F32)
    back, gain_two, shift_two = layer_norm_back(
        x2_ref[...], vec_ref[2:3], total_of([t[...] for t in term_refs])
    )
    dx2 = dy + back
    e2 = dx2.astype(LOW)
    e2_ref[...] = e2
    d_all = dot(e2, wo_ref[...]).astype(LOW)
    mask = (place_ref[...] >= low_ref[...]) & (place_ref[...] <= high_ref[...])
    dqs = []
    for index, start in enumerate(range(0, cq_ref.shape[1], head_width)):
        span = slice(start, start + head_width)
        q, d, ek, ev = cq_ref[:, span], d_all[:, span], ek_ref[span], ev_ref[span]
        weights = jnp.where(mask, jnp.exp(dot(q, ek) - lse_ref[:, index : index + 1]), 0.0)
        weight_grad = dot(d, ev)
        delta = jnp.sum(weights * weight_grad, axis=1, keepdims=True)
        score_grad = (weights * (weight_grad - delta)).astype(LOW)
        dqs.append(dot_t(score_grad, ek))
        dek_ref[span] = t_dot(q, score_grad).astype(LOW)
        dev_ref[span] = t_dot(d, weights.astype(LOW)).astype(LOW)
    dcq = (jnp.concatenate(dqs, axis=1).astype(LOW).astype(F32) * 0.125).astype(LOW)
    dcq_ref[...] = dcq
    here = here_ref[0]
    for k in range(n):
        at = tile_rows(here ^ k, col)
        out = odd_ref if k % 2 else even_ref
        out[k // 2, :col] = dek_ref[at]
        out[k // 2, col:] = dev_ref[at]
    back, gain_one, shift_one = layer_norm_back(x1_ref[...], vec_ref[1:2], dot(dcq, wq_ref[...]))
    dx1 = dx2 + back
    dx1_ref[...] = dx1
    e1 = dx1.astype(LOW)
    e1_ref[...] = e1
    sums = [gain_one, gain_two, shift_one, shift_two]
    sums += [row_sum(e1), row_sum(dcq), row_sum(e2), row_sum(dy)]
    sum_ref[...] = jnp.concatenate(sums, axis=0)


def cross_weights_kernel(n, here_ref, h_ref, dcq_ref, c_ref, e_ref, kv_even, kv_odd, even_ref, *refs):
    odd_refs, (q_ref, o_ref) = refs[:2], refs[2:]
    col = even_ref.shape[1] // 2
    width = q_ref.shape[1]
    q_ref[...] = t_dot(h_ref[...], dcq_ref[...]).astype(LOW)
    o_ref[...] = t_dot(c_ref[...], e_ref[...]).astype(LOW)
    here = here_ref[0]
    for k in range(n):
        at = tile_rows(here ^ k, col)
        out, i = (odd_refs[2 * k // n], k // 2 % (n // 4)) if k % 2 else (even_ref, k // 2)
        out[i, :col, :width] = q_ref[at]
        out[i, col:, :width] = o_ref[at]
    even_ref[:, :, width:] = kv_even[...]
    for i in range(2):
        odd_refs[i][:, :, width:] = kv_odd[i * n // 4 : (i + 1) * n // 4]


def self_backward_kernel(n, split, head_width, *refs):
    blocks, refs = refs[:n], refs[n:]
    wo_ref, w_ref, q_ref, k_ref, v_ref, lse_ref, low_ref, high_ref, place_ref = refs[:9]
    e_ref, dq_ref, dkv_ref, even_ref, odd_ref, dk_ref, dv_ref = refs[9:]
    rows = blocks[0].shape[0]
    own = wo_ref.shape[0]
    for i, k in enumerate(range(0, n, split)):
        e_ref[i * rows : (i + 1) * rows] = blocks[k][...]
    dk_ref[...] = jnp.zeros_like(dk_ref)
    dv_ref[...] = jnp.zeros_like(dv_ref)
    wide = pairs_at_once(n, rows, split)
    step = 2 * rows * wide // split

    @pl.loop(0, n // 2 // wide)
    def _(i):
        at = tile_rows(i, step)
        mask = (place_ref[...] >= low_ref[at]) & (place_ref[...] <= high_ref[at])
        d_all = dot_t(e_ref[at], wo_ref[...]).astype(LOW)
        dqs, dks, dvs = [], [], []
        for index, start in enumerate(range(0, own, head_width)):
            span = slice(start, start + head_width)
            q, k, v, d = q_ref[at, span], k_ref[:, span], v_ref[:, span], d_all[:, span]
            weights = jnp.where(mask, jnp.exp(dot_t(q, k) - lse_ref[at, index : index + 1]), 0.0)
            weight_grad = dot_t(d, v)
            delta = jnp.sum(weights * weight_grad, axis=1, keepdims=True)
            score_grad = (weights * (weight_grad - delta)).astype(LOW)
            dqs.append(dot(score_grad, k))
            dks.append(t_dot(score_grad, q))
            dvs.append(t_dot(weights.astype(LOW), d))
        dq = jnp.concatenate(dqs, axis=1).astype(LOW).astype(F32) * 0.125
        dq_ref[at] = dq.astype(LOW)
        dk_ref[...] += jnp.concatenate(dks, axis=1)
        dv_ref[...] += jnp.concatenate(dvs, axis=1)

    dkv_ref[:, :own] = dk_ref[...].astype(LOW)
    dkv_ref[:, own:] = dv_ref[...].astype(LOW)
    if split > 1:
        return

    @pl.loop(0, n // 2 // wide)
    def _(i):
        at = tile_rows(i, step)
        put_slots(
            even_ref, odd_ref, i * wide, dot_t(dq_ref[at], w_ref[:, :own]) + dot_t(dkv_ref[at], w_ref[:, own : 3 * own])
        )


def place_ffn_kernel(n, m, layers, *refs):
    up_ref, down_ref, up_out, down_out, fc1_out = refs
    piece = fc1_out.shape[1]
    for layer in range(layers):
        down_out[layer] = down_ref[layer, :piece].astype(F32)
        fc1_out[layer : layer + 1] = down_ref[layer, piece : piece + 16, :piece].astype(F32)[:1]
        for device in range(n):
            high, low = device // m, device % m
            for j in range(m):
                at = (n * j + m * high + (j + low) % m) * piece
                start = (layer * m + j) * piece
                block = up_ref[device, :, start : start + piece]
                up_out[layer, :, at : at + piece] = block.astype(F32)


def place_attention_kernel(n, layers, *refs):
    late, both, outs = refs[0], refs[1 : layers + 1], refs[layers + 1 :]
    qkv_out, o_out, q_out, kv_out, cross_out = outs
    col = both[0].shape[1] // 8
    rows = both[0].shape[0] // n
    for layer in range(layers):
        for i in range(n):
            for part in range(5):
                out, at = (kv_out, part) if part < 2 else (qkv_out, part - 2)
                start = (5 * layer + part) * col
                block = late[i, :, start : start + col]
                out[layer, :, (at * n + i) * col : (at * n + i + 1) * col] = block.astype(F32)
            for out, part in ((q_out, 5), (cross_out, 6), (o_out, 7)):
                block = both[layer][i * rows : (i + 1) * rows, part * col : (part + 1) * col]
                out[layer, :, i * col : (i + 1) * col] = block.astype(F32)


def last_backward_kernel(terms, *refs):
    dx1_ref, refs = refs[0], refs[1:]
    term_refs, refs = refs[:terms], refs[terms:]
    x_ref, vec_ref, dx_ref, e_ref, sum_ref = refs
    back, gain, shift = layer_norm_back(
        x_ref[...].astype(F32), vec_ref[0:1], total_of([t[...] for t in term_refs])
    )
    dx = dx1_ref[...] + back
    dx_ref[...] = dx
    e_ref[...] = dx.astype(LOW)
    sum_ref[...] = jnp.concatenate([gain, shift], axis=0)


def stored_positions(row_index, row_count, dev_count):
    device = row_index // row_count
    offset = row_index % row_count
    half_rows = row_count // 2
    return jnp.where(
        offset < half_rows,
        device * half_rows + offset,
        (2 * dev_count - 1 - device) * half_rows + offset - half_rows,
    )


def ranges_of(starts, length):
    return starts, jnp.concatenate([starts[1:], jnp.full((1,), length, jnp.int32)]) - 1


def group_of(places, starts):
    return jnp.sum((starts[None, :] <= places[:, None]).astype(jnp.int32), axis=1) - 1


def pick(table, index):
    slots = jnp.arange(table.shape[0], dtype=jnp.int32)
    return jnp.sum(jnp.where(index[:, None] == slots[None, :], table[None, :], 0), axis=1)


def on_device(
    tokens,
    encoder_states,
    grad_out,
    doc_starts,
    source_doc,
    source_offsets,
    self_qkv,
    self_out,
    cross_q,
    cross_kv,
    cross_out,
    ffn_in,
    ffn_out,
    norm_gains,
    vec_biases,
    fc1_bias,
):
    n, m = lax.axis_size("ctx"), lax.axis_size("fsdp")
    c, f = lax.axis_index("ctx"), lax.axis_index("fsdp")
    layers = self_qkv.shape[0]
    rows, width = tokens.shape[1:]
    source_rows = encoder_states.shape[1]
    length, source_length = n * rows, n * source_rows
    held = self_out.shape[1]
    hidden = ffn_out.shape[1] * m
    head_width = width // HEADS
    groups = min(n, HEADS)
    split = n // groups
    group, part = c // split, c % split
    own = width // groups
    col = width // n
    piece = hidden // (n * m)
    units = m * piece
    high_c, low_c = c // m, c % m
    here = jnp.stack([c, f]).astype(jnp.int32)
    queries = length // split
    packs = split == 1 and col % 128 == 0 and units == width and piece == held

    slot_rows = ((c ^ jnp.arange(n, dtype=jnp.int32)) * rows)[:, None] + jnp.arange(
        rows, dtype=jnp.int32
    )[None, :]
    places = stored_positions(slot_rows.reshape(-1), rows, n)
    own_places = places.reshape(n // split, split, rows)[:, 0].reshape(-1)
    doc_low, doc_high = ranges_of(doc_starts[0], length)
    self_bounds = [
        pick(doc_low, group_of(own_places, doc_starts[0]))[:, None],
        own_places[:, None],
        places[None, :],
    ]
    source_low, source_high = ranges_of(source_offsets[0], source_length)
    read_doc = pick(source_doc[0], group_of(places[:rows], doc_starts[0]))
    cross_bounds = [
        pick(source_low, read_doc)[:, None],
        pick(source_high, read_doc)[:, None],
        jnp.arange(source_length, dtype=jnp.int32)[None, :],
    ]

    def fetch_out():
        start = group * own
        got = lax.dynamic_slice(self_out, (0, start % held, 0), (layers, own, width))
        got = jnp.where(f == start // held, got, jnp.zeros_like(got))
        covered = [{(device // split) * own // held} for device in range(n)]
        while any(len(planes) < m for planes in covered):
            pairs = []
            for device, planes in enumerate(covered):
                reached = set()
                for plane in sorted(planes):
                    free = [p for p in (plane + 1, plane - 1) if 0 <= p < m and p not in planes | reached]
                    if free:
                        reached.add(free[0])
                        pairs.append((device * m + plane, device * m + free[0]))
                planes |= reached
            got = got + lax.ppermute(got, ("ctx", "fsdp"), pairs)
        return got

    def columns(array, layer, start, count):
        return lax.dynamic_slice(array, (layer, 0, start), (1, array.shape[1], count))[0]

    first_rows = jnp.concatenate([tokens[0], encoder_states[0]])
    first_slots = gather_slots(first_rows)
    unit_start = (m * high_c + (f + low_c) % m) * piece
    last_slots = gather_slots(after(grad_out[0], first_slots))
    vec_rows = jnp.concatenate([norm_gains, vec_biases], axis=1)
    fc1_rows = lax.dynamic_slice(fc1_bias, (0, unit_start), (layers, piece))
    fc1_rows = jnp.pad(fc1_rows, ((0, 0), (0, held - piece)))
    vec_rows = jnp.concatenate([vec_rows.reshape(-1, held), fc1_rows])
    if packs:
        arrays = dict(qkv=self_qkv, kv=cross_kv, q=cross_q, out=cross_out, up=ffn_in, down=ffn_out)
        arrays["self_out"] = self_out
        arrays["vec"] = jnp.pad(vec_rows.T, ((0, 0), (0, 128 - vec_rows.shape[0])))
        first_size = (7 + layers) * col
        sizes = {
            "first": (held, first_size + 128),
            "attention": (held, 7 * col),
            "ffn": (held + piece, units),
        }

        def pack(jobs, wait=()):
            fed = [arrays[name] for kind, layer in jobs for name in FED[kind]]
            return call(
                partial(pack_kernel, m, n, jobs),
                [here] + fed,
                [like(sizes[kind], LOW) for kind, layer in jobs],
                0,
                scratch=[pltpu.SemaphoreType.DMA((8 * len(jobs) + 8,))],
                smem=1,
                far=len(fed),
                wait=wait,
            )

        packed = pack([("first", 0)])
        packed += pack([("ffn", 0)], [first_slots[-1], last_slots[-1]])
        for layer in range(1, layers):
            packed += pack([("attention", layer), ("ffn", layer)])
        got = []
        for index, operand in enumerate(packed):
            if index > 1:
                operand = after(operand, got[index - 2])
            tiled = operand.shape[0] == held
            got.append(lax.all_gather(operand, "fsdp", axis=0, tiled=tiled))
        w_qkv = w_rest = got[0::2]
        w_ffn = [[both] for both in got[1::2]]
        skip = [3 * col] * layers
        ordered = got[0][:, first_size : first_size + vec_rows.shape[0]].T.astype(F32)
        w_out = got[0][:, 7 * col : first_size].reshape(n, col, layers, col)
        w_out = lax.all_to_all(w_out, "ctx", 0, 0).transpose(2, 1, 0, 3).reshape(layers, col, width)
    else:
        w_out = fetch_out()
        ordered = gather_planes(vec_rows.T).T.astype(F32)
        w_qkv, w_rest, w_ffn, skip = [], [], [], [0] * layers
        for layer in range(layers):
            blocks = [columns(self_qkv, layer, i * width + group * own, own) for i in range(3)]
            w_qkv.append(gather_planes(jnp.concatenate(blocks, axis=1)))
            blocks = [columns(cross_kv, layer, i * width + c * col, col) for i in range(2)]
            blocks += [columns(cross_q, layer, c * col, col), columns(cross_out, layer, c * col, col)]
            w_rest.append(gather_planes(jnp.concatenate(blocks, axis=1)))
            blocks = [
                columns(ffn_in, layer, (n * j + m * high_c + (j + low_c) % m) * piece, piece)
                for j in range(m)
            ]
            down = lax.dynamic_slice(ffn_out, (layer, unit_start, 0), (1, piece, width))[0]
            w_ffn.append([gather_planes(jnp.concatenate(blocks, axis=1)), gather_planes(down)])
    vectors = ordered[:-layers].reshape(layers, -1, width)
    up_bias = ordered[-layers:].reshape(layers, m, held)[:, :, :piece].reshape(layers, units)
    w_sems = pltpu.SemaphoreType.DMA((2 * m,))
    w_scratch = [pltpu.VMEM((width, units), LOW), pltpu.VMEM((units, width), LOW), w_sems]
    qv_bias = lax.dynamic_slice(vectors, (0, 6, group * own), (layers, 2, own))
    ev_bias = lax.dynamic_slice(vectors, (0, 10, c * col), (layers, 1, col))
    ev_bias = jnp.pad(ev_bias, ((0, 0), (0, 0), (col, 0)))

    def own_slots(values):
        if split == 1:
            return values
        shaped = values.reshape((n // split, split, rows) + values.shape[1:])
        return shaped[:, 0].reshape((-1,) + values.shape[1:])

    def share(parts):
        if split == 1:
            return parts[0]
        total = lax.dynamic_index_in_dim(parts, part, 0, False).astype(F32)
        for other in range(1, split):
            term = lax.dynamic_index_in_dim(parts, part ^ other, 0, False)
            total = total + swap(term, other).astype(F32)
        return total

    def half_slots(width_of, kind=LOW):
        return [like((n // 2, rows, width_of), kind)] * 2

    (encoder_all,) = call(
        partial(assemble_kernel, n, rows),
        [here] + first_slots,
        [like((source_length, width), LOW)],
        0,
        smem=1,
    )

    def prepare(layer, wait=()):
        return call(
            partial(cross_prepare_kernel, col, skip[layer]),
            [w_rest[layer], encoder_all, ev_bias[layer]],
            [like((2 * col, width + source_length), LOW)],
            4 * source_length * width * col,
            wait=wait,
        )[0]

    x = tokens[0]
    h1_slots = first_slots
    kept = []
    matmul = 2 * length * width
    for layer in range(layers):
        vec = vectors[layer]
        w_t = after(prepared if layer else prepare(0, packed[2:] if packs else ()), h1_slots)
        near = gather_near(w_t)
        joined = layer > 0
        h1_all, q, k, v, a, self_lse, *parts = call(
            partial(self_forward_kernel, n, rows, split, layer == 0, joined, head_width),
            h1_slots
            + [vec, after(qv_bias[layer], w_t), w_qkv[layer]]
            + self_bounds
            + [w_out[layer]] * joined,
            [like((length, width), LOW), like((queries, own), LOW)]
            + [like((length, own), LOW)] * 2
            + [like((queries, own), LOW), like((queries, own // head_width), F32)]
            + half_slots(width) * joined,
            matmul * 4 * own + 4 * queries * length * own,
            steps=int(packs),
            tiles={n + 2: ((width, 3 * own), None)} if packs else None,
        )
        if not joined:
            parts = call(
                partial(self_out_kernel, n, rows, split),
                [a, w_out[layer]],
                half_slots(width),
                matmul * own,
            )
        even, odd = parts
        near, odd = lax.optimization_barrier((near, odd))
        terms = reduce_slots(even, odd)
        w_slots, where = gather_joined(w_t, near)
        x1, x2, h2, cq, mixed, cross_lse, h3, wq_t, wo_t, ek_t, ev_t = call(
            partial(mid_forward_kernel, n, len(terms), len(w_slots), where, head_width),
            [here, x] + terms + w_slots + [vec] + cross_bounds,
            [like((rows, width), F32)] * 2
            + [like((rows, width), LOW)] * 3
            + [like((rows, HEADS), F32), like((rows, width), LOW)]
            + [like((width, width), LOW)] * 2
            + [like((width, source_length), LOW)] * 2,
            4 * rows * width * (width + source_length),
            smem=1,
        )
        h3_slots = gather_slots(h3)
        weight_count = len(w_ffn[layer])
        first = n + 1 + weight_count
        tile = 4 * rows
        g, slope, even, odd = call(
            partial(ffn_forward_kernel, n, weight_count),
            h3_slots + [up_bias[layer][None]] + w_ffn[layer],
            [like((length, units), LOW)] * 2 + half_slots(width),
            2 * matmul * units,
            scratch=[pltpu.VMEM((length, width), LOW)] + w_scratch,
            far=weight_count,
            steps=n // 4,
            tiles={first + i: ((tile, units), 0) for i in range(2)}
            | {first + 2 + i: ((2, rows, width), 0) for i in range(2)},
        )
        last = layer == layers - 1
        if last:
            result_parts = (even, odd)
        else:
            terms = reduce_slots(even, odd)
        kept.append(
            (x, x1, x2, h1_all, q, k, v, a, self_lse, h2, cq, mixed, cross_lse)
            + (h3_slots, g, slope, wq_t, wo_t, ek_t, ev_t)
        )
        if last:
            continue
        prepared = prepare(layer + 1)
        outs = call(
            partial(between_kernel, len(terms), False),
            [x2] + terms + [vec, vectors[layer + 1]],
            [like((rows, width), F32), like((rows, width), LOW)],
            rows * width * 20,
        )
        x = outs[0]
        h1_slots = gather_slots(outs[1])

    r = width // (n * m)
    grad_x, e3_slots = grad_out[0], last_slots
    enc_total = jnp.zeros((source_length, width), F32)
    vec_sums = [None] * layers
    moves = [
        (i * m + p, ((n // m) * ((p - i % m) % m) + i // m) * m + p) for i in range(n) for p in range(m)
    ]

    def to_rows(summed):
        return lax.all_to_all(summed.reshape(n, r, summed.shape[1]), "ctx", 0, 0)

    finish = []
    for layer in reversed(range(layers)):
        x, x1, x2, h1_all, q, k, v, a, self_lse, h2, cq, mixed, cross_lse = kept[layer][:13]
        h3_slots, g, slope, wq_t, wo_t, ek_t, ev_t = kept[layer][13:]
        vec = vectors[layer]
        if finish:
            slope = after(slope, cross_grad)
        weight_count = len(w_ffn[layer])
        first = n + 1 + weight_count
        tile = 4 * rows
        du, fc1_grad, even, odd = call(
            partial(ffn_backward_kernel, n, weight_count),
            e3_slots + [slope] + w_ffn[layer],
            [like((length, units), LOW), like((1, units), F32)] + half_slots(width),
            2 * matmul * units,
            scratch=[pltpu.VMEM((length, width), LOW)] + w_scratch,
            far=weight_count,
            steps=n // 4,
            tiles={n: ((tile, units), 0), first: ((tile, units), 0)}
            | {first + 2 + i: ((2, rows, width), 0) for i in range(2)},
        )
        terms = reduce_slots(even, odd)
        shapes = [like((m, n * r, units), LOW), like((m, piece + 16, width), LOW)]
        if units == width:
            shapes = [like((m, n * r + piece + 16, width), LOW)]
        ffn_grads = call(
            partial(ffn_weights_kernel, n, m),
            [here, after(du, terms[0]), g, fc1_grad] + h3_slots + e3_slots,
            shapes,
            2 * matmul * units,
            scratch=[pltpu.VMEM((length, width), LOW)] * 2,
            smem=1,
        )
        x1 = after(x1, ffn_grads)
        if layer == 0:
            result_terms = reduce_slots(*result_parts)
        dx1, e1, e2, dcq, even, odd, sums = call(
            partial(mid_backward_kernel, n, len(terms), head_width),
            [here, grad_x]
            + terms
            + [x1, x2, vec, wq_t, wo_t, ek_t, ev_t, cq, cross_lse]
            + cross_bounds,
            [like((rows, width), F32)]
            + [like((rows, width), LOW)] * 3
            + [like((n // 2, 2 * col, source_length), LOW)] * 2
            + [like((8, width), F32)],
            4 * rows * width * width + 10 * rows * source_length * width,
            scratch=[pltpu.VMEM((width, source_length), LOW)] * 2,
            smem=1,
        )
        ffn_sums = [reduce_planes(grad) for grad in after(ffn_grads, dx1 if layer else terms)]
        e1_slots = gather_slots(e1)
        kv_parts = [even, odd]
        even, *odd = call(
            partial(cross_weights_kernel, n),
            [here, h2, dcq, mixed, e2] + kv_parts,
            [like((n // size, 2 * col, width + source_length), LOW) for size in (2, 4, 4)],
            4 * rows * width * width,
            scratch=[pltpu.VMEM((width, width), LOW)] * 2,
            smem=1,
            wait=[entry[2] for entry in finish[-1:]] + ([] if layer else result_terms[1:]),
        )
        w_terms = reduce_slots(even, list(odd), hold=e1_slots)
        e1_own, dq, dkv, even, odd = call(
            partial(self_backward_kernel, n, split, head_width),
            e1_slots + [w_out[layer], w_qkv[layer], after(q, w_terms[0]), k, v, self_lse] + self_bounds,
            [like((queries, width), LOW), like((queries, own), LOW), like((length, 2 * own), LOW)]
            + half_slots(width),
            matmul * 4 * own + 10 * queries * length * own,
            scratch=[pltpu.VMEM((length, own), F32)] * 2,
            steps=int(packs),
            tiles={n + 1: ((width, 3 * own), None)} if packs else None,
        )
        if split > 1:
            shaped = dkv.reshape(n // split, split, rows, 2 * own)
            total = shaped[:, 0].astype(F32)
            for other in range(1, split):
                total = total + swap(shaped[:, other], other).astype(F32)
            dkv = total.astype(LOW).reshape(-1, 2 * own)
            even = dot_t(jnp.concatenate([dq, dkv], axis=1), w_qkv[layer][:, : 3 * own])
            even = even.reshape(n // 2, rows, width)
            odd = jnp.zeros_like(even)
        terms = reduce_slots(even, after(odd, w_terms))
        before = []
        if layer == 0:
            sums_of = [ffn_sums] + [done[1] for done in reversed(finish)]
            up_rows = to_rows(jnp.concatenate([sums[0][: n * r] for sums in sums_of], axis=1))
            down_rows = [sums[0][n * r :] if units == width else sums[1] for sums in sums_of]
            down_rows = lax.ppermute(jnp.stack(down_rows), ("ctx", "fsdp"), moves)
            before = [up_rows, down_rows]
            *ffn_grads, fc1_own = call(
                partial(place_ffn_kernel, n, m, layers),
                [up_rows, down_rows],
                [like((layers, r, hidden), F32), like((layers, piece, width), F32), like((layers, piece), F32)],
                layers * r * hidden,
            )
        grad_x, e3, last_sums = call(
            partial(last_backward_kernel, len(terms)),
            [dx1] + terms + [x, vec],
            [like((rows, width), F32), like((rows, width), LOW), like((2, width), F32)],
            rows * width * 20,
            wait=before,
        )

        e3_slots = gather_slots(e3) if layer else None
        hold = (e3_slots[2], e3_slots[4]) if layer else terms[0]
        own_parts = [h1_all, dq, dkv, a, e1_own] if split == 1 else []
        cross_grad, enc_total, ev_sum, *enc_parts = call(
            partial(attention_weights_kernel, n, m, skip[layer], len(terms), split == 1),
            [here]
            + w_terms
            + own_parts
            + [encoder_all, w_rest[layer], after(enc_total, hold)],
            [like((m, n * r, (8 if split == 1 else 4) * col), LOW)]
            + [like((source_length, width), F32), like((2 * col, 1), F32)]
            + [like((n // 2, source_rows, width), F32)] * 2,
            8 * source_length * col * width + matmul * 4 * own,
            smem=1,
            wait=ffn_sums,
        )
        if split > 1:
            qkv_grad = t_dot(own_slots(h1_all), jnp.concatenate([dq, dkv], axis=1)).astype(LOW)
            qkv_grad = share(qkv_grad.reshape(width, 3, split, col).transpose(2, 0, 1, 3))
            qkv_grad = qkv_grad.astype(LOW).reshape(n, m, r, 3 * col).transpose(1, 0, 2, 3)
            o_grad = share(t_dot(a, e1_own).astype(LOW).reshape(split, own // split, width))
            o_grad = o_grad.astype(LOW).reshape(m, r, n, col).transpose(0, 2, 1, 3)
            kv_q = jnp.split(cross_grad, [2 * col], axis=2)
            self_grad = jnp.concatenate([qkv_grad, o_grad], axis=3).reshape(m, n * r, 4 * col)
            parts = [kv_q[0], self_grad[:, :, : 3 * col], kv_q[1], self_grad[:, :, 3 * col :]]
            cross_grad = jnp.concatenate(parts, axis=2)
        both_sum = reduce_planes(cross_grad)
        finish.append((layer, ffn_sums, both_sum))
        zero = jnp.zeros((1, width), F32)
        summed = jnp.concatenate(
            [last_sums[0:1], sums[0:2], last_sums[1:2], sums[2:4], zero, zero]
            + [sums[4:6], zero, sums[6:8]]
        )
        owned_q = share(row_sum(dq).reshape(split, col))
        owned_v = share(row_sum(dkv[:, own:]).reshape(split, col))
        blank = jnp.zeros((col,), F32)
        owned = [blank] * 6 + [owned_q, owned_v, blank, blank, ev_sum[col:, 0], blank, blank]
        vec_sums[layer] = (summed, jnp.stack(owned))

    finish.sort(key=lambda entry: entry[0])
    (result,) = call(
        partial(between_kernel, len(result_terms), True),
        [kept[-1][2]] + result_terms + [vectors[-1]],
        [like((rows, width), LOW)],
        rows * width * 20,
    )
    summed = jnp.concatenate([pair[0] for pair in vec_sums])
    owned = jnp.concatenate([pair[1] for pair in vec_sums])
    enc_grad = total_of(reduce_slots(*enc_parts, F32))
    summed = turn(summed, 1).reshape(-1, n, col).transpose(1, 0, 2)
    vec = total_of(reduce_slots(summed[0::2], summed[1::2], F32)) + owned
    (late,) = call(
        late_kernel,
        [entry[2] for entry in finish],
        [like((n * r, layers * 5 * col), LOW)],
        0,
        wait=[up_rows, down_rows],
    )
    late_rows = to_rows(late)
    (vec,) = call(copy_kernel, [vec], [like(vec.shape, F32)], 0, wait=[late])
    attention_grads = call(
        partial(place_attention_kernel, n, layers),
        [late_rows] + [entry[2] for entry in finish],
        [like((layers, r, parts * width), F32) for parts in (3, 1, 1, 2, 1)],
        layers * r * 8 * width,
    )
    vec = sum_planes(vec.reshape(-1, m, col // m).transpose(1, 0, 2))
    vec = vec.reshape(layers, -1, col // m)
    return (
        (result[None], grad_x[None], enc_grad[None])
        + tuple(attention_grads)
        + tuple(ffn_grads)
        + (vec[:, :3], vec[:, 3:], fc1_own)
    )


def solution(mesh):
    tokens = P("fsdp", "ctx", None)
    per_stream = P("fsdp", None)
    weight = P(None, "fsdp", None)
    vector = P(None, None, "fsdp")
    grad = P(None, ("ctx", "fsdp"), None)
    vector_grad = P(None, None, ("ctx", "fsdp"))
    return jax.shard_map(
        on_device,
        mesh=mesh,
        in_specs=(tokens,) * 3 + (per_stream,) * 3 + (weight,) * 7 + (vector,) * 2 + (P(None, "fsdp"),),
        out_specs=(tokens,) * 3 + (grad,) * 7 + (vector_grad,) * 2 + (P(None, ("ctx", "fsdp")),),
        check_vma=False,
    )
```

```python
from functools import partial

import jax
import jax.numpy as jnp
from jax import lax
from jax.experimental import pallas as pl
from jax.experimental.pallas import tpu as pltpu
from jax.sharding import PartitionSpec as P

HEADS = 16
EPSILON = 1e-05
NEGATIVE = -1e30
F32 = jnp.float32
LOW = jnp.bfloat16
VMEM = pl.BlockSpec(memory_space=pltpu.VMEM)
SMEM = pl.BlockSpec(memory_space=pltpu.SMEM)
FAR = pl.BlockSpec(memory_space=pl.ANY)
VMEM_BYTES = 60 * 2**20


def swap(values, bits):
    count = lax.axis_size("ctx")
    return lax.ppermute(values, "ctx", [(i, i ^ bits) for i in range(count)])


def gather_near(rows):
    if lax.axis_size("ctx") == 8:
        return swap(rows, 2), swap(rows, 4)
    return ()


def gather_slots(rows, near=None):
    count = lax.axis_size("ctx")
    if count == 8:
        near_x, near_y = near or gather_near(rows)
        half = rows.shape[0] // 2
        far = jnp.concatenate([swap(near_x[:half], 4), swap(near_y[half:], 2)])
        blocks = []
        for block in (rows, near_x, near_y, far):
            blocks += [block, swap(block, 1)]
        return blocks
    blocks = [rows]
    bit = 1
    while bit < count:
        blocks = blocks + [swap(block, bit) for block in blocks]
        bit *= 2
    return blocks


def gather_joined(rows, near):
    count = lax.axis_size("ctx")
    size = rows.shape[0]
    if count == 8:
        half = size // 2
        joined = swap(jnp.concatenate([rows, *near]), 1)
        far = jnp.concatenate([swap(near[0][:half], 4), swap(near[1][half:], 2)])
        arrays = [rows, *near, far, joined, swap(far, 1)]
        where = [(0, 0), (4, 0), (1, 0), (4, size), (2, 0), (4, 2 * size), (3, 0), (5, 0)]
        return arrays, where
    return gather_slots(rows), [(k, 0) for k in range(count)]


def reduce_slots(even, odd, kind=LOW, hold=None):
    count = lax.axis_size("ctx")
    odd = [swap(block.astype(kind), 1) for block in (odd if isinstance(odd, list) else [odd])]
    if count == 8:
        size = odd[0].shape[0]
        chip = [even[i].astype(F32) + odd[i // size][i % size].astype(F32) for i in range(4)]
        sent = [chip[i].astype(kind) for i in (1, 2, 3)]
        if hold is not None:
            sent = after(sent, hold)
        return [chip[0]] + [swap(sent[i], 2 * i + 2) for i in range(3)]
    chip = even.astype(F32) + jnp.concatenate(odd).astype(F32)
    bit = count // 4
    while bit:
        chip = chip[:bit] + swap(chip[bit : 2 * bit].astype(kind), 2 * bit).astype(F32)
        bit //= 2
    return [chip[0]]


def total_of(terms):
    total = terms[0].astype(F32)
    for term in terms[1:]:
        total = total + term.astype(F32)
    return total


def turn(values, axis):
    count = lax.axis_size("ctx")
    here = lax.axis_index("ctx")
    width = values.shape[axis] // count
    return jnp.concatenate(
        [
            lax.dynamic_slice_in_dim(values, (here ^ k) * width, width, axis)
            for k in range(count)
        ],
        axis=axis,
    )


def sum_planes(parts):
    count = lax.axis_size("fsdp")
    here = lax.axis_index("fsdp")
    total = lax.dynamic_index_in_dim(parts, here, 0, False)
    for step in range(1, count):
        term = lax.dynamic_index_in_dim(parts, (here + step) % count, 0, False)
        total = total + lax.ppermute(term, "fsdp", [(i, (i + step) % count) for i in range(count)])
    return total


def after(values, other):
    return lax.optimization_barrier((values, other))[0]


def gather_planes(values):
    return lax.all_gather(values, "fsdp", axis=0, tiled=True)


def reduce_planes(parts):
    return lax.psum_scatter(parts, "fsdp", scatter_dimension=0, tiled=False)


def layer_norm(values, gain_row, offset_row):
    center = values - jnp.mean(values, axis=-1, keepdims=True)
    spread = jnp.mean(center * center, axis=-1, keepdims=True)
    return center * lax.rsqrt(spread + EPSILON) * gain_row + offset_row


def layer_norm_back(values, gain_row, grad):
    center = values - jnp.mean(values, axis=-1, keepdims=True)
    inverse = lax.rsqrt(jnp.mean(center * center, axis=-1, keepdims=True) + EPSILON)
    normed = center * inverse
    scaled = grad * gain_row
    back = inverse * (
        scaled
        - jnp.mean(scaled, axis=-1, keepdims=True)
        - normed * jnp.mean(scaled * normed, axis=-1, keepdims=True)
    )
    return back, row_sum(grad * normed), row_sum(grad)


def row_sum(values):
    return jnp.sum(values.astype(F32), axis=0, keepdims=True)


def dot(left, right):
    return jnp.dot(left, right, preferred_element_type=F32)


def dot_t(left, right):
    return lax.dot_general(left, right, (((1,), (1,)), ((), ())), preferred_element_type=F32)


def t_dot(left, right):
    return lax.dot_general(left, right, (((0,), (0,)), ((), ())), preferred_element_type=F32)


def call(kernel, ins, outs, flops, scratch=(), smem=0, far=0, wait=(), steps=0, tiles=None):
    count, extra = len(ins), len(wait)

    def spec(index, array):
        if not steps and not (tiles and index in tiles):
            return VMEM
        block, axis = (tiles or {}).get(index, (array.shape, None))
        dims = len(block)
        if not steps:
            return pl.BlockSpec(block, lambda: (0,) * dims)
        return pl.BlockSpec(block, lambda i: tuple(i if d == axis else 0 for d in range(dims)))

    def body(*refs):
        kernel(*refs[:count], *refs[count + extra :])

    moved = sum(a.size * a.dtype.itemsize for a in ins)
    moved += sum(a.size * a.dtype.itemsize for a in outs)
    return pl.pallas_call(
        body,
        grid=(steps,) if steps else (),
        in_specs=[SMEM] * smem
        + [spec(i, ins[i]) for i in range(smem, count - far)]
        + [FAR] * (far + extra),
        out_specs=[spec(count + i, array) for i, array in enumerate(outs)],
        out_shape=outs,
        scratch_shapes=list(scratch),
        compiler_params=pltpu.CompilerParams(vmem_limit_bytes=VMEM_BYTES),
        cost_estimate=pl.CostEstimate(flops=int(flops), bytes_accessed=int(moved), transcendentals=0),
    )(*ins, *wait)


def like(shape, kind):
    return jax.ShapeDtypeStruct(tuple(shape), kind)


def tile_rows(rows, size):
    return pl.ds(pl.multiple_of(rows * size, size), size)


def join_rows(blocks, out_ref):
    rows = blocks[0].shape[0]
    for k, block in enumerate(blocks):
        out_ref[k * rows : (k + 1) * rows] = block[...]


def put_slots(even_ref, odd_ref, index, values):
    rows = even_ref.shape[1]
    for i in range(values.shape[0] // (2 * rows)):
        even_ref[index + i] = values[2 * i * rows : (2 * i + 1) * rows].astype(LOW)
        odd_ref[index + i] = values[(2 * i + 1) * rows : (2 * i + 2) * rows].astype(LOW)


def pairs_at_once(n, rows, split):
    return 2 if split == 1 and n % 4 == 0 and n * rows <= 1024 else 1


def self_forward_kernel(n, rows, split, raw, joined, head_width, *refs):
    blocks, refs = refs[:n], refs[n:]
    vec_ref, bias_ref, w_ref, low_ref, high_ref, place_ref = refs[:6]
    (wo_ref, *refs) = refs[6:] if joined else (None, *refs[6:])
    h_ref, q_ref, k_ref, v_ref, a_ref, lse_ref, *out_refs = refs
    own = k_ref.shape[1]
    for k in range(n):
        block = blocks[k][:rows]
        if raw:
            block = layer_norm(block.astype(F32), vec_ref[0:1], vec_ref[3:4]).astype(LOW)
        h_ref[k * rows : (k + 1) * rows] = block

    @pl.loop(0, n // 2)
    def _(i):
        at = tile_rows(i, 2 * rows)
        z = dot(h_ref[at], w_ref[:, : 3 * own])
        q = ((z[:, :own] + bias_ref[0:1]) * 0.125).astype(LOW)
        if split == 1:
            q_ref[at] = q
        else:
            q_ref[tile_rows(i, rows)] = q[:rows]
        k_ref[at] = z[:, own : 2 * own].astype(LOW)
        v_ref[at] = (z[:, 2 * own :] + bias_ref[1:2]).astype(LOW)

    wide = pairs_at_once(n, rows, split)
    step = 2 * rows * wide // split

    @pl.loop(0, n // 2 // wide)
    def _(i):
        at = tile_rows(i, step)
        mask = (place_ref[...] >= low_ref[at]) & (place_ref[...] <= high_ref[at])
        outs, masses = [], []
        for start in range(0, own, head_width):
            span = slice(start, start + head_width)
            scores = jnp.where(mask, dot_t(q_ref[at, span], k_ref[:, span]), NEGATIVE)
            top = jnp.max(scores, axis=1, keepdims=True)
            raised = jnp.exp(scores - top)
            mass = jnp.sum(raised, axis=1, keepdims=True)
            outs.append(dot((raised * (1.0 / mass)).astype(LOW), v_ref[:, span]))
            masses.append(top + jnp.log(mass))
        a = jnp.concatenate(outs, axis=1).astype(LOW)
        a_ref[at] = a
        lse_ref[at] = jnp.concatenate(masses, axis=1)
        if joined:
            put_product(split, a, wo_ref, *out_refs, i * wide)


def put_product(split, a, wo_ref, even_ref, odd_ref, i):
    y = dot(a, wo_ref[...])
    if split > 1:
        y = jnp.concatenate([y, jnp.zeros_like(y)])
    put_slots(even_ref, odd_ref, i, y)


def self_out_kernel(n, rows, split, a_ref, wo_ref, even_ref, odd_ref):
    wide = pairs_at_once(n, rows, split)
    step = 2 * rows * wide // split

    @pl.loop(0, n // 2 // wide)
    def _(i):
        put_product(split, a_ref[tile_rows(i, step)], wo_ref, even_ref, odd_ref, i * wide)


def mid_forward_kernel(n, terms, arrays, where, head_width, here_ref, *refs):
    x_ref, refs = refs[0], refs[1:]
    term_refs, refs = refs[:terms], refs[terms:]
    w_refs, refs = refs[:arrays], refs[arrays:]
    vec_ref, low_ref, high_ref, place_ref = refs[:4]
    x1_ref, x2_ref, h2_ref, cq_ref, c_ref, lse_ref, h3_ref = refs[4:11]
    wq_ref, wo_ref, ek_ref, ev_ref = refs[11:]
    col = w_refs[0].shape[0] // 2
    width = wq_ref.shape[1]
    here = here_ref[0]
    for k in range(n):
        at = tile_rows(here ^ k, col)
        array, first = where[k]
        top, bottom = pl.ds(first, col), pl.ds(first + col, col)
        wq_ref[at] = w_refs[array][top, :width]
        wo_ref[at] = w_refs[array][bottom, :width]
        ek_ref[at] = w_refs[array][top, width:]
        ev_ref[at] = w_refs[array][bottom, width:]
    x1 = x_ref[...].astype(F32) + total_of([t[...] for t in term_refs]) + vec_ref[8:9]
    x1_ref[...] = x1
    h2 = layer_norm(x1, vec_ref[1:2], vec_ref[4:5]).astype(LOW)
    h2_ref[...] = h2
    cq_ref[...] = ((dot_t(h2, wq_ref[...]) + vec_ref[9:10]) * 0.125).astype(LOW)
    mask = (place_ref[...] >= low_ref[...]) & (place_ref[...] <= high_ref[...])
    outs, masses = [], []
    for start in range(0, cq_ref.shape[1], head_width):
        span = slice(start, start + head_width)
        scores = jnp.where(mask, dot(cq_ref[:, span], ek_ref[span]), NEGATIVE)
        top = jnp.max(scores, axis=1, keepdims=True)
        raised = jnp.exp(scores - top)
        mass = jnp.sum(raised, axis=1, keepdims=True)
        outs.append(dot_t((raised * (1.0 / mass)).astype(LOW), ev_ref[span]))
        masses.append(top + jnp.log(mass))
    c_ref[...] = jnp.concatenate(outs, axis=1).astype(LOW)
    lse_ref[...] = jnp.concatenate(masses, axis=1)
    x2 = x1 + dot_t(c_ref[...], wo_ref[...]) + vec_ref[11:12]
    x2_ref[...] = x2
    h3_ref[...] = layer_norm(x2, vec_ref[2:3], vec_ref[5:6]).astype(LOW)


def copies_of(sources, up_ref, down_ref, sems):
    if len(sources) == 2:
        pairs = [(sources[0], up_ref), (sources[1], down_ref)]
    else:
        planes, both = sources[0].shape[:2]
        size = up_ref.shape[0] // planes
        pairs = []
        for j in range(planes):
            at = pl.ds(j * size, size)
            pairs.append((sources[0].at[j, pl.ds(0, size)], up_ref.at[at]))
            pairs.append((sources[0].at[j, pl.ds(size, size)], down_ref.at[at]))
    return [pltpu.make_async_copy(a, b, sems.at[i]) for i, (a, b) in enumerate(pairs)]


def ffn_forward_kernel(n, sources, *refs):
    blocks, refs = refs[:n], refs[n:]
    bias_ref, refs = refs[0], refs[1:]
    sources, refs = refs[:sources], refs[sources:]
    g_ref, slope_ref, even_ref, odd_ref, h_ref, up_ref, down_ref, sems = refs
    step = pl.program_id(0)

    @pl.when(step == 0)
    def _():
        copies = copies_of(sources, up_ref, down_ref, sems)
        for copy in copies:
            copy.start()
        join_rows(blocks, h_ref)
        for copy in copies:
            copy.wait()

    u = dot(h_ref[tile_rows(step, g_ref.shape[0])], up_ref[...]) + bias_ref[...]
    share = 0.5 + 0.5 * lax.erf(u * 0.7071067811865476)
    g = (u * share).astype(LOW)
    g_ref[...] = g
    slope_ref[...] = (share + u * (jnp.exp(-0.5 * u * u) * 0.3989422804014327)).astype(LOW)
    put_slots(even_ref, odd_ref, 0, dot(g, down_ref[...]))


def ffn_backward_kernel(n, sources, *refs):
    blocks, refs = refs[:n], refs[n:]
    slope_ref, refs = refs[0], refs[1:]
    sources, refs = refs[:sources], refs[sources:]
    du_ref, sum_ref, even_ref, odd_ref, e_ref, up_ref, down_ref, sems = refs
    step = pl.program_id(0)

    @pl.when(step == 0)
    def _():
        copies = copies_of(sources, up_ref, down_ref, sems)
        for copy in copies:
            copy.start()
        join_rows(blocks, e_ref)
        sum_ref[...] = jnp.zeros_like(sum_ref)
        for copy in copies:
            copy.wait()

    grad = dot_t(e_ref[tile_rows(step, du_ref.shape[0])], down_ref[...])
    du = (grad * slope_ref[...].astype(F32)).astype(LOW)
    du_ref[...] = du
    sum_ref[...] += row_sum(du)
    put_slots(even_ref, odd_ref, 0, dot_t(du, up_ref[...]))


def pack_kernel(m, n, jobs, where_ref, *refs):
    count = sum(len(FED[kind]) for kind, layer in jobs)
    sources, packed, sems = refs[:count], refs[count:-1], refs[-1]
    c, f = where_ref[0], where_ref[1]
    high, low = c // m, c % m
    copies = []

    def add(source, target):
        copies.append(pltpu.make_async_copy(source, target, sems.at[len(copies)]))

    def columns(start, size):
        return pl.ds(pl.multiple_of(start, 128), size)

    for (kind, layer), target in zip(jobs, packed):
        fed, sources = sources[: len(FED[kind])], sources[len(FED[kind]) :]
        at = 0
        if kind == "ffn":
            up, down = fed
            rows, piece = up.shape[1], down.shape[1] // n
            for j in range(m):
                start = (n * j + m * high + (j + low) % m) * piece
                add(up.at[layer, :, columns(start, piece)], target.at[pl.ds(0, rows), pl.ds(j * piece, piece)])
            start = (m * high + (f + low) % m) * piece
            add(down.at[layer, pl.ds(pl.multiple_of(start, piece), piece)], target.at[pl.ds(rows, piece)])
            continue
        for source, (name, parts) in zip(fed, FED[kind].items()):
            if parts == 0:
                add(source, target.at[:, pl.ds(at, source.shape[1])])
                continue
            width = source.shape[2] // parts
            col = width // n
            if name == "self_out":
                for l in range(source.shape[0]):
                    add(source.at[l, :, columns(c * col, col)], target.at[:, pl.ds(at, col)])
                    at += col
                continue
            for i in range(parts):
                add(source.at[layer, :, columns(i * width + c * col, col)], target.at[:, pl.ds(at, col)])
                at += col
    for copy in copies:
        copy.start()
    for copy in copies:
        copy.wait()


FED = {
    "first": {"qkv": 3, "kv": 2, "q": 1, "out": 1, "self_out": 1, "vec": 0},
    "attention": {"qkv": 3, "kv": 2, "q": 1, "out": 1},
    "ffn": {"up": 1, "down": 1},
}


def late_kernel(*refs):
    out_ref = refs[-1]
    size = out_ref.shape[1] // (len(refs) - 1)
    for layer, ref in enumerate(refs[:-1]):
        out_ref[:, layer * size : (layer + 1) * size] = ref[:, :size]


def copy_kernel(*refs):
    count = len(refs) // 2
    for in_ref, out_ref in zip(refs[:count], refs[count:]):
        out_ref[...] = in_ref[...]


def assemble_kernel(n, skip, here_ref, *refs):
    out_ref = refs[n]
    size = refs[0].shape[0] - skip
    for k in range(n):
        out_ref[tile_rows(here_ref[0] ^ k, size)] = refs[k][skip:]


def cross_prepare_kernel(col, skip, w_ref, enc_ref, bias_ref, out_ref):
    kv = dot(enc_ref[...], w_ref[:, skip : skip + 2 * col]) + bias_ref[...]
    width = w_ref.shape[0]
    out_ref[:, width:] = kv.T.astype(LOW)
    out_ref[:, :width] = w_ref[:, skip + 2 * col : skip + 4 * col].astype(F32).T.astype(LOW)


def between_kernel(terms, last, *refs):
    x2_ref, refs = refs[0], refs[1:]
    term_refs, refs = refs[:terms], refs[terms:]
    y = x2_ref[...] + total_of([t[...] for t in term_refs]) + refs[0][12:13]
    if last:
        refs[1][...] = y.astype(LOW)
    else:
        next_ref, y_ref, h_ref = refs[1:]
        y_ref[...] = y
        h_ref[...] = layer_norm(y, next_ref[0:1], next_ref[3:4]).astype(LOW)


def put_folded(out_ref, grad, at, n, m):
    size, width = grad.shape[0] // m, grad.shape[1] // n
    for p in range(m):
        for i in range(n):
            block = grad[p * size : (p + 1) * size, i * width : (i + 1) * width]
            out_ref[p, i * size : (i + 1) * size, at : at + width] = block


def attention_weights_kernel(n, m, skip, terms, full, first, last, here_ref, *refs):
    w_refs, refs = refs[:terms], refs[terms:]
    own_refs, refs = (refs[:5], refs[5:]) if full else ((), refs)
    enc_ref, w_kv_ref, *refs = refs
    before = 0.0 if first else refs.pop(0)[...]
    out_ref, total_ref, sum_ref, *halves = refs
    col = w_refs[0].shape[0] // 2
    width = w_kv_ref.shape[0]
    grad = total_of([t[:, :width] for t in w_refs]).astype(LOW)
    for i in range(2):
        at = (5 + i if full else 2 + i) * col
        put_folded(out_ref, grad[i * col : (i + 1) * col], at, n, m)
    dkv_t = total_of([t[:, width:] for t in w_refs])
    sum_ref[...] = jnp.sum(dkv_t.astype(LOW).astype(F32), axis=1, keepdims=True)
    dkv = dkv_t.T.astype(LOW)
    total_ref[...] = before + dot_t(dkv, w_kv_ref[:, skip : skip + 2 * col])
    put_by_rows(out_ref, t_dot(enc_ref[...], dkv).astype(LOW), 0, width, n, m)
    for k in range(n if last else 0):
        half = halves[k % 2]
        half[k // 2] = total_ref[tile_rows(here_ref[0] ^ k, half.shape[1])]
    if not full:
        return
    h_ref, dq_ref, dkv_ref, a_ref, e_ref = own_refs
    own = dq_ref.shape[1]
    step = min(256, width)
    for first in range(0, width, step):
        part = h_ref[:, first : first + step]
        grad = jnp.concatenate([t_dot(part, dq_ref[...]), t_dot(part, dkv_ref[...])], axis=1)
        put_by_rows(out_ref, grad.astype(LOW), first, width, n, m, 2 * own)
    put_folded(out_ref, t_dot(a_ref[...], e_ref[...]).astype(LOW), 7 * own, n, m)


def put_by_rows(out_ref, grad, first, total, n, m, at=0):
    size = total // (n * m)
    for i in range(grad.shape[0] // size):
        block = first // size + i
        device, plane = block // m, block % m
        part = grad[i * size : (i + 1) * size]
        out_ref[plane, device * size : (device + 1) * size, at : at + grad.shape[1]] = part


def ffn_weights_kernel(n, m, here_ref, du_ref, g_ref, sum_ref, *refs):
    h_blocks, e_blocks, outs = refs[:n], refs[n : 2 * n], refs[2 * n : -2]
    h_ref, e_ref = refs[-2:]
    up_ref, down_ref = outs if len(outs) == 2 else (outs[0], None)
    join_rows(h_blocks, h_ref)
    join_rows(e_blocks, e_ref)
    piece = g_ref.shape[1] // m
    low = here_ref[0] % m
    first = h_ref.shape[1] // m if down_ref is None else 0
    down_ref = up_ref if down_ref is None else down_ref
    for j in range(m):
        plane = (low + j) % m
        grad = t_dot(g_ref[:, j * piece : (j + 1) * piece], e_ref[...]).astype(LOW)
        down_ref[plane, first : first + piece] = grad
        part = jnp.broadcast_to(sum_ref[:, j * piece : (j + 1) * piece], (16, piece))
        top = lax.broadcasted_iota(jnp.int32, (16, piece), 0) == 0
        down_ref[plane, first + piece :] = jnp.zeros((16, down_ref.shape[2]), LOW)
        down_ref[plane, first + piece :, :piece] = jnp.where(top, part, 0.0).astype(LOW)
    step = min(256, h_ref.shape[1])
    for first in range(0, h_ref.shape[1], step):
        grad = t_dot(h_ref[:, first : first + step], du_ref[...]).astype(LOW)
        put_by_rows(up_ref, grad, first, h_ref.shape[1], n, m)


def mid_backward_kernel(n, terms, head_width, here_ref, *refs):
    dy_ref, refs = refs[0], refs[1:]
    term_refs, refs = refs[:terms], refs[terms:]
    x1_ref, x2_ref, vec_ref, wq_ref, wo_ref, ek_ref, ev_ref, cq_ref, lse_ref = refs[:9]
    low_ref, high_ref, place_ref = refs[9:12]
    dx1_ref, e1_ref, e2_ref, dcq_ref, even_ref, odd_ref, sum_ref = refs[12:19]
    dek_ref, dev_ref = refs[19:]
    col = even_ref.shape[1] // 2
    dy = dy_ref[...].astype(F32)
    back, gain_two, shift_two = layer_norm_back(
        x2_ref[...], vec_ref[2:3], total_of([t[...] for t in term_refs])
    )
    dx2 = dy + back
    e2 = dx2.astype(LOW)
    e2_ref[...] = e2
    d_all = dot(e2, wo_ref[...]).astype(LOW)
    mask = (place_ref[...] >= low_ref[...]) & (place_ref[...] <= high_ref[...])
    dqs = []
    for index, start in enumerate(range(0, cq_ref.shape[1], head_width)):
        span = slice(start, start + head_width)
        q, d, ek, ev = cq_ref[:, span], d_all[:, span], ek_ref[span], ev_ref[span]
        weights = jnp.where(mask, jnp.exp(dot(q, ek) - lse_ref[:, index : index + 1]), 0.0)
        weight_grad = dot(d, ev)
        delta = jnp.sum(weights * weight_grad, axis=1, keepdims=True)
        score_grad = (weights * (weight_grad - delta)).astype(LOW)
        dqs.append(dot_t(score_grad, ek))
        dek_ref[span] = t_dot(q, score_grad).astype(LOW)
        dev_ref[span] = t_dot(d, weights.astype(LOW)).astype(LOW)
    dcq = (jnp.concatenate(dqs, axis=1).astype(LOW).astype(F32) * 0.125).astype(LOW)
    dcq_ref[...] = dcq
    here = here_ref[0]
    for k in range(n):
        at = tile_rows(here ^ k, col)
        out = odd_ref if k % 2 else even_ref
        out[k // 2, :col] = dek_ref[at]
        out[k // 2, col:] = dev_ref[at]
    back, gain_one, shift_one = layer_norm_back(x1_ref[...], vec_ref[1:2], dot(dcq, wq_ref[...]))
    dx1 = dx2 + back
    dx1_ref[...] = dx1
    e1 = dx1.astype(LOW)
    e1_ref[...] = e1
    sums = [gain_one, gain_two, shift_one, shift_two]
    sums += [row_sum(e1), row_sum(dcq), row_sum(e2), row_sum(dy)]
    sum_ref[...] = jnp.concatenate(sums, axis=0)


def cross_weights_kernel(n, here_ref, h_ref, dcq_ref, c_ref, e_ref, kv_even, kv_odd, even_ref, *refs):
    odd_refs, (q_ref, o_ref) = refs[:2], refs[2:]
    col = even_ref.shape[1] // 2
    width = q_ref.shape[1]
    q_ref[...] = t_dot(h_ref[...], dcq_ref[...]).astype(LOW)
    o_ref[...] = t_dot(c_ref[...], e_ref[...]).astype(LOW)
    here = here_ref[0]
    for k in range(n):
        at = tile_rows(here ^ k, col)
        out, i = (odd_refs[2 * k // n], k // 2 % (n // 4)) if k % 2 else (even_ref, k // 2)
        out[i, :col, :width] = q_ref[at]
        out[i, col:, :width] = o_ref[at]
    even_ref[:, :, width:] = kv_even[...]
    for i in range(2):
        odd_refs[i][:, :, width:] = kv_odd[i * n // 4 : (i + 1) * n // 4]


def self_backward_kernel(n, split, head_width, *refs):
    blocks, refs = refs[:n], refs[n:]
    wo_ref, w_ref, q_ref, k_ref, v_ref, lse_ref, low_ref, high_ref, place_ref = refs[:9]
    e_ref, dq_ref, dkv_ref, even_ref, odd_ref, dk_ref, dv_ref = refs[9:]
    rows = blocks[0].shape[0]
    own = wo_ref.shape[0]
    for i, k in enumerate(range(0, n, split)):
        e_ref[i * rows : (i + 1) * rows] = blocks[k][...]
    dk_ref[...] = jnp.zeros_like(dk_ref)
    dv_ref[...] = jnp.zeros_like(dv_ref)
    wide = pairs_at_once(n, rows, split)
    step = 2 * rows * wide // split

    @pl.loop(0, n // 2 // wide)
    def _(i):
        at = tile_rows(i, step)
        mask = (place_ref[...] >= low_ref[at]) & (place_ref[...] <= high_ref[at])
        d_all = dot_t(e_ref[at], wo_ref[...]).astype(LOW)
        dqs, dks, dvs = [], [], []
        for index, start in enumerate(range(0, own, head_width)):
            span = slice(start, start + head_width)
            q, k, v, d = q_ref[at, span], k_ref[:, span], v_ref[:, span], d_all[:, span]
            weights = jnp.where(mask, jnp.exp(dot_t(q, k) - lse_ref[at, index : index + 1]), 0.0)
            weight_grad = dot_t(d, v)
            delta = jnp.sum(weights * weight_grad, axis=1, keepdims=True)
            score_grad = (weights * (weight_grad - delta)).astype(LOW)
            dqs.append(dot(score_grad, k))
            dks.append(t_dot(score_grad, q))
            dvs.append(t_dot(weights.astype(LOW), d))
        dq = jnp.concatenate(dqs, axis=1).astype(LOW).astype(F32) * 0.125
        dq_ref[at] = dq.astype(LOW)
        dk_ref[...] += jnp.concatenate(dks, axis=1)
        dv_ref[...] += jnp.concatenate(dvs, axis=1)

    dkv_ref[:, :own] = dk_ref[...].astype(LOW)
    dkv_ref[:, own:] = dv_ref[...].astype(LOW)
    if split > 1:
        return

    @pl.loop(0, n // 2 // wide)
    def _(i):
        at = tile_rows(i, step)
        put_slots(
            even_ref, odd_ref, i * wide, dot_t(dq_ref[at], w_ref[:, :own]) + dot_t(dkv_ref[at], w_ref[:, own : 3 * own])
        )


def place_ffn_kernel(n, m, layers, *refs):
    up_ref, down_ref, up_out, down_out, fc1_out = refs
    piece = fc1_out.shape[1]
    for layer in range(layers):
        down_out[layer] = down_ref[layer, :piece].astype(F32)
        fc1_out[layer : layer + 1] = down_ref[layer, piece : piece + 16, :piece].astype(F32)[:1]
        for device in range(n):
            high, low = device // m, device % m
            for j in range(m):
                at = (n * j + m * high + (j + low) % m) * piece
                start = (layer * m + j) * piece
                block = up_ref[device, :, start : start + piece]
                up_out[layer, :, at : at + piece] = block.astype(F32)


def place_attention_kernel(n, layers, *refs):
    late, both, outs = refs[0], refs[1 : layers + 1], refs[layers + 1 :]
    qkv_out, o_out, q_out, kv_out, cross_out = outs
    col = both[0].shape[1] // 8
    rows = both[0].shape[0] // n
    for layer in range(layers):
        for i in range(n):
            for part in range(5):
                out, at = (kv_out, part) if part < 2 else (qkv_out, part - 2)
                start = (5 * layer + part) * col
                block = late[i, :, start : start + col]
                out[layer, :, (at * n + i) * col : (at * n + i + 1) * col] = block.astype(F32)
            for out, part in ((q_out, 5), (cross_out, 6), (o_out, 7)):
                block = both[layer][i * rows : (i + 1) * rows, part * col : (part + 1) * col]
                out[layer, :, i * col : (i + 1) * col] = block.astype(F32)


def last_backward_kernel(terms, *refs):
    dx1_ref, refs = refs[0], refs[1:]
    term_refs, refs = refs[:terms], refs[terms:]
    x_ref, vec_ref, dx_ref, e_ref, sum_ref = refs
    back, gain, shift = layer_norm_back(
        x_ref[...].astype(F32), vec_ref[0:1], total_of([t[...] for t in term_refs])
    )
    dx = dx1_ref[...] + back
    dx_ref[...] = dx
    e_ref[...] = dx.astype(LOW)
    sum_ref[...] = jnp.concatenate([gain, shift], axis=0)


def stored_positions(row_index, row_count, dev_count):
    device = row_index // row_count
    offset = row_index % row_count
    half_rows = row_count // 2
    return jnp.where(
        offset < half_rows,
        device * half_rows + offset,
        (2 * dev_count - 1 - device) * half_rows + offset - half_rows,
    )


def ranges_of(starts, length):
    return starts, jnp.concatenate([starts[1:], jnp.full((1,), length, jnp.int32)]) - 1


def group_of(places, starts):
    return jnp.sum((starts[None, :] <= places[:, None]).astype(jnp.int32), axis=1) - 1


def pick(table, index):
    slots = jnp.arange(table.shape[0], dtype=jnp.int32)
    return jnp.sum(jnp.where(index[:, None] == slots[None, :], table[None, :], 0), axis=1)


def on_device(
    tokens,
    encoder_states,
    grad_out,
    doc_starts,
    source_doc,
    source_offsets,
    self_qkv,
    self_out,
    cross_q,
    cross_kv,
    cross_out,
    ffn_in,
    ffn_out,
    norm_gains,
    vec_biases,
    fc1_bias,
):
    n, m = lax.axis_size("ctx"), lax.axis_size("fsdp")
    c, f = lax.axis_index("ctx"), lax.axis_index("fsdp")
    layers = self_qkv.shape[0]
    rows, width = tokens.shape[1:]
    source_rows = encoder_states.shape[1]
    length, source_length = n * rows, n * source_rows
    held = self_out.shape[1]
    hidden = ffn_out.shape[1] * m
    head_width = width // HEADS
    groups = min(n, HEADS)
    split = n // groups
    group, part = c // split, c % split
    own = width // groups
    col = width // n
    piece = hidden // (n * m)
    units = m * piece
    high_c, low_c = c // m, c % m
    here = jnp.stack([c, f]).astype(jnp.int32)
    queries = length // split
    packs = split == 1 and col % 128 == 0 and units == width and piece == held

    slot_rows = ((c ^ jnp.arange(n, dtype=jnp.int32)) * rows)[:, None] + jnp.arange(
        rows, dtype=jnp.int32
    )[None, :]
    places = stored_positions(slot_rows.reshape(-1), rows, n)
    own_places = places.reshape(n // split, split, rows)[:, 0].reshape(-1)
    doc_low, doc_high = ranges_of(doc_starts[0], length)
    self_bounds = [
        pick(doc_low, group_of(own_places, doc_starts[0]))[:, None],
        own_places[:, None],
        places[None, :],
    ]
    source_low, source_high = ranges_of(source_offsets[0], source_length)
    read_doc = pick(source_doc[0], group_of(places[:rows], doc_starts[0]))
    cross_bounds = [
        pick(source_low, read_doc)[:, None],
        pick(source_high, read_doc)[:, None],
        jnp.arange(source_length, dtype=jnp.int32)[None, :],
    ]

    def fetch_out():
        start = group * own
        got = lax.dynamic_slice(self_out, (0, start % held, 0), (layers, own, width))
        got = jnp.where(f == start // held, got, jnp.zeros_like(got))
        covered = [{(device // split) * own // held} for device in range(n)]
        while any(len(planes) < m for planes in covered):
            pairs = []
            for device, planes in enumerate(covered):
                reached = set()
                for plane in sorted(planes):
                    free = [p for p in (plane + 1, plane - 1) if 0 <= p < m and p not in planes | reached]
                    if free:
                        reached.add(free[0])
                        pairs.append((device * m + plane, device * m + free[0]))
                planes |= reached
            got = got + lax.ppermute(got, ("ctx", "fsdp"), pairs)
        return got

    def columns(array, layer, start, count):
        return lax.dynamic_slice(array, (layer, 0, start), (1, array.shape[1], count))[0]

    first_rows = jnp.concatenate([tokens[0], encoder_states[0]])
    first_slots = gather_slots(first_rows)
    unit_start = (m * high_c + (f + low_c) % m) * piece
    last_slots = gather_slots(after(grad_out[0], first_slots))
    vec_rows = jnp.concatenate([norm_gains, vec_biases], axis=1)
    fc1_rows = lax.dynamic_slice(fc1_bias, (0, unit_start), (layers, piece))
    fc1_rows = jnp.pad(fc1_rows, ((0, 0), (0, held - piece)))
    vec_rows = jnp.concatenate([vec_rows.reshape(-1, held), fc1_rows])
    if packs:
        arrays = dict(qkv=self_qkv, kv=cross_kv, q=cross_q, out=cross_out, up=ffn_in, down=ffn_out)
        arrays["self_out"] = self_out
        arrays["vec"] = jnp.pad(vec_rows.T, ((0, 0), (0, 128 - vec_rows.shape[0])))
        first_size = (7 + layers) * col
        sizes = {
            "first": (held, first_size + 128),
            "attention": (held, 7 * col),
            "ffn": (held + piece, units),
        }

        def pack(jobs, wait=()):
            fed = [arrays[name] for kind, layer in jobs for name in FED[kind]]
            return call(
                partial(pack_kernel, m, n, jobs),
                [here] + fed,
                [like(sizes[kind], LOW) for kind, layer in jobs],
                0,
                scratch=[pltpu.SemaphoreType.DMA((8 * len(jobs) + 8,))],
                smem=1,
                far=len(fed),
                wait=wait,
            )

        packed = pack([("first", 0)])
        packed += pack([("ffn", 0)], [first_slots[-1], last_slots[-1]])
        for layer in range(1, layers):
            packed += pack([("attention", layer), ("ffn", layer)])
        got = []
        for index, operand in enumerate(packed):
            if index > 1:
                operand = after(operand, got[index - 2])
            tiled = operand.shape[0] == held
            got.append(lax.all_gather(operand, "fsdp", axis=0, tiled=tiled))
        w_qkv = w_rest = got[0::2]
        w_ffn = [[both] for both in got[1::2]]
        skip = [3 * col] * layers
        ordered = got[0][:, first_size : first_size + vec_rows.shape[0]].T.astype(F32)
        w_out = got[0][:, 7 * col : first_size].reshape(n, col, layers, col)
        w_out = lax.all_to_all(w_out, "ctx", 0, 0).transpose(2, 1, 0, 3).reshape(layers, col, width)
    else:
        w_out = fetch_out()
        ordered = gather_planes(vec_rows.T).T.astype(F32)
        w_qkv, w_rest, w_ffn, skip = [], [], [], [0] * layers
        for layer in range(layers):
            blocks = [columns(self_qkv, layer, i * width + group * own, own) for i in range(3)]
            w_qkv.append(gather_planes(jnp.concatenate(blocks, axis=1)))
            blocks = [columns(cross_kv, layer, i * width + c * col, col) for i in range(2)]
            blocks += [columns(cross_q, layer, c * col, col), columns(cross_out, layer, c * col, col)]
            w_rest.append(gather_planes(jnp.concatenate(blocks, axis=1)))
            blocks = [
                columns(ffn_in, layer, (n * j + m * high_c + (j + low_c) % m) * piece, piece)
                for j in range(m)
            ]
            down = lax.dynamic_slice(ffn_out, (layer, unit_start, 0), (1, piece, width))[0]
            w_ffn.append([gather_planes(jnp.concatenate(blocks, axis=1)), gather_planes(down)])
    vectors = ordered[:-layers].reshape(layers, -1, width)
    up_bias = ordered[-layers:].reshape(layers, m, held)[:, :, :piece].reshape(layers, units)
    w_sems = pltpu.SemaphoreType.DMA((2 * m,))
    w_scratch = [pltpu.VMEM((width, units), LOW), pltpu.VMEM((units, width), LOW), w_sems]
    qv_bias = lax.dynamic_slice(vectors, (0, 6, group * own), (layers, 2, own))
    ev_bias = lax.dynamic_slice(vectors, (0, 10, c * col), (layers, 1, col))
    ev_bias = jnp.pad(ev_bias, ((0, 0), (0, 0), (col, 0)))

    def own_slots(values):
        if split == 1:
            return values
        shaped = values.reshape((n // split, split, rows) + values.shape[1:])
        return shaped[:, 0].reshape((-1,) + values.shape[1:])

    def share(parts):
        if split == 1:
            return parts[0]
        total = lax.dynamic_index_in_dim(parts, part, 0, False).astype(F32)
        for other in range(1, split):
            term = lax.dynamic_index_in_dim(parts, part ^ other, 0, False)
            total = total + swap(term, other).astype(F32)
        return total

    def half_slots(width_of, kind=LOW):
        return [like((n // 2, rows, width_of), kind)] * 2

    (encoder_all,) = call(
        partial(assemble_kernel, n, rows),
        [here] + first_slots,
        [like((source_length, width), LOW)],
        0,
        smem=1,
    )

    def prepare(layer, wait=()):
        return call(
            partial(cross_prepare_kernel, col, skip[layer]),
            [w_rest[layer], encoder_all, ev_bias[layer]],
            [like((2 * col, width + source_length), LOW)],
            4 * source_length * width * col,
            wait=wait,
        )[0]

    x = tokens[0]
    h1_slots = first_slots
    kept = []
    matmul = 2 * length * width
    for layer in range(layers):
        vec = vectors[layer]
        w_t = after(prepared if layer else prepare(0, packed[2:] if packs else ()), h1_slots)
        near = gather_near(w_t)
        joined = layer > 0
        h1_all, q, k, v, a, self_lse, *parts = call(
            partial(self_forward_kernel, n, rows, split, layer == 0, joined, head_width),
            h1_slots
            + [vec, after(qv_bias[layer], w_t), w_qkv[layer]]
            + self_bounds
            + [w_out[layer]] * joined,
            [like((length, width), LOW), like((queries, own), LOW)]
            + [like((length, own), LOW)] * 2
            + [like((queries, own), LOW), like((queries, own // head_width), F32)]
            + half_slots(width) * joined,
            matmul * 4 * own + 4 * queries * length * own,
            steps=int(packs),
            tiles={n + 2: ((width, 3 * own), None)} if packs else None,
        )
        if not joined:
            parts = call(
                partial(self_out_kernel, n, rows, split),
                [a, w_out[layer]],
                half_slots(width),
                matmul * own,
            )
        even, odd = parts
        near, odd = lax.optimization_barrier((near, odd))
        terms = reduce_slots(even, odd)
        w_slots, where = gather_joined(w_t, near)
        x1, x2, h2, cq, mixed, cross_lse, h3, wq_t, wo_t, ek_t, ev_t = call(
            partial(mid_forward_kernel, n, len(terms), len(w_slots), where, head_width),
            [here, x] + terms + w_slots + [vec] + cross_bounds,
            [like((rows, width), F32)] * 2
            + [like((rows, width), LOW)] * 3
            + [like((rows, HEADS), F32), like((rows, width), LOW)]
            + [like((width, width), LOW)] * 2
            + [like((width, source_length), LOW)] * 2,
            4 * rows * width * (width + source_length),
            smem=1,
        )
        h3_slots = gather_slots(h3)
        weight_count = len(w_ffn[layer])
        first = n + 1 + weight_count
        tile = 4 * rows
        g, slope, even, odd = call(
            partial(ffn_forward_kernel, n, weight_count),
            h3_slots + [up_bias[layer][None]] + w_ffn[layer],
            [like((length, units), LOW)] * 2 + half_slots(width),
            2 * matmul * units,
            scratch=[pltpu.VMEM((length, width), LOW)] + w_scratch,
            far=weight_count,
            steps=n // 4,
            tiles={first + i: ((tile, units), 0) for i in range(2)}
            | {first + 2 + i: ((2, rows, width), 0) for i in range(2)},
        )
        last = layer == layers - 1
        if last:
            result_parts = (even, odd)
        else:
            terms = reduce_slots(even, odd)
        kept.append(
            (x, x1, x2, h1_all, q, k, v, a, self_lse, h2, cq, mixed, cross_lse)
            + (h3_slots, g, slope, wq_t, wo_t, ek_t, ev_t)
        )
        if last:
            continue
        prepared = prepare(layer + 1)
        outs = call(
            partial(between_kernel, len(terms), False),
            [x2] + terms + [vec, vectors[layer + 1]],
            [like((rows, width), F32), like((rows, width), LOW)],
            rows * width * 20,
        )
        x = outs[0]
        h1_slots = gather_slots(outs[1])

    r = width // (n * m)
    grad_x, e3_slots = grad_out[0], last_slots
    enc_total = None
    vec_sums = [None] * layers
    moves = [
        (i * m + p, ((n // m) * ((p - i % m) % m) + i // m) * m + p) for i in range(n) for p in range(m)
    ]

    def to_rows(summed):
        return lax.all_to_all(summed.reshape(n, r, summed.shape[1]), "ctx", 0, 0)

    finish = []
    for layer in reversed(range(layers)):
        x, x1, x2, h1_all, q, k, v, a, self_lse, h2, cq, mixed, cross_lse = kept[layer][:13]
        h3_slots, g, slope, wq_t, wo_t, ek_t, ev_t = kept[layer][13:]
        vec = vectors[layer]
        if finish:
            slope = after(slope, cross_grad)
        weight_count = len(w_ffn[layer])
        first = n + 1 + weight_count
        tile = 4 * rows
        du, fc1_grad, even, odd = call(
            partial(ffn_backward_kernel, n, weight_count),
            e3_slots + [slope] + w_ffn[layer],
            [like((length, units), LOW), like((1, units), F32)] + half_slots(width),
            2 * matmul * units,
            scratch=[pltpu.VMEM((length, width), LOW)] + w_scratch,
            far=weight_count,
            steps=n // 4,
            tiles={n: ((tile, units), 0), first: ((tile, units), 0)}
            | {first + 2 + i: ((2, rows, width), 0) for i in range(2)},
        )
        terms = reduce_slots(even, odd)
        shapes = [like((m, n * r, units), LOW), like((m, piece + 16, width), LOW)]
        if units == width:
            shapes = [like((m, n * r + piece + 16, width), LOW)]
        ffn_grads = call(
            partial(ffn_weights_kernel, n, m),
            [here, after(du, terms[0]), g, fc1_grad] + h3_slots + e3_slots,
            shapes,
            2 * matmul * units,
            scratch=[pltpu.VMEM((length, width), LOW)] * 2,
            smem=1,
        )
        x1 = after(x1, ffn_grads)
        if layer == 0:
            result_terms = reduce_slots(*result_parts)
        dx1, e1, e2, dcq, even, odd, sums = call(
            partial(mid_backward_kernel, n, len(terms), head_width),
            [here, grad_x]
            + terms
            + [x1, x2, vec, wq_t, wo_t, ek_t, ev_t, cq, cross_lse]
            + cross_bounds,
            [like((rows, width), F32)]
            + [like((rows, width), LOW)] * 3
            + [like((n // 2, 2 * col, source_length), LOW)] * 2
            + [like((8, width), F32)],
            4 * rows * width * width + 10 * rows * source_length * width,
            scratch=[pltpu.VMEM((width, source_length), LOW)] * 2,
            smem=1,
        )
        ffn_sums = [reduce_planes(grad) for grad in after(ffn_grads, dx1 if layer else terms)]
        e1_slots = gather_slots(e1)
        kv_parts = [even, odd]
        even, *odd = call(
            partial(cross_weights_kernel, n),
            [here, h2, dcq, mixed, e2] + kv_parts,
            [like((n // size, 2 * col, width + source_length), LOW) for size in (2, 4, 4)],
            4 * rows * width * width,
            scratch=[pltpu.VMEM((width, width), LOW)] * 2,
            smem=1,
            wait=[entry[2] for entry in finish[-1:]] + ([] if layer else result_terms[1:]),
        )
        w_terms = reduce_slots(even, list(odd), hold=e1_slots)
        e1_own, dq, dkv, even, odd = call(
            partial(self_backward_kernel, n, split, head_width),
            e1_slots + [w_out[layer], w_qkv[layer], after(q, w_terms[0]), k, v, self_lse] + self_bounds,
            [like((queries, width), LOW), like((queries, own), LOW), like((length, 2 * own), LOW)]
            + half_slots(width),
            matmul * 4 * own + 10 * queries * length * own,
            scratch=[pltpu.VMEM((length, own), F32)] * 2,
            steps=int(packs),
            tiles={n + 1: ((width, 3 * own), None)} if packs else None,
        )
        if split > 1:
            shaped = dkv.reshape(n // split, split, rows, 2 * own)
            total = shaped[:, 0].astype(F32)
            for other in range(1, split):
                total = total + swap(shaped[:, other], other).astype(F32)
            dkv = total.astype(LOW).reshape(-1, 2 * own)
            even = dot_t(jnp.concatenate([dq, dkv], axis=1), w_qkv[layer][:, : 3 * own])
            even = even.reshape(n // 2, rows, width)
            odd = jnp.zeros_like(even)
        terms = reduce_slots(even, after(odd, w_terms))
        before = []
        if layer == 0:
            sums_of = [ffn_sums] + [done[1] for done in reversed(finish)]
            up_rows = to_rows(jnp.concatenate([sums[0][: n * r] for sums in sums_of], axis=1))
            down_rows = [sums[0][n * r :] if units == width else sums[1] for sums in sums_of]
            down_rows = lax.ppermute(jnp.stack(down_rows), ("ctx", "fsdp"), moves)
            before = [up_rows, down_rows]
            *ffn_grads, fc1_own = call(
                partial(place_ffn_kernel, n, m, layers),
                [up_rows, down_rows],
                [like((layers, r, hidden), F32), like((layers, piece, width), F32), like((layers, piece), F32)],
                layers * r * hidden,
            )
        grad_x, e3, last_sums = call(
            partial(last_backward_kernel, len(terms)),
            [dx1] + terms + [x, vec],
            [like((rows, width), F32), like((rows, width), LOW), like((2, width), F32)],
            rows * width * 20,
            wait=before,
        )

        e3_slots = gather_slots(e3) if layer else None
        hold = (e3_slots[2], e3_slots[4]) if layer else terms[0]
        own_parts = [h1_all, dq, dkv, a, e1_own] if split == 1 else []
        cross_grad, enc_total, ev_sum, *enc_parts = call(
            partial(
                attention_weights_kernel,
                n,
                m,
                skip[layer],
                len(terms),
                split == 1,
                layer == layers - 1,
                layer == 0,
            ),
            [here]
            + w_terms
            + own_parts
            + [after(encoder_all, hold), w_rest[layer]]
            + ([] if enc_total is None else [enc_total]),
            [like((m, n * r, (8 if split == 1 else 4) * col), LOW)]
            + [like((source_length, width), F32), like((2 * col, 1), F32)]
            + [like((n // 2, source_rows, width), F32)] * (0 if layer else 2),
            8 * source_length * col * width + matmul * 4 * own,
            smem=1,
            wait=ffn_sums,
        )
        if split > 1:
            qkv_grad = t_dot(own_slots(h1_all), jnp.concatenate([dq, dkv], axis=1)).astype(LOW)
            qkv_grad = share(qkv_grad.reshape(width, 3, split, col).transpose(2, 0, 1, 3))
            qkv_grad = qkv_grad.astype(LOW).reshape(n, m, r, 3 * col).transpose(1, 0, 2, 3)
            o_grad = share(t_dot(a, e1_own).astype(LOW).reshape(split, own // split, width))
            o_grad = o_grad.astype(LOW).reshape(m, r, n, col).transpose(0, 2, 1, 3)
            kv_q = jnp.split(cross_grad, [2 * col], axis=2)
            self_grad = jnp.concatenate([qkv_grad, o_grad], axis=3).reshape(m, n * r, 4 * col)
            parts = [kv_q[0], self_grad[:, :, : 3 * col], kv_q[1], self_grad[:, :, 3 * col :]]
            cross_grad = jnp.concatenate(parts, axis=2)
        both_sum = reduce_planes(cross_grad)
        finish.append((layer, ffn_sums, both_sum))
        zero = jnp.zeros((1, width), F32)
        summed = jnp.concatenate(
            [last_sums[0:1], sums[0:2], last_sums[1:2], sums[2:4], zero, zero]
            + [sums[4:6], zero, sums[6:8]]
        )
        owned_q = share(row_sum(dq).reshape(split, col))
        owned_v = share(row_sum(dkv[:, own:]).reshape(split, col))
        blank = jnp.zeros((col,), F32)
        owned = [blank] * 6 + [owned_q, owned_v, blank, blank, ev_sum[col:, 0], blank, blank]
        vec_sums[layer] = (summed, jnp.stack(owned))

    finish.sort(key=lambda entry: entry[0])
    (result,) = call(
        partial(between_kernel, len(result_terms), True),
        [kept[-1][2]] + result_terms + [vectors[-1]],
        [like((rows, width), LOW)],
        rows * width * 20,
    )
    summed = jnp.concatenate([pair[0] for pair in vec_sums])
    owned = jnp.concatenate([pair[1] for pair in vec_sums])
    enc_grad = total_of(reduce_slots(*enc_parts, F32))
    summed = turn(summed, 1).reshape(-1, n, col).transpose(1, 0, 2)
    vec = total_of(reduce_slots(summed[0::2], summed[1::2], F32)) + owned
    (late,) = call(
        late_kernel,
        [entry[2] for entry in finish],
        [like((n * r, layers * 5 * col), LOW)],
        0,
        wait=[up_rows, down_rows],
    )
    late_rows = to_rows(late)
    (vec,) = call(copy_kernel, [vec], [like(vec.shape, F32)], 0, wait=[late])
    attention_grads = call(
        partial(place_attention_kernel, n, layers),
        [late_rows] + [entry[2] for entry in finish],
        [like((layers, r, parts * width), F32) for parts in (3, 1, 1, 2, 1)],
        layers * r * 8 * width,
    )
    vec = sum_planes(vec.reshape(-1, m, col // m).transpose(1, 0, 2))
    vec = vec.reshape(layers, -1, col // m)
    return (
        (result[None], grad_x[None], enc_grad[None])
        + tuple(attention_grads)
        + tuple(ffn_grads)
        + (vec[:, :3], vec[:, 3:], fc1_own)
    )


def solution(mesh):
    tokens = P("fsdp", "ctx", None)
    per_stream = P("fsdp", None)
    weight = P(None, "fsdp", None)
    vector = P(None, None, "fsdp")
    grad = P(None, ("ctx", "fsdp"), None)
    vector_grad = P(None, None, ("ctx", "fsdp"))
    return jax.shard_map(
        on_device,
        mesh=mesh,
        in_specs=(tokens,) * 3 + (per_stream,) * 3 + (weight,) * 7 + (vector,) * 2 + (P(None, "fsdp"),),
        out_specs=(tokens,) * 3 + (grad,) * 7 + (vector_grad,) * 2 + (P(None, ("ctx", "fsdp")),),
        check_vma=False,
    )
```
